32 devices in a mesh: ctx: 8 (over y, x, core), fsdp: 4 (over z).
Axes of the slice: x: 2, y: 2, z: 4, core: 2. Of those that a mesh axis runs over, the one named last changes fastest.
Arguments:
- tokens: bfloat16 [8, 2, 256, 768], P('ctx', None, 'fsdp'), may hold values from -6 to 6
- block_owner: int32 [8, 2], replicated, may hold values from 0 to 15, as said below
- first_gain: bfloat16 [768], P('fsdp'), may hold values from 0.099609375 to 1.8984375
- first_shift: bfloat16 [768], P('fsdp'), may hold values from -3 to 3
- mixer_in: bfloat16 [768, 2304], P('fsdp'), may hold values from -0.21875 to 0.21875
- mixer_out: bfloat16 [768, 768], P('fsdp'), may hold values from -3.5 to 3.5
- mixer_bias: bfloat16 [768], P('fsdp'), may hold values from -2 to 2
- second_gain: bfloat16 [768], P('fsdp'), may hold values from 0.099609375 to 1.8984375
- second_shift: bfloat16 [768], P('fsdp'), may hold values from -3 to 3
- up_weight: bfloat16 [3072, 768], P('fsdp'), may hold values from -0.21875 to 0.21875
- up_bias: bfloat16 [3072], P('fsdp'), may hold values from -3 to 3
- down_weight: bfloat16 [3072, 768], P('fsdp'), may hold values from -0.109375 to 0.109375
- down_bias: bfloat16 [768], P('fsdp'), may hold values from -2 to 2
- out_grad: bfloat16 [8, 2, 256, 768], P('ctx', None, 'fsdp'), may hold values from -6 to 6
Outputs:
- block_out: bfloat16 [8, 2, 256, 768], P('ctx', None, 'fsdp')
- tokens_grad: float32 [8, 2, 256, 768], P('ctx', None, 'fsdp')
- first_gain_grad: float32 [768], P('fsdp')
- first_shift_grad: float32 [768], P('fsdp')
- mixer_in_grad: float32 [768, 2304], P('fsdp')
- mixer_out_grad: float32 [768, 768], P('fsdp')
- mixer_bias_grad: float32 [768], P('fsdp')
- second_gain_grad: float32 [768], P('fsdp')
- second_shift_grad: float32 [768], P('fsdp')
- up_weight_grad: float32 [3072, 768], P('fsdp')
- up_bias_grad: float32 [3072], P('fsdp')
- down_weight_grad: float32 [3072, 768], P('fsdp')
- down_bias_grad: float32 [768], P('fsdp')
The draws below stay inside these ranges and needn't reach their ends.
Inputs may be any that keep to these rules, and one draw needn't show every extreme that they name: `block_owner`: row c holds a block number b < 8 and 15 - b; every block number appears exactly once.
All inputs are finite; a program needn't handle non-finite values.
Results may differ from the reference program's by a relative error of at most 0.028.
Values may be sent and summed in bfloat16 or wider, within the bound.
No kernel may reach another device: no remote copies, remote signals or barrier semaphores. Data moves between devices by JAX's collectives and lax.ppermute only.
A program may use at most 256 MiB of HBM per device.

```python
from functools import partial
import jax
import jax.numpy as jnp
from jax import lax

HEADS = 12
HEAD_DIM = 64
FF = 3072
D = 768
BLOCK = 256
BLOCKS = 16
SEQ = 4096


def draw_block_owner(key, part):
    key = jax.random.fold_in(key, 7)
    early = jax.random.permutation(key, BLOCKS // 2).astype(jnp.int32)
    return jnp.stack([early, BLOCKS - 1 - early], axis=1)


def level_of(rng, extent, split, least, largest):
    def one(position, blocks):
        steps = jax.random.uniform(jax.random.fold_in(jax.random.fold_in(rng, 6), position), (blocks,), jnp.float32, least / len(split), largest / len(split))
        return jnp.repeat(jnp.exp(steps), extent[position] // blocks).reshape((-1,) + (1,) * (len(extent) - position - 1))

    level = one(*split[0])
    for cut in split[1:]:
        level = level * one(*cut)
    return level


def centred(stream_key, shape, scale, most, cuts=(), kind=jnp.bfloat16):
    values = jax.random.normal(stream_key, shape, jnp.float32) * scale
    if len(cuts) > 0:
        values = level_of(stream_key, shape, cuts, -0.22, 0.18) * values
    return jnp.clip(values, min=-most, max=most).astype(kind)


def setup_inputs(seed: int = 0) -> dict:
    streams_of = jax.random.split(jax.random.key(seed), 15)
    return {
        "tokens": centred(streams_of[0], (BLOCKS // 2, 2, BLOCK, D), 1.0, 6.0, ((0, 8), (2, 4))),
        "block_owner": draw_block_owner(jax.random.fold_in(streams_of[14], 71), 0),
        "first_gain": jnp.clip(1.0 + 0.18 * jax.random.normal(streams_of[2], (D,), jnp.float32), 0.099609375, 1.8984375).astype(jnp.bfloat16),
        "first_shift": centred(streams_of[3], (D,), 0.5, 3.0, ((0, 4),)),
        "mixer_in": centred(streams_of[4], (D, 3 * D), D ** -0.5, 0.21875, ((0, 4),)),
        "mixer_out": centred(streams_of[5], (D, D), (max(1, D * 16 // SEQ)) ** -0.5, 3.5, ((0, 4),)),
        "mixer_bias": centred(streams_of[6], (D,), 0.3, 2.0, ((0, 4),)),
        "second_gain": jnp.clip(1.0 + 0.18 * jax.random.normal(streams_of[7], (D,), jnp.float32), 0.099609375, 1.8984375).astype(jnp.bfloat16),
        "second_shift": centred(streams_of[8], (D,), 0.5, 3.0, ((0, 4),)),
        "up_weight": centred(streams_of[9], (FF, D), D ** -0.5, 0.21875, ((0, 4),)),
        "up_bias": centred(streams_of[10], (FF,), 0.5, 3.0, ((0, 4),)),
        "down_weight": centred(streams_of[11], (FF, D), FF ** -0.5, 0.109375, ((0, 4),)),
        "down_bias": centred(streams_of[12], (D,), 0.3, 2.0, ((0, 4),)),
        "out_grad": centred(streams_of[13], (BLOCKS // 2, 2, BLOCK, D), 1.0, 6.0, ((0, 8), (2, 4))),
    }


EPS = 1e-05
MASKED = -1e+30
HIGH = lax.Precision.HIGHEST

@jax.custom_vjp
def low(v):
    return lax.optimization_barrier(v.astype(jnp.bfloat16)).astype(jnp.float32)

@jax.custom_vjp
def low_back(v):
    return v

def low_keep(v):
    return (low(v), None)

def low_pass(kept, grad):
    return (grad,)

def back_keep(v):
    return (v, None)

def back_low(kept, grad):
    return (low(grad),)
low.defvjp(low_keep, low_pass)
low_back.defvjp(back_keep, back_low)

def both_round(values):
    return low_back(low(values))

def layer_norm(values, gain, shift):
    center = values - lax.optimization_barrier(jnp.mean(values, axis=-1, keepdims=True))
    spread = lax.optimization_barrier(jnp.mean(center * center, axis=-1, keepdims=True))
    return center * lax.rsqrt(spread + EPS) * gain + shift

def attend_block(queries, keys, values, first):
    rows = queries.shape[0]
    count = keys.shape[0]
    score = jnp.einsum('qhd,khd->hqk', queries, keys, precision=HIGH) * HEAD_DIM ** (-0.5)
    score = low_back(score)
    query_pos = first + jnp.arange(rows, dtype=jnp.int32)
    key_pos = jnp.arange(count, dtype=jnp.int32)
    seen = (key_pos[None, :] <= query_pos[:, None])[None]
    score = jnp.where(seen, score, MASKED)
    top = lax.optimization_barrier(jnp.max(score, axis=-1, keepdims=True))
    expo = jnp.where(seen, jnp.exp(score - top), 0.0)
    prob = low(expo / lax.optimization_barrier(jnp.sum(expo, axis=-1, keepdims=True)))
    return jnp.einsum('hqk,khd->qhd', prob, values, precision=HIGH)

def block_forward(tokens, first_gain, first_shift, mixer_in, mixer_out, mixer_bias, second_gain, second_shift, up_weight, up_bias, down_weight, down_bias, order):
    blocks = tokens.reshape(BLOCKS, BLOCK, D)
    back_order = jnp.argsort(order).astype(jnp.int32)
    seq = blocks[back_order].reshape(SEQ, D)
    normed = low(layer_norm(seq, first_gain, first_shift))
    mixed = both_round(jnp.dot(normed, mixer_in, precision=HIGH))
    query = mixed[:, :D].reshape(SEQ, HEADS, HEAD_DIM)
    keys = mixed[:, D:2 * D].reshape(SEQ, HEADS, HEAD_DIM)
    values = mixed[:, 2 * D:].reshape(SEQ, HEADS, HEAD_DIM)
    outputs = []
    for index in range(BLOCKS):
        upper = (index + 1) * BLOCK
        step_fn = jax.checkpoint(partial(attend_block, first=index * BLOCK))
        outputs.append(step_fn(query[index * BLOCK:upper], keys[:upper], values[:upper]))
    attend = both_round(jnp.concatenate(outputs, axis=0).reshape(SEQ, D))
    branch = low_back(jnp.dot(attend, mixer_out, precision=HIGH) + mixer_bias)
    resid = seq + branch
    second = low(layer_norm(resid, second_gain, second_shift))
    pre = low_back(jnp.dot(second, up_weight.T, precision=HIGH) + up_bias)
    act = low(jax.nn.gelu(pre, approximate=True))
    feed = low_back(jnp.dot(act, down_weight, precision=HIGH) + down_bias)
    result = resid + feed
    return result.reshape(BLOCKS, BLOCK, D)[order].reshape(BLOCKS // 2, 2, BLOCK, D)

def reference(tokens, block_owner, first_gain, first_shift, mixer_in, mixer_out, mixer_bias, second_gain, second_shift, up_weight, up_bias, down_weight, down_bias, out_grad):
    order = block_owner.reshape(-1).astype(jnp.int32)
    params = (tokens.astype(jnp.float32), first_gain.astype(jnp.float32), first_shift.astype(jnp.float32), mixer_in.astype(jnp.float32), mixer_out.astype(jnp.float32), mixer_bias.astype(jnp.float32), second_gain.astype(jnp.float32), second_shift.astype(jnp.float32), up_weight.astype(jnp.float32), up_bias.astype(jnp.float32), down_weight.astype(jnp.float32), down_bias.astype(jnp.float32))
    result, pull = jax.vjp(partial(block_forward, order=order), *params)
    grads = pull(out_grad.astype(jnp.float32))
    return (result.astype(jnp.bfloat16), grads[0], grads[1], grads[2], grads[3], grads[4], grads[5], grads[6], grads[7], grads[8], grads[9], grads[10], grads[11])
```

```python
import functools

import jax
import jax.numpy as jnp
from jax import lax
from jax.experimental import pallas as pl
from jax.experimental.pallas import tpu as pltpu
from jax.sharding import PartitionSpec as P

HEADS = 12
HEAD_DIM = 64

EPS = 1e-05
MASKED = -1e30
F32 = jnp.float32
BF16 = jnp.bfloat16
VMEM_LIMIT = 56 * 1024 * 1024


def swap(x, axis, mask):
    return lax.ppermute(x, axis, [(i, i ^ mask) for i in range(lax.axis_size(axis))])


def add16(left, right):
    return (left.astype(F32) + right.astype(F32)).astype(BF16)


def z_gather(x):
    return [x] + [swap(x, "fsdp", r) for r in range(1, lax.axis_size("fsdp"))]


def z_exchange(pieces):
    return [pieces[0]] + [swap(pieces[r], "fsdp", r) for r in range(1, len(pieces))]


def z_sum(pieces):
    return sum(piece.astype(F32) for piece in z_exchange(pieces))


def chip_spread(x, bits):
    masks = [2 << b for b in range(bits)]
    if bits == 0:
        return x[None]
    half = x.shape[0] // 2

    def walk(part, order):
        found = {0: part}
        for mask in order:
            found.update({r | mask: swap(piece, "ctx", mask) for r, piece in found.items()})
        return found

    if bits == 1:
        found = walk(x, masks)
        return jnp.stack([found[2 * r] for r in range(1 << bits)])
    front, back = walk(x[:half], masks), walk(x[half:], masks[::-1])
    return jnp.stack(
        [jnp.concatenate([front[2 * r], back[2 * r]]) for r in range(1 << bits)]
    )


def ctx_spread(x):
    n = lax.axis_size("ctx")
    held = chip_spread(x, n.bit_length() - 2)
    return jnp.stack([held, swap(held, "ctx", 1)], axis=1).reshape((n,) + x.shape)


def chip_collect(x):
    bits = x.shape[0].bit_length() - 1
    half = x.shape[1] // 2

    def fold(pieces, order):
        for mask in order:
            keep = [r for r in sorted(pieces) if not r & mask]
            came = swap(jnp.stack([pieces[r | mask] for r in keep]), "ctx", 2 * mask)
            pieces = {r: add16(pieces[r], came[i]) for i, r in enumerate(keep)}
        return pieces[0]

    masks = [1 << b for b in range(bits)]
    if bits < 2:
        return fold({r: x[r] for r in range(1 << bits)}, masks)
    front = fold({r: x[r, :half] for r in range(1 << bits)}, masks)
    back = fold({r: x[r, half:] for r in range(1 << bits)}, masks[::-1])
    return jnp.concatenate([front, back])


def ctx_collect(x):
    n = x.shape[0]
    paired = x.reshape((n // 2, 2) + x.shape[1:])
    return chip_collect(add16(paired[:, 0], swap(paired[:, 1], "ctx", 1)))


def rest_total(x, bits):
    x = add16(x, swap(x, "ctx", 1))
    mask = 2 << bits
    while mask < lax.axis_size("ctx"):
        x = add16(x, swap(x, "ctx", mask))
        mask *= 2
    return x


def ctx_total(x):
    mask = 1
    while mask < lax.axis_size("ctx"):
        x = x + swap(x, "ctx", mask)
        mask *= 2
    return x


def pick(stacked, index):
    return lax.dynamic_index_in_dim(stacked, index, 0, keepdims=False)


def shuffle_kernel(table, x_ref, out_ref):
    width = x_ref.shape[2]
    extra = out_ref.shape[2] - width
    for i in range(out_ref.shape[0]):
        out_ref[i, :, :width] = x_ref[table[i]].astype(out_ref.dtype)
        if extra:
            out_ref[i, :, width:] = jnp.zeros((x_ref.shape[1], extra), out_ref.dtype)


def shuffle(x, table, kind, width=None):
    shape = (table.shape[0], x.shape[1], width or x.shape[2])
    return pl.pallas_call(
        shuffle_kernel,
        grid_spec=pltpu.PrefetchScalarGridSpec(
            num_scalar_prefetch=1,
            grid=(),
            in_specs=[pl.BlockSpec(memory_space=pltpu.VMEM)],
            out_specs=pl.BlockSpec(memory_space=pltpu.VMEM),
        ),
        out_shape=jax.ShapeDtypeStruct(shape, kind),
        compiler_params=pltpu.CompilerParams(vmem_limit_bytes=VMEM_LIMIT),
    )(table, x)


def mm(left, right):
    return jnp.dot(left, right, preferred_element_type=F32)


def contract_rows(left, right):
    return lax.dot_general(left, right, (((0,), (0,)), ((), ())), preferred_element_type=F32)


def contract_cols(left, right):
    return lax.dot_general(left, right, (((1,), (1,)), ((), ())), preferred_element_type=F32)


def head_rows(values, at, heads):
    rows = lax.broadcasted_iota(jnp.int32, values.shape, 0) - at
    return [
        jnp.where((rows >= h * HEAD_DIM) & (rows < (h + 1) * HEAD_DIM), values, 0.0).astype(BF16)
        for h in range(heads)
    ]


def head_cols(values, at, heads):
    cols = lax.broadcasted_iota(jnp.int32, values.shape, 1) - at
    return [
        jnp.where((cols >= h * HEAD_DIM) & (cols < (h + 1) * HEAD_DIM), values, 0.0).astype(BF16)
        for h in range(heads)
    ]


def causal_mask(size, flip):
    keys = lax.broadcasted_iota(jnp.int32, (size, size), 0) ^ flip
    queries = lax.broadcasted_iota(jnp.int32, (size, size), 1) ^ flip
    return keys <= queries


def attend_kernel(meta, q_ref, kv_ref, out_ref, sum_ref, lse_ref, *, heads):
    size, wide = q_ref.shape[1:]
    count = kv_ref.shape[0]
    width = heads * HEAD_DIM
    scale = HEAD_DIM ** (-0.5)
    for j in range(2):
        block = meta[count + j]
        turned = head_rows(jnp.transpose(q_ref[j].astype(F32)) * scale, 0, heads)

        def visit(place, carry, diagonal):
            keys = kv_ref[place, :, :wide]
            values = jnp.transpose(kv_ref[place, :, 2 * width - wide :].astype(F32)).astype(BF16)
            later = []
            for h in range(heads):
                score = mm(keys, turned[h])
                if diagonal:
                    score = jnp.where(causal_mask(size, meta[count + 2]), score, MASKED)
                top = jnp.max(score, axis=0, keepdims=True)
                if not diagonal:
                    top = jnp.maximum(top, carry[2 * h])
                weight = jnp.exp(score - top)
                total = jnp.sum(weight, axis=0, keepdims=True)
                at = wide - width + h * HEAD_DIM
                gain = mm(values[at : at + HEAD_DIM], weight.astype(BF16))
                spot = slice(h * HEAD_DIM, (h + 1) * HEAD_DIM)
                if not diagonal:
                    fade = jnp.exp(carry[2 * h] - top)
                    total = total + carry[2 * h + 1] * fade
                    gain = gain + sum_ref[j, spot] * fade
                sum_ref[j, spot] = gain
                later += [top, total]
            return tuple(later)

        carry = visit(j, None, True)
        carry = lax.fori_loop(0, block, lambda n, c: visit(meta[n], c, False), carry)
        for h in range(heads):
            spot = slice(h * HEAD_DIM, (h + 1) * HEAD_DIM)
            sum_ref[j, spot] = sum_ref[j, spot] / carry[2 * h + 1]
            lse_ref[j, h : h + 1] = carry[2 * h] + jnp.log(carry[2 * h + 1])
        out_ref[j] = jnp.transpose(sum_ref[j]).astype(BF16)


def attend_back_kernel(
    meta, q_ref, kv_ref, grad_ref, sum_ref, lse_ref, dq_ref, dkv_ref, acc_ref, dq_acc, *, heads
):
    size, wide = q_ref.shape[1:]
    count = kv_ref.shape[0]
    width = heads * HEAD_DIM
    pad = wide - width
    scale = HEAD_DIM ** (-0.5)
    acc_ref[...] = jnp.zeros_like(acc_ref)
    for j in range(2):
        block = meta[count + j]
        query = q_ref[j].astype(F32) * scale
        plain = head_cols(query, 0, heads)
        turned = head_rows(jnp.transpose(query), 0, heads)
        grad_turned = jnp.transpose(grad_ref[j].astype(F32))
        dots = [
            jnp.sum(
                grad_turned[h * HEAD_DIM : (h + 1) * HEAD_DIM]
                * sum_ref[j, h * HEAD_DIM : (h + 1) * HEAD_DIM],
                axis=0,
                keepdims=True,
            )
            for h in range(heads)
        ]
        if pad:
            grad_turned = jnp.concatenate([jnp.zeros((pad, size), F32), grad_turned], axis=0)
        grads = head_cols(jnp.transpose(grad_turned), pad, heads)
        grads_turned = head_rows(grad_turned, pad, heads)
        dq_acc[...] = jnp.zeros_like(dq_acc)

        def visit(place, diagonal):
            keys = kv_ref[place, :, :wide]
            values = kv_ref[place, :, 2 * width - wide :]
            keys_turned = jnp.transpose(keys.astype(F32)).astype(BF16)
            key_grad = jnp.zeros((size, wide), F32)
            value_grad = jnp.zeros((size, wide), F32)
            for h in range(heads):
                score = mm(keys, turned[h])
                if diagonal:
                    score = jnp.where(causal_mask(size, meta[count + 2]), score, MASKED)
                prob = jnp.exp(score - lse_ref[j, h : h + 1])
                prob_grad = mm(values, grads_turned[h])
                score_grad = (prob * (prob_grad - dots[h])).astype(BF16)
                value_grad += mm(prob.astype(BF16), grads[h])
                key_grad += mm(score_grad, plain[h])
                spot = slice(h * HEAD_DIM, (h + 1) * HEAD_DIM)
                dq_acc[spot] += mm(keys_turned[spot], score_grad)
            acc_ref[place, :, :wide] += key_grad
            acc_ref[place, :, 2 * width - wide :] += value_grad

        visit(j, True)

        def step(n, carry):
            visit(meta[n], False)
            return carry

        lax.fori_loop(0, block, step, 0)
        dq_ref[j] = jnp.transpose(dq_acc[...] * scale).astype(BF16)
    dkv_ref[...] = acc_ref[...].astype(BF16)


def in_vmem(kernel, meta, arrays, outs, scratch=()):
    spec = pl.BlockSpec(memory_space=pltpu.VMEM)
    return pl.pallas_call(
        kernel,
        grid_spec=pltpu.PrefetchScalarGridSpec(
            num_scalar_prefetch=1,
            grid=(),
            in_specs=[spec] * len(arrays),
            out_specs=[spec] * len(outs),
            scratch_shapes=list(scratch),
        ),
        out_shape=outs,
        compiler_params=pltpu.CompilerParams(vmem_limit_bytes=VMEM_LIMIT),
    )(meta, *arrays)


def norm_parts(values):
    center = values - jnp.mean(values, axis=-1, keepdims=True)
    rate = lax.rsqrt(jnp.mean(center * center, axis=-1, keepdims=True) + EPS)
    return center * rate, rate


def norm_back(unit, rate, gain, grad):
    e = gain * grad
    return rate * (
        e
        - jnp.mean(e, axis=-1, keepdims=True)
        - unit * jnp.mean(e * unit, axis=-1, keepdims=True)
    )


def after(x, *others):
    return lax.optimization_barrier((x,) + others)[0]


def per_device(
    tokens,
    block_owner,
    first_gain,
    first_shift,
    mixer_in,
    mixer_out,
    mixer_bias,
    second_gain,
    second_shift,
    up_weight,
    up_bias,
    down_weight,
    down_bias,
    out_grad,
):
    groups = lax.axis_size("fsdp")
    member = lax.axis_index("fsdp")
    n_ctx = lax.axis_size("ctx")
    here = lax.axis_index("ctx")
    slot, width = tokens.shape[2:]
    block_len = slot * groups
    local_rows = 2 * slot
    count_rows = 2 * block_len
    blocks = 2 * n_ctx
    share = width // groups
    hidden = up_weight.shape[0]
    hidden_cut = hidden // n_ctx
    heads = -(-HEADS // groups)
    part = heads * HEAD_DIM
    wide = -(-part // 128) * 128
    chip_bits = n_ctx.bit_length() - 2
    fetch_bits = max(b for b in range(chip_bits + 1) if share % (16 << b) == 0)
    fetch = 1 << fetch_bits
    chip = (here // 2) % fetch
    spread_f = jnp.arange(groups, dtype=jnp.int32)
    spread_c = jnp.arange(n_ctx, dtype=jnp.int32)
    spread_h = jnp.arange(fetch, dtype=jnp.int32)

    fetch_table = (
        (spread_h[None, :] ^ chip) * groups + (spread_f[:, None] ^ member)
    ).reshape(-1)
    ctx_table = spread_c ^ here
    f_table = spread_f ^ member

    own = tokens.reshape(2, slot, width)
    rows = own.reshape(local_rows, width).astype(F32)
    grad16 = out_grad.reshape(2, slot, width)

    vectors = z_gather(
        jnp.concatenate(
            [first_gain, first_shift, mixer_bias, second_gain, second_shift, down_bias, up_bias]
        ).reshape(1, -1)
    )
    vectors_rel = jnp.concatenate(vectors)
    vectors_nat = jnp.concatenate([pick(vectors_rel, f_table[i])[None] for i in range(groups)])
    gain_one, shift_one, mix_bias, gain_two, shift_two, bias_down = (
        vectors_nat[:, i * share : (i + 1) * share].reshape(width).astype(F32) for i in range(6)
    )
    up_bias_part = lax.dynamic_slice_in_dim(
        vectors_rel[:, 6 * share :], here * hidden_cut, hidden_cut, 1
    ).reshape(groups * hidden_cut)

    group_tokens = jnp.stack(z_gather(own), axis=1).reshape(count_rows, width)
    in_cut = lax.dynamic_slice_in_dim(mixer_in, chip * (share // fetch), share // fetch, 0)
    in_cut = in_cut.reshape(-1, 3, width)
    in_cut = jnp.pad(in_cut, ((0, 0), (0, 0), (0, groups * part - width)))
    in_cut = in_cut.reshape(-1, 3, groups, part)
    in_cut = jnp.stack([in_cut[:, 1], in_cut[:, 2], in_cut[:, 0]], axis=2)
    in_cut = in_cut.transpose(1, 0, 2, 3).reshape(groups, share // fetch, 3 * part)
    in_pieces = z_exchange([pick(in_cut, member ^ r) for r in range(groups)])
    in_parts = chip_spread(jnp.stack(in_pieces), fetch_bits)
    proj_in = shuffle(
        in_parts.reshape(fetch * groups, share // fetch, 3 * part),
        fetch_table,
        BF16,
        2 * part + wide,
    ).reshape(width, 2 * part + wide)

    unit_one, _ = norm_parts(group_tokens.astype(F32))
    normed16 = (unit_one * gain_one + shift_one).astype(BF16)
    mixed = mm(normed16, proj_in).astype(BF16)
    keyval = mixed[:, : 2 * part].reshape(2, block_len, 2 * part)
    query = mixed[:, 2 * part :].reshape(2, block_len, wide)
    keyvals = ctx_spread(keyval).reshape(blocks, block_len, 2 * part)

    owners = block_owner.reshape(-1)
    places = jnp.sum(
        jnp.where(
            owners[None, :] == jnp.arange(blocks, dtype=jnp.int32)[:, None],
            jnp.arange(blocks, dtype=jnp.int32)[None, :],
            0,
        ),
        axis=1,
    )
    places = ((places // 2) ^ here) * 2 + places % 2
    meta = jnp.concatenate(
        [
            places,
            lax.dynamic_index_in_dim(block_owner, here, 0, keepdims=False),
            (member * slot)[None],
        ]
    ).astype(jnp.int32)

    out_cut = lax.dynamic_slice_in_dim(mixer_out, chip * (share // fetch), share // fetch, 0)
    out_cut = after(out_cut, mixed)
    out_parts = chip_spread(jnp.stack(z_gather(out_cut)), fetch_bits)
    proj_out = shuffle(
        out_parts.reshape(fetch * groups, share // fetch, width), fetch_table, BF16
    ).reshape(width, width)
    ffn_cut = jnp.concatenate(
        [
            lax.dynamic_slice_in_dim(up_weight, here * hidden_cut, hidden_cut, 0),
            lax.dynamic_slice_in_dim(down_weight, here * hidden_cut, hidden_cut, 0),
        ]
    )
    ffn_parts = z_gather(after(ffn_cut, mixed))
    up_part = jnp.concatenate([w[:hidden_cut] for w in ffn_parts])
    down_part = jnp.concatenate([w[hidden_cut:] for w in ffn_parts])
    grads_all = ctx_spread(after(grad16, keyvals)).reshape(n_ctx * local_rows, width)

    attended, sums, lse = in_vmem(
        functools.partial(attend_kernel, heads=heads),
        meta,
        (query, keyvals),
        [
            jax.ShapeDtypeStruct((2, block_len, part), BF16),
            jax.ShapeDtypeStruct((2, part, block_len), F32),
            jax.ShapeDtypeStruct((2, heads, block_len), F32),
        ],
    )
    attended = attended.reshape(2, groups, slot, part)
    attended = z_exchange([attended[:, r].reshape(local_rows, part) for r in range(groups)])
    attended = jnp.stack(attended)
    attend16 = jnp.concatenate([pick(attended, f_table[i]) for i in range(groups)], axis=1)
    attend16 = attend16[:, :width]

    resid = rows + (mm(attend16, proj_out) + mix_bias)
    unit_two, rate_two = norm_parts(resid)
    second16 = (unit_two * gain_two + shift_two).astype(BF16)

    second_all = ctx_spread(second16.reshape(2, slot, width)).reshape(n_ctx * local_rows, width)
    pre = contract_cols(second_all, up_part) + up_bias_part.astype(F32)
    act, gate_pull = jax.vjp(functools.partial(jax.nn.gelu, approximate=True), pre)
    act16 = act.astype(BF16)
    pre_grad = gate_pull(contract_cols(grads_all, down_part))[0].astype(BF16)
    second_part = mm(pre_grad, up_part).astype(BF16)
    second_grad = ctx_collect(second_part.reshape(n_ctx, 2, slot, width))
    second_grad = second_grad.reshape(local_rows, width).astype(F32)
    resid_grad = grad16.reshape(local_rows, width).astype(F32) + norm_back(
        unit_two, rate_two, gain_two, second_grad
    )
    branch_grad16 = resid_grad.astype(BF16)
    attend_grad = contract_cols(branch_grad16, proj_out).astype(BF16)
    attend_grad = jnp.pad(attend_grad, ((0, 0), (0, groups * part - width)))
    attend_grad = attend_grad.reshape(local_rows, groups, part).transpose(1, 0, 2)
    attend_grad = z_exchange([pick(attend_grad, member ^ r) for r in range(groups)])
    attend_grads = jnp.stack([g.reshape(2, slot, part) for g in attend_grad], axis=1)
    attend_grads = attend_grads.reshape(2, block_len, part)

    query_grad, keyval_grads = in_vmem(
        functools.partial(attend_back_kernel, heads=heads),
        meta,
        (query, keyvals, attend_grads, sums, lse),
        [
            jax.ShapeDtypeStruct((2, block_len, part), BF16),
            jax.ShapeDtypeStruct((blocks, block_len, 2 * part), BF16),
        ],
        [
            pltpu.VMEM((blocks, block_len, 2 * part), F32),
            pltpu.VMEM((part, block_len), F32),
        ],
    )
    keyval_grad = ctx_collect(keyval_grads.reshape(n_ctx, 2, block_len, 2 * part))
    mixed_grad = jnp.concatenate(
        [keyval_grad.reshape(count_rows, 2 * part), query_grad.reshape(count_rows, part)], axis=1
    )
    normed_part = contract_cols(mixed_grad, proj_in[:, : 3 * part])
    normed_pieces = normed_part.astype(BF16).reshape(2, groups, slot, width)
    normed_grad = z_sum([normed_pieces[:, r] for r in range(groups)]).reshape(local_rows, width)
    unit_own, rate_own = norm_parts(rows)
    tokens_grad = resid_grad + norm_back(unit_own, rate_own, gain_one, normed_grad)

    ffn_terms = jnp.concatenate(
        [
            contract_rows(pre_grad, second_all).astype(BF16).reshape(groups, 1, hidden_cut, width),
            contract_rows(act16, grads_all).astype(BF16).reshape(groups, 1, hidden_cut, width),
        ],
        axis=1,
    )
    ffn_term = z_sum([ffn_terms[r] for r in range(groups)]).astype(BF16)
    ffn_grads = ctx_spread(ffn_term)
    ffn_grads = ffn_grads.reshape(n_ctx * 2, hidden_cut, width)
    ffn_grads = shuffle(
        ffn_grads, jnp.concatenate([2 * ctx_table, 2 * ctx_table + 1]), F32
    ).reshape(2, hidden, width)

    feed_part = mm(act16, down_part).astype(BF16)
    feed = ctx_collect(feed_part.reshape(n_ctx, 2, slot, width)).reshape(local_rows, width)
    block_out = (resid + feed.astype(F32) + bias_down).astype(BF16)

    out_term = contract_rows(attend16, branch_grad16).astype(BF16).reshape(groups, share, width)
    out_term = z_sum([pick(out_term, member ^ r) for r in range(groups)]).astype(BF16)
    out_term = rest_total(out_term, fetch_bits).reshape(fetch, share // fetch, width)
    out_term = chip_collect(shuffle(out_term, spread_h ^ chip, BF16))
    mixer_out_grad = shuffle(chip_spread(out_term, fetch_bits), spread_h ^ chip, F32)
    mixer_out_grad = mixer_out_grad.reshape(share, width)

    in_term = contract_rows(normed16, mixed_grad).astype(BF16)
    in_term = rest_total(in_term, fetch_bits).reshape(groups * fetch, share // fetch, 3 * part)
    in_term = shuffle(
        in_term,
        ((spread_f[None, :] ^ member) * fetch + (spread_h[:, None] ^ chip)).reshape(-1),
        BF16,
    ).reshape(fetch, groups, share // fetch, 3 * part)
    in_term = chip_collect(in_term)
    in_term = jnp.stack(z_exchange([in_term[r] for r in range(groups)]))
    in_term = chip_spread(in_term, fetch_bits)
    in_term = shuffle(
        in_term.reshape(fetch * groups, share // fetch, 3 * part),
        ((spread_h[:, None] ^ chip) * groups + (spread_f[None, :] ^ member)).reshape(-1),
        F32,
    ).reshape(fetch, groups, share // fetch, 3, part)
    in_term = in_term.transpose(0, 2, 3, 1, 4).reshape(share, 3, groups * part)[:, :, :width]
    mixer_in_grad = jnp.concatenate([in_term[:, 2], in_term[:, 0], in_term[:, 1]], axis=1)

    early = jnp.stack(
        [
            jnp.sum(branch_grad16.astype(F32), axis=0),
            jnp.sum(second_grad * unit_two, axis=0),
            jnp.sum(second_grad, axis=0),
            jnp.sum(grad16.reshape(local_rows, width).astype(F32), axis=0),
        ]
    )
    early = early.reshape(4, groups, share).transpose(1, 0, 2).reshape(groups, 4 * share)
    up_bias_terms = jnp.sum(pre_grad.astype(F32), axis=0).reshape(groups, hidden_cut)
    up_bias_terms = lax.dynamic_update_slice(
        jnp.zeros((groups, hidden), F32), up_bias_terms, (0, here * hidden_cut)
    )
    early = ctx_total(
        z_sum(
            [
                jnp.concatenate([pick(early, member ^ r), up_bias_terms[r]])[None]
                for r in range(groups)
            ]
        )
    )[0]
    late = jnp.stack([jnp.sum(normed_part * unit_one, axis=0), jnp.sum(normed_part, axis=0)])
    late = late.reshape(2, groups, share).transpose(1, 0, 2).reshape(groups, 1, 2 * share)
    late = ctx_total(z_sum([pick(late, member ^ r) for r in range(groups)]))[0]

    return (
        block_out.reshape(1, 2, slot, width),
        tokens_grad.reshape(1, 2, slot, width),
        late[:share],
        late[share:],
        mixer_in_grad,
        mixer_out_grad,
        early[:share],
        early[share : 2 * share],
        early[2 * share : 3 * share],
        ffn_grads[0],
        early[4 * share :],
        ffn_grads[1],
        early[3 * share : 4 * share],
    )


def solution(mesh):
    in_specs = (
        P("ctx", None, "fsdp", None),
        P(),
        P("fsdp"),
        P("fsdp"),
        P("fsdp", None),
        P("fsdp", None),
        P("fsdp"),
        P("fsdp"),
        P("fsdp"),
        P("fsdp", None),
        P("fsdp"),
        P("fsdp", None),
        P("fsdp"),
        P("ctx", None, "fsdp", None),
    )
    out_specs = (
        P("ctx", None, "fsdp", None),
        P("ctx", None, "fsdp", None),
        P("fsdp"),
        P("fsdp"),
        P("fsdp", None),
        P("fsdp", None),
        P("fsdp"),
        P("fsdp"),
        P("fsdp"),
        P("fsdp", None),
        P("fsdp"),
        P("fsdp", None),
        P("fsdp"),
    )
    return jax.shard_map(
        per_device, mesh=mesh, in_specs=in_specs, out_specs=out_specs, check_vma=False
    )
```

```python
import functools

import jax
import jax.numpy as jnp
from jax import lax
from jax.experimental import pallas as pl
from jax.experimental.pallas import tpu as pltpu
from jax.sharding import PartitionSpec as P

HEADS = 12
HEAD_DIM = 64

EPS = 1e-05
MASKED = -1e30
F32 = jnp.float32
BF16 = jnp.bfloat16
VMEM_LIMIT = 56 * 1024 * 1024


def swap(x, axis, mask):
    return lax.ppermute(x, axis, [(i, i ^ mask) for i in range(lax.axis_size(axis))])


def add16(left, right):
    return (left.astype(F32) + right.astype(F32)).astype(BF16)


def z_gather(x):
    return [x] + [swap(x, "fsdp", r) for r in range(1, lax.axis_size("fsdp"))]


def z_exchange(pieces):
    return [pieces[0]] + [swap(pieces[r], "fsdp", r) for r in range(1, len(pieces))]


def z_sum(pieces):
    return sum(piece.astype(F32) for piece in z_exchange(pieces))


def chip_spread(x, chips):
    return [x] + [swap(x, "ctx", 2 * r) for r in range(1, chips)]


def ctx_spread(x):
    held = chip_spread(x, lax.axis_size("ctx") // 2)
    return held + [swap(piece, "ctx", 1) for piece in held]


def ctx_collect(keep, send):
    came = swap(send, "ctx", 1)
    pieces = [add16(keep[r], came[r]) for r in range(keep.shape[0])]
    return sum(
        piece.astype(F32)
        for piece in [pieces[0]] + [swap(pieces[r], "ctx", 2 * r) for r in range(1, len(pieces))]
    )


def pick(stacked, index):
    return lax.dynamic_index_in_dim(stacked, index, 0, keepdims=False)


def shuffle_kernel(table, x_ref, out_ref):
    width = x_ref.shape[2]
    extra = out_ref.shape[2] - width
    for i in range(out_ref.shape[0]):
        out_ref[i, :, :width] = x_ref[table[i]].astype(out_ref.dtype)
        if extra:
            out_ref[i, :, width:] = jnp.zeros((x_ref.shape[1], extra), out_ref.dtype)


def shuffle(x, table, kind, width=None):
    shape = (table.shape[0], x.shape[1], width or x.shape[2])
    return pl.pallas_call(
        shuffle_kernel,
        grid_spec=pltpu.PrefetchScalarGridSpec(
            num_scalar_prefetch=1,
            grid=(),
            in_specs=[pl.BlockSpec(memory_space=pltpu.VMEM)],
            out_specs=pl.BlockSpec(memory_space=pltpu.VMEM),
        ),
        out_shape=jax.ShapeDtypeStruct(shape, kind),
        compiler_params=pltpu.CompilerParams(vmem_limit_bytes=VMEM_LIMIT),
    )(table, x)


def mm(left, right):
    return jnp.dot(left, right, preferred_element_type=F32)


def contract_rows(left, right):
    return lax.dot_general(left, right, (((0,), (0,)), ((), ())), preferred_element_type=F32)


def contract_cols(left, right):
    return lax.dot_general(left, right, (((1,), (1,)), ((), ())), preferred_element_type=F32)


def head_rows(values, at, heads):
    rows = lax.broadcasted_iota(jnp.int32, values.shape, 0) - at
    return [
        jnp.where((rows >= h * HEAD_DIM) & (rows < (h + 1) * HEAD_DIM), values, 0.0).astype(BF16)
        for h in range(heads)
    ]


def head_cols(values, at, heads):
    cols = lax.broadcasted_iota(jnp.int32, values.shape, 1) - at
    return [
        jnp.where((cols >= h * HEAD_DIM) & (cols < (h + 1) * HEAD_DIM), values, 0.0).astype(BF16)
        for h in range(heads)
    ]


def causal_mask(size, flip):
    keys = lax.broadcasted_iota(jnp.int32, (size, size), 0) ^ flip
    queries = lax.broadcasted_iota(jnp.int32, (size, size), 1) ^ flip
    return keys <= queries


def load_pieces(pieces, kv_ref, sems):
    copies = [
        pltpu.make_async_copy(piece, kv_ref.at[pl.ds(2 * i, 2)], sems.at[i])
        for i, piece in enumerate(pieces)
    ]
    for copy in copies:
        copy.start()
    return copies


def attend_kernel(meta, *refs, heads, pieces, groups):
    q_ref = refs[0]
    piece_refs = refs[1 : 1 + pieces]
    outs = refs[1 + pieces : 1 + pieces + groups]
    sum_ref, lse_ref, kv_ref, sems = refs[1 + pieces + groups :]
    size, wide = q_ref.shape[1:]
    slot = size // groups
    count = 2 * pieces
    width = heads * HEAD_DIM
    scale = HEAD_DIM ** (-0.5)
    copies = load_pieces(piece_refs, kv_ref, sems)
    for copy in copies:
        copy.wait()
    for j in range(2):
        block = meta[count + j]
        turned = head_rows(jnp.transpose(q_ref[j].astype(F32)) * scale, 0, heads)

        def visit(place, carry, diagonal):
            keys = kv_ref[place, :, :wide]
            values = jnp.transpose(kv_ref[place, :, 2 * width - wide :].astype(F32)).astype(BF16)
            later = []
            for h in range(heads):
                score = mm(keys, turned[h])
                if diagonal:
                    score = jnp.where(causal_mask(size, meta[count + 2]), score, MASKED)
                top = jnp.max(score, axis=0, keepdims=True)
                if not diagonal:
                    top = jnp.maximum(top, carry[2 * h])
                weight = jnp.exp(score - top)
                total = jnp.sum(weight, axis=0, keepdims=True)
                at = wide - width + h * HEAD_DIM
                gain = mm(values[at : at + HEAD_DIM], weight.astype(BF16))
                spot = slice(h * HEAD_DIM, (h + 1) * HEAD_DIM)
                if not diagonal:
                    fade = jnp.exp(carry[2 * h] - top)
                    total = total + carry[2 * h + 1] * fade
                    gain = gain + sum_ref[j, spot] * fade
                sum_ref[j, spot] = gain
                later += [top, total]
            return tuple(later)

        carry = visit(j, None, True)
        carry = lax.fori_loop(0, block, lambda n, c: visit(meta[n], c, False), carry)
        for h in range(heads):
            spot = slice(h * HEAD_DIM, (h + 1) * HEAD_DIM)
            sum_ref[j, spot] = sum_ref[j, spot] / carry[2 * h + 1]
            lse_ref[j, h : h + 1] = carry[2 * h] + jnp.log(carry[2 * h + 1])
        result = jnp.transpose(sum_ref[j]).astype(BF16)
        for r in range(groups):
            outs[r][j] = result[r * slot : (r + 1) * slot]


def attend_back_kernel(meta, *refs, heads, pieces, groups):
    q_ref = refs[0]
    piece_refs = refs[1 : 1 + pieces]
    grad_refs = refs[1 + pieces : 1 + pieces + groups]
    sum_ref, lse_ref, dq_ref, keep_ref, send_ref, kv_ref, sems, acc_ref, dq_acc = refs[
        1 + pieces + groups :
    ]
    size, wide = q_ref.shape[1:]
    count = 2 * pieces
    width = heads * HEAD_DIM
    pad = wide - width
    scale = HEAD_DIM ** (-0.5)
    copies = load_pieces(piece_refs, kv_ref, sems)
    acc_ref[...] = jnp.zeros_like(acc_ref)
    for copy in copies:
        copy.wait()
    for j in range(2):
        block = meta[count + j]
        query = q_ref[j].astype(F32) * scale
        plain = head_cols(query, 0, heads)
        turned = head_rows(jnp.transpose(query), 0, heads)
        grad = jnp.concatenate([grad_refs[r][j] for r in range(groups)], axis=0)
        grad_turned = jnp.transpose(grad.astype(F32))
        dots = [
            jnp.sum(
                grad_turned[h * HEAD_DIM : (h + 1) * HEAD_DIM]
                * sum_ref[j, h * HEAD_DIM : (h + 1) * HEAD_DIM],
                axis=0,
                keepdims=True,
            )
            for h in range(heads)
        ]
        if pad:
            grad_turned = jnp.concatenate([jnp.zeros((pad, size), F32), grad_turned], axis=0)
        grads = head_cols(jnp.transpose(grad_turned), pad, heads)
        grads_turned = head_rows(grad_turned, pad, heads)
        dq_acc[...] = jnp.zeros_like(dq_acc)

        def visit(place, diagonal):
            keys = kv_ref[place, :, :wide]
            values = kv_ref[place, :, 2 * width - wide :]
            keys_turned = jnp.transpose(keys.astype(F32)).astype(BF16)
            key_grad = jnp.zeros((size, wide), F32)
            value_grad = jnp.zeros((size, wide), F32)
            for h in range(heads):
                score = mm(keys, turned[h])
                if diagonal:
                    score = jnp.where(causal_mask(size, meta[count + 2]), score, MASKED)
                prob = jnp.exp(score - lse_ref[j, h : h + 1])
                prob_grad = mm(values, grads_turned[h])
                score_grad = (prob * (prob_grad - dots[h])).astype(BF16)
                value_grad += mm(prob.astype(BF16), grads[h])
                key_grad += mm(score_grad, plain[h])
                spot = slice(h * HEAD_DIM, (h + 1) * HEAD_DIM)
                dq_acc[spot] += mm(keys_turned[spot], score_grad)
            acc_ref[place, :, :wide] += key_grad
            acc_ref[place, :, 2 * width - wide :] += value_grad

        visit(j, True)

        def step(n, carry):
            visit(meta[n], False)
            return carry

        lax.fori_loop(0, block, step, 0)
        dq_ref[j] = jnp.transpose(dq_acc[...] * scale).astype(BF16)
    for i in range(pieces):
        to_ref = keep_ref if i < pieces // 2 else send_ref
        to_ref[i % (pieces // 2)] = acc_ref[2 * i : 2 * i + 2].astype(BF16)


def in_grad_kernel(meta, normed_ref, grad_ref, late_ref, keep_ref, send_ref, term_ref, *, cut, share):
    term_ref[...] = contract_rows(normed_ref[...], grad_ref[...])
    here, member = meta[0], meta[1]
    fetch, groups, tall, wide = keep_ref.shape
    for core, to_ref in enumerate((keep_ref, send_ref)):
        for r in range(fetch):
            for z in range(groups):
                owner = member ^ z
                start = owner * share + ((here ^ (2 * r + core)) & (2 * fetch - 1)) * cut
                rows = term_ref[pl.ds(pl.multiple_of(start, 8), cut)]
                to_ref[r, z] = jnp.concatenate([rows, late_ref[owner]], axis=0).astype(BF16)


def in_home_kernel(meta, *refs, cut, fetch, part, width):
    pieces, out_ref, late_ref = refs[:-2], refs[-2], refs[-1]
    here, member = meta[0], meta[1]
    groups = pieces[0].shape[0]
    for i, piece in enumerate(pieces):
        r = 2 * (i % fetch) + i // fetch
        start = pl.multiple_of(((here ^ r) & (2 * fetch - 1)) * cut, 8)
        held = [piece[z ^ member].astype(F32) for z in range(groups)]
        for k, home in enumerate((width, 2 * width, 0)):
            whole = jnp.concatenate([h[:cut, k * part : (k + 1) * part] for h in held], axis=1)
            out_ref[pl.ds(start, cut), home : home + width] = whole[:, :width]
        if i == 0:
            late_ref[...] = sum(h[cut:] for h in held)


def in_vmem(kernel, meta, arrays, outs, scratch=(), flops=0, there=()):
    vmem = pl.BlockSpec(memory_space=pltpu.VMEM)
    anywhere = pl.BlockSpec(memory_space=pl.ANY)
    return pl.pallas_call(
        kernel,
        grid_spec=pltpu.PrefetchScalarGridSpec(
            num_scalar_prefetch=1,
            grid=(),
            in_specs=[anywhere if i in there else vmem for i in range(len(arrays))],
            out_specs=[vmem] * len(outs),
            scratch_shapes=list(scratch),
        ),
        out_shape=outs,
        compiler_params=pltpu.CompilerParams(vmem_limit_bytes=VMEM_LIMIT),
        cost_estimate=pl.CostEstimate(flops=flops, bytes_accessed=1 << 20, transcendentals=0),
    )(meta, *arrays)


def norm_parts(values):
    center = values - jnp.mean(values, axis=-1, keepdims=True)
    rate = lax.rsqrt(jnp.mean(center * center, axis=-1, keepdims=True) + EPS)
    return center * rate, rate


def norm_back(unit, rate, gain, grad):
    e = gain * grad
    return rate * (
        e
        - jnp.mean(e, axis=-1, keepdims=True)
        - unit * jnp.mean(e * unit, axis=-1, keepdims=True)
    )


def after(x, *others):
    return lax.optimization_barrier((x,) + others)[0]


def per_device(
    tokens,
    block_owner,
    first_gain,
    first_shift,
    mixer_in,
    mixer_out,
    mixer_bias,
    second_gain,
    second_shift,
    up_weight,
    up_bias,
    down_weight,
    down_bias,
    out_grad,
):
    groups = lax.axis_size("fsdp")
    member = lax.axis_index("fsdp")
    n_ctx = lax.axis_size("ctx")
    here = lax.axis_index("ctx")
    slot, width = tokens.shape[2:]
    block_len = slot * groups
    local_rows = 2 * slot
    count_rows = 2 * block_len
    blocks = 2 * n_ctx
    share = width // groups
    hidden = up_weight.shape[0]
    hidden_cut = hidden // n_ctx
    heads = -(-HEADS // groups)
    part = heads * HEAD_DIM
    wide = -(-part // 128) * 128
    chips = n_ctx // 2
    fetch = max(f for f in (1, 2, 4, 8, 16) if f <= chips and share % (16 * f) == 0)
    fold = max(f for f in (1, 2, 4, 8, 16) if f <= chips and share % (16 * f) == 0)
    chip = (here // 2) % fetch
    cut = share // (2 * fold)
    spread_f = jnp.arange(groups, dtype=jnp.int32)
    spread_c = jnp.arange(n_ctx, dtype=jnp.int32)
    spread_h = jnp.arange(fetch, dtype=jnp.int32)

    own = tokens.reshape(2, slot, width)
    rows = own.reshape(local_rows, width).astype(F32)
    grad16 = out_grad.reshape(2, slot, width)
    place_index = jnp.stack([here, member]).astype(jnp.int32)

    group_tokens = jnp.stack(z_gather(own), axis=1).reshape(count_rows, width)
    in_cut = lax.dynamic_slice_in_dim(mixer_in, chip * (share // fetch), share // fetch, 0)
    in_cut = in_cut.reshape(-1, 3, width)
    in_cut = jnp.pad(in_cut, ((0, 0), (0, 0), (0, groups * part - width)))
    in_cut = in_cut.reshape(-1, 3, groups, part)
    in_cut = jnp.stack([in_cut[:, 1], in_cut[:, 2], in_cut[:, 0]], axis=2)
    in_cut = in_cut.transpose(1, 0, 2, 3).reshape(groups, share // fetch, 3 * part)
    norm_row = jnp.pad(jnp.concatenate([first_gain, first_shift]), (0, 3 * part - 2 * share))
    norm_rows = jnp.broadcast_to(norm_row, (groups, 16, 3 * part))
    in_cut = jnp.concatenate([in_cut, norm_rows], axis=1)
    in_pieces = jnp.stack(z_exchange([pick(in_cut, member ^ r) for r in range(groups)]))
    norm_nat = jnp.concatenate(
        [pick(in_pieces[:, share // fetch], member ^ r)[None] for r in range(groups)]
    ).astype(F32)
    gain_one = norm_nat[:, :share].reshape(width)
    shift_one = norm_nat[:, share : 2 * share].reshape(width)
    in_parts = jnp.stack(chip_spread(in_pieces[:, : share // fetch], fetch))
    fetch_table = (
        (spread_h[None, :] ^ chip) * groups + (spread_f[:, None] ^ member)
    ).reshape(-1)
    proj_in = shuffle(
        in_parts.reshape(fetch * groups, share // fetch, 3 * part),
        fetch_table,
        BF16,
        2 * part + wide,
    ).reshape(width, 2 * part + wide)

    unit_one, _ = norm_parts(group_tokens.astype(F32))
    normed16 = (unit_one * gain_one + shift_one).astype(BF16)
    mixed = mm(normed16, proj_in).astype(BF16)
    keyval = mixed[:, : 2 * part].reshape(2, block_len, 2 * part)
    query = mixed[:, 2 * part :].reshape(2, block_len, wide)
    keyvals = ctx_spread(keyval)

    owners = block_owner.reshape(-1)
    numbers = jnp.arange(blocks, dtype=jnp.int32)
    places = jnp.sum(jnp.where(owners[None, :] == numbers[:, None], numbers[None, :], 0), axis=1)
    offset = (places // 2) ^ here
    places = (offset % 2) * n_ctx + (offset // 2) * 2 + places % 2
    meta = jnp.concatenate(
        [
            places,
            lax.dynamic_index_in_dim(block_owner, here, 0, keepdims=False),
            (member * slot)[None],
        ]
    ).astype(jnp.int32)

    grads_all = lax.all_gather(grad16.reshape(local_rows, width), "ctx", axis=0, tiled=True)
    order = jnp.concatenate([spread_c[0::2], spread_c[1::2]]) ^ here
    grads_all = shuffle(grads_all.reshape(n_ctx, local_rows, width), order, BF16)
    grads_all = grads_all.reshape(n_ctx * local_rows, width)
    extra = jnp.concatenate([mixer_bias, second_gain, second_shift, down_bias]).reshape(1, 4 * share)
    extra = jnp.concatenate([extra, jnp.pad(up_bias, (0, 4 * share - hidden))[None]])
    extra = jnp.pad(extra, ((0, 14), (0, width - 4 * share)))
    out_pack = after(jnp.concatenate([mixer_out, extra]), group_tokens)
    out_pack = lax.all_gather(out_pack, "fsdp", axis=0, tiled=True)
    out_pack = out_pack.reshape(groups, share + 16, width)
    proj_out = out_pack[:, :share].reshape(width, width)
    mix_bias, gain_two, shift_two, bias_down = (
        out_pack[:, share, i * share : (i + 1) * share].reshape(width).astype(F32)
        for i in range(4)
    )
    up_bias_part = lax.dynamic_slice_in_dim(
        out_pack[:, share + 1], here * hidden_cut, hidden_cut, 1
    ).reshape(groups * hidden_cut)
    ffn_cut = jnp.concatenate(
        [
            lax.dynamic_slice_in_dim(up_weight, here * hidden_cut, hidden_cut, 0),
            lax.dynamic_slice_in_dim(down_weight, here * hidden_cut, hidden_cut, 0),
        ]
    )
    ffn_parts = lax.all_gather(after(ffn_cut, group_tokens), "fsdp", axis=0, tiled=True)
    ffn_parts = ffn_parts.reshape(groups, 2, hidden_cut, width)
    up_part = ffn_parts[:, 0].reshape(groups * hidden_cut, width)
    down_part = ffn_parts[:, 1].reshape(groups * hidden_cut, width)

    attend_flops = 10 * blocks * block_len * block_len * wide * heads
    pair = jax.ShapeDtypeStruct((2, slot, part), BF16)
    results = in_vmem(
        functools.partial(attend_kernel, heads=heads, pieces=n_ctx, groups=groups),
        meta,
        [query] + keyvals,
        [pair] * groups
        + [
            jax.ShapeDtypeStruct((2, part, block_len), F32),
            jax.ShapeDtypeStruct((2, heads, block_len), F32),
        ],
        [
            pltpu.VMEM((blocks, block_len, 2 * part), BF16),
            pltpu.SemaphoreType.DMA((n_ctx,)),
        ],
        attend_flops,
        range(1, 1 + n_ctx),
    )
    sums, lse = results[groups:]
    attended = jnp.stack(z_exchange(results[:groups])).reshape(groups, local_rows, part)
    attend16 = jnp.concatenate([pick(attended, member ^ i) for i in range(groups)], axis=1)
    attend16 = attend16[:, :width]

    resid = rows + (mm(attend16, proj_out) + mix_bias)
    unit_two, rate_two = norm_parts(resid)
    second16 = (unit_two * gain_two + shift_two).astype(BF16)

    second_all = jnp.concatenate(ctx_spread(second16))
    pre = contract_cols(second_all, up_part) + up_bias_part.astype(F32)
    act, gate_pull = jax.vjp(functools.partial(jax.nn.gelu, approximate=True), pre)
    act16 = act.astype(BF16)
    pre_grad = gate_pull(contract_cols(grads_all, down_part))[0].astype(BF16)
    second_part = mm(pre_grad, up_part).astype(BF16).reshape(2, chips, local_rows, width)
    second_grad = ctx_collect(second_part[0], second_part[1])
    resid_grad = grad16.reshape(local_rows, width).astype(F32) + norm_back(
        unit_two, rate_two, gain_two, second_grad
    )
    branch_grad16 = resid_grad.astype(BF16)
    attend_grad = contract_cols(branch_grad16, proj_out).astype(BF16)
    attend_grad = jnp.pad(attend_grad, ((0, 0), (0, groups * part - width)))
    attend_grad = attend_grad.reshape(2, slot, groups, part).transpose(2, 0, 1, 3)
    attend_grads = z_exchange([pick(attend_grad, member ^ r) for r in range(groups)])

    half = jax.ShapeDtypeStruct((chips, 2, block_len, 2 * part), BF16)
    query_grad, keyval_keep, keyval_send = in_vmem(
        functools.partial(attend_back_kernel, heads=heads, pieces=n_ctx, groups=groups),
        meta,
        [query] + keyvals + attend_grads + [sums, lse],
        [jax.ShapeDtypeStruct((2, block_len, part), BF16), half, half],
        [
            pltpu.VMEM((blocks, block_len, 2 * part), BF16),
            pltpu.SemaphoreType.DMA((n_ctx,)),
            pltpu.VMEM((blocks, block_len, 2 * part), F32),
            pltpu.VMEM((part, block_len), F32),
        ],
        attend_flops,
        range(1, 1 + n_ctx),
    )
    keyval_grad = ctx_collect(keyval_keep, keyval_send).astype(BF16)
    mixed_grad = jnp.concatenate(
        [keyval_grad.reshape(count_rows, 2 * part), query_grad.reshape(count_rows, part)], axis=1
    )
    normed_part = contract_cols(mixed_grad, proj_in[:, : 3 * part])
    normed_pieces = normed_part.astype(BF16).reshape(2, groups, slot, width)
    normed_grad = z_sum([normed_pieces[:, r] for r in range(groups)]).reshape(local_rows, width)
    unit_own, rate_own = norm_parts(rows)
    tokens_grad = resid_grad + norm_back(unit_own, rate_own, gain_one, normed_grad)

    late = jnp.stack([jnp.sum(normed_part * unit_one, axis=0), jnp.sum(normed_part, axis=0)])
    late = late.reshape(2, groups, share).transpose(1, 0, 2).reshape(groups, 1, 2 * share)
    late = jnp.pad(late, ((0, 0), (0, 7), (0, 3 * part - 2 * share)))
    tall = cut + 8
    half = jax.ShapeDtypeStruct((fold, groups, tall, 3 * part), BF16)
    in_keep, in_send = in_vmem(
        functools.partial(in_grad_kernel, cut=cut, share=share),
        place_index,
        [normed16, mixed_grad, late],
        [half, half],
        [pltpu.VMEM((width, 3 * part), F32)],
    )
    in_came = swap(in_send, "ctx", 1)
    in_sums = [add16(in_keep[r], in_came[r]) for r in range(fold)]
    in_term = sum(
        piece.astype(F32)
        for piece in [in_sums[0]] + [swap(in_sums[r], "ctx", 2 * r) for r in range(1, fold)]
    ).astype(BF16)
    mask = 2 * fold
    while mask < n_ctx:
        in_term = add16(in_term, swap(in_term, "ctx", mask))
        mask *= 2
    in_term = jnp.stack(z_exchange([in_term[r] for r in range(groups)]))
    in_held = chip_spread(in_term, fold)
    in_held = in_held + [swap(piece, "ctx", 1) for piece in in_held]
    mixer_in_grad, late = in_vmem(
        functools.partial(in_home_kernel, cut=cut, fetch=fold, part=part, width=width),
        place_index,
        in_held,
        [
            jax.ShapeDtypeStruct((share, 3 * width), F32),
            jax.ShapeDtypeStruct((8, 3 * part), F32),
        ],
    )

    ffn_terms = jnp.concatenate(
        [
            contract_rows(pre_grad, second_all).astype(BF16).reshape(groups, hidden_cut, width),
            contract_rows(act16, grads_all).astype(BF16).reshape(groups, hidden_cut, width),
        ],
        axis=1,
    ).reshape(groups * 2 * hidden_cut, width)
    ffn_term = lax.psum_scatter(ffn_terms, "fsdp", scatter_dimension=0, tiled=True)
    ffn_grads = lax.all_gather(ffn_term, "ctx", axis=0, tiled=True)
    ffn_grads = ffn_grads.reshape(n_ctx, 2, hidden_cut, width).astype(F32)

    feed_part = mm(act16, down_part).astype(BF16).reshape(2, chips, local_rows, width)
    feed_part = after(feed_part, branch_grad16)
    feed = ctx_collect(feed_part[0], feed_part[1])
    block_out = (resid + feed + bias_down).astype(BF16)

    early = jnp.stack(
        [
            jnp.sum(branch_grad16.astype(F32), axis=0),
            jnp.sum(second_grad * unit_two, axis=0),
            jnp.sum(second_grad, axis=0),
            jnp.sum(grad16.reshape(local_rows, width).astype(F32), axis=0),
        ]
    )
    early = early.reshape(4, groups, share).transpose(1, 0, 2).reshape(groups, 1, 4 * share)
    up_bias_terms = jnp.sum(pre_grad.astype(F32), axis=0).reshape(groups, 1, hidden_cut)
    up_bias_terms = lax.dynamic_update_slice(
        jnp.zeros((groups, 1, width), F32), up_bias_terms, (0, 0, here * hidden_cut)
    )
    early = jnp.pad(early, ((0, 0), (0, 0), (0, width - 4 * share)))
    early = jnp.concatenate([early, up_bias_terms, jnp.zeros((groups, 14, width), F32)], axis=1)
    out_term = contract_rows(attend16, branch_grad16).reshape(groups, share, width)
    out_term = jnp.concatenate([out_term, early], axis=1).astype(BF16)
    out_term = out_term.reshape(groups * (share + 16), width)
    out_term = lax.psum_scatter(out_term, "fsdp", scatter_dimension=0, tiled=True)
    out_term = lax.psum(out_term, "ctx").astype(F32)

    return (
        block_out.reshape(1, 2, slot, width),
        tokens_grad.reshape(1, 2, slot, width),
        late[0, :share],
        late[0, share : 2 * share],
        mixer_in_grad,
        out_term[:share],
        out_term[share, :share],
        out_term[share, share : 2 * share],
        out_term[share, 2 * share : 3 * share],
        ffn_grads[:, 0].reshape(hidden, width),
        out_term[share + 1, :hidden],
        ffn_grads[:, 1].reshape(hidden, width),
        out_term[share, 3 * share : 4 * share],
    )


def solution(mesh):
    in_specs = (
        P("ctx", None, "fsdp", None),
        P(),
        P("fsdp"),
        P("fsdp"),
        P("fsdp", None),
        P("fsdp", None),
        P("fsdp"),
        P("fsdp"),
        P("fsdp"),
        P("fsdp", None),
        P("fsdp"),
        P("fsdp", None),
        P("fsdp"),
        P("ctx", None, "fsdp", None),
    )
    out_specs = (
        P("ctx", None, "fsdp", None),
        P("ctx", None, "fsdp", None),
        P("fsdp"),
        P("fsdp"),
        P("fsdp", None),
        P("fsdp", None),
        P("fsdp"),
        P("fsdp"),
        P("fsdp"),
        P("fsdp", None),
        P("fsdp"),
        P("fsdp", None),
        P("fsdp"),
    )
    return jax.shard_map(
        per_device, mesh=mesh, in_specs=in_specs, out_specs=out_specs, check_vma=False
    )
```

```python
import functools

import jax
import jax.numpy as jnp
from jax import lax
from jax.experimental import pallas as pl
from jax.experimental.pallas import tpu as pltpu
from jax.sharding import PartitionSpec as P

HEADS = 12
HEAD_DIM = 64

EPS = 1e-05
MASKED = -1e30
F32 = jnp.float32
BF16 = jnp.bfloat16
VMEM_LIMIT = 56 * 1024 * 1024


def swap(x, axis, mask):
    return lax.ppermute(x, axis, [(i, i ^ mask) for i in range(lax.axis_size(axis))])


def add16(left, right):
    return (left.astype(F32) + right.astype(F32)).astype(BF16)


def z_gather(x):
    return [x] + [swap(x, "fsdp", r) for r in range(1, lax.axis_size("fsdp"))]


def z_exchange(pieces):
    return [pieces[0]] + [swap(pieces[r], "fsdp", r) for r in range(1, len(pieces))]


def z_sum(pieces):
    return sum(piece.astype(F32) for piece in z_exchange(pieces))


def chip_spread(x, chips):
    return [x] + [swap(x, "ctx", 2 * r) for r in range(1, chips)]


def ctx_spread(x):
    held = chip_spread(x, lax.axis_size("ctx") // 2)
    return held + [swap(piece, "ctx", 1) for piece in held]


def ctx_collect(keep, send):
    came = swap(send, "ctx", 1)
    pieces = [add16(keep[r], came[r]) for r in range(keep.shape[0])]
    return [pieces[0]] + [swap(pieces[r], "ctx", 2 * r) for r in range(1, len(pieces))]


def pick(stacked, index):
    return lax.dynamic_index_in_dim(stacked, index, 0, keepdims=False)


def shuffle_kernel(table, x_ref, out_ref):
    width = x_ref.shape[2]
    extra = out_ref.shape[2] - width
    for i in range(out_ref.shape[0]):
        out_ref[i, :, :width] = x_ref[table[i]].astype(out_ref.dtype)
        if extra:
            out_ref[i, :, width:] = jnp.zeros((x_ref.shape[1], extra), out_ref.dtype)


def shuffle(x, table, kind, width=None):
    shape = (table.shape[0], x.shape[1], width or x.shape[2])
    return pl.pallas_call(
        shuffle_kernel,
        grid_spec=pltpu.PrefetchScalarGridSpec(
            num_scalar_prefetch=1,
            grid=(),
            in_specs=[pl.BlockSpec(memory_space=pltpu.VMEM)],
            out_specs=pl.BlockSpec(memory_space=pltpu.VMEM),
        ),
        out_shape=jax.ShapeDtypeStruct(shape, kind),
        compiler_params=pltpu.CompilerParams(vmem_limit_bytes=VMEM_LIMIT),
    )(table, x)


def mm(left, right):
    return jnp.dot(left, right, preferred_element_type=F32)


def contract_rows(left, right):
    return lax.dot_general(left, right, (((0,), (0,)), ((), ())), preferred_element_type=F32)


def contract_cols(left, right):
    return lax.dot_general(left, right, (((1,), (1,)), ((), ())), preferred_element_type=F32)


def head_rows(values, at, heads):
    rows = lax.broadcasted_iota(jnp.int32, values.shape, 0) - at
    return [
        jnp.where((rows >= h * HEAD_DIM) & (rows < (h + 1) * HEAD_DIM), values, 0.0).astype(BF16)
        for h in range(heads)
    ]


def head_cols(values, at, heads):
    cols = lax.broadcasted_iota(jnp.int32, values.shape, 1) - at
    return [
        jnp.where((cols >= h * HEAD_DIM) & (cols < (h + 1) * HEAD_DIM), values, 0.0).astype(BF16)
        for h in range(heads)
    ]


def causal_mask(size, flip):
    keys = lax.broadcasted_iota(jnp.int32, (size, size), 0) ^ flip
    queries = lax.broadcasted_iota(jnp.int32, (size, size), 1) ^ flip
    return keys <= queries


def load_pieces(pieces, kv_ref, sems):
    copies = [
        pltpu.make_async_copy(piece, kv_ref.at[pl.ds(2 * i, 2)], sems.at[i])
        for i, piece in enumerate(pieces)
    ]
    for copy in copies:
        copy.start()
    return copies


def attend_kernel(meta, *refs, heads, pieces, groups):
    q_ref = refs[0]
    piece_refs = refs[1 : 1 + pieces]
    outs = refs[1 + pieces : 1 + pieces + groups]
    sum_ref, lse_ref, kv_ref, sems = refs[1 + pieces + groups :]
    size, wide = q_ref.shape[1:]
    slot = size // groups
    count = 2 * pieces
    width = heads * HEAD_DIM
    scale = HEAD_DIM ** (-0.5)
    copies = load_pieces(piece_refs, kv_ref, sems)
    for copy in copies:
        copy.wait()
    for j in range(2):
        block = meta[count + j]
        turned = head_rows(jnp.transpose(q_ref[j].astype(F32)) * scale, 0, heads)

        def visit(place, carry, diagonal):
            keys = kv_ref[place, :, :wide]
            values = jnp.transpose(kv_ref[place, :, 2 * width - wide :].astype(F32)).astype(BF16)
            later = []
            for h in range(heads):
                score = mm(keys, turned[h])
                if diagonal:
                    score = jnp.where(causal_mask(size, meta[count + 2]), score, MASKED)
                top = jnp.max(score, axis=0, keepdims=True)
                if not diagonal:
                    top = jnp.maximum(top, carry[2 * h])
                weight = jnp.exp(score - top)
                total = jnp.sum(weight, axis=0, keepdims=True)
                at = wide - width + h * HEAD_DIM
                gain = mm(values[at : at + HEAD_DIM], weight.astype(BF16))
                spot = slice(h * HEAD_DIM, (h + 1) * HEAD_DIM)
                if not diagonal:
                    fade = jnp.exp(carry[2 * h] - top)
                    total = total + carry[2 * h + 1] * fade
                    gain = gain + sum_ref[j, spot] * fade
                sum_ref[j, spot] = gain
                later += [top, total]
            return tuple(later)

        carry = visit(j, None, True)
        carry = lax.fori_loop(0, block, lambda n, c: visit(meta[n], c, False), carry)
        for h in range(heads):
            spot = slice(h * HEAD_DIM, (h + 1) * HEAD_DIM)
            sum_ref[j, spot] = sum_ref[j, spot] / carry[2 * h + 1]
            lse_ref[j, h : h + 1] = carry[2 * h] + jnp.log(carry[2 * h + 1])
        result = jnp.transpose(sum_ref[j]).astype(BF16)
        for r in range(groups):
            outs[r][j] = result[r * slot : (r + 1) * slot]


def attend_back_kernel(meta, *refs, heads, pieces, groups):
    q_ref = refs[0]
    piece_refs = refs[1 : 1 + pieces]
    grad_refs = refs[1 + pieces : 1 + pieces + groups]
    sum_ref, lse_ref, dq_ref, keep_ref, send_ref, kv_ref, sems, acc_ref, dq_acc = refs[
        1 + pieces + groups :
    ]
    size, wide = q_ref.shape[1:]
    count = 2 * pieces
    width = heads * HEAD_DIM
    pad = wide - width
    scale = HEAD_DIM ** (-0.5)
    copies = load_pieces(piece_refs, kv_ref, sems)
    acc_ref[...] = jnp.zeros_like(acc_ref)
    for copy in copies:
        copy.wait()
    for j in range(2):
        block = meta[count + j]
        query = q_ref[j].astype(F32) * scale
        plain = head_cols(query, 0, heads)
        turned = head_rows(jnp.transpose(query), 0, heads)
        grad = jnp.concatenate([grad_refs[r][j] for r in range(groups)], axis=0)
        grad_turned = jnp.transpose(grad.astype(F32))
        dots = [
            jnp.sum(
                grad_turned[h * HEAD_DIM : (h + 1) * HEAD_DIM]
                * sum_ref[j, h * HEAD_DIM : (h + 1) * HEAD_DIM],
                axis=0,
                keepdims=True,
            )
            for h in range(heads)
        ]
        if pad:
            grad_turned = jnp.concatenate([jnp.zeros((pad, size), F32), grad_turned], axis=0)
        grads = head_cols(jnp.transpose(grad_turned), pad, heads)
        grads_turned = head_rows(grad_turned, pad, heads)
        dq_acc[...] = jnp.zeros_like(dq_acc)

        def visit(place, diagonal):
            keys = kv_ref[place, :, :wide]
            values = kv_ref[place, :, 2 * width - wide :]
            keys_turned = jnp.transpose(keys.astype(F32)).astype(BF16)
            key_grad = jnp.zeros((size, wide), F32)
            value_grad = jnp.zeros((size, wide), F32)
            for h in range(heads):
                score = mm(keys, turned[h])
                if diagonal:
                    score = jnp.where(causal_mask(size, meta[count + 2]), score, MASKED)
                prob = jnp.exp(score - lse_ref[j, h : h + 1])
                prob_grad = mm(values, grads_turned[h])
                score_grad = (prob * (prob_grad - dots[h])).astype(BF16)
                value_grad += mm(prob.astype(BF16), grads[h])
                key_grad += mm(score_grad, plain[h])
                spot = slice(h * HEAD_DIM, (h + 1) * HEAD_DIM)
                dq_acc[spot] += mm(keys_turned[spot], score_grad)
            acc_ref[place, :, :wide] += key_grad
            acc_ref[place, :, 2 * width - wide :] += value_grad

        visit(j, True)

        def step(n, carry):
            visit(meta[n], False)
            return carry

        lax.fori_loop(0, block, step, 0)
        dq_ref[j] = jnp.transpose(dq_acc[...] * scale).astype(BF16)
    for i in range(pieces):
        to_ref = keep_ref if i < pieces // 2 else send_ref
        to_ref[i % (pieces // 2)] = acc_ref[2 * i : 2 * i + 2].astype(BF16)


def project_kernel(meta, *refs, groups, fetch):
    tokens = refs[:groups]
    norm_ref = refs[groups]
    parts = refs[groups + 1 : groups + 1 + fetch]
    kv_ref, q_ref, normed_ref, unit_ref, proj_ref = refs[groups + 1 + fetch :]
    member, chip = meta[1], meta[2]
    depth, across = proj_ref.shape
    share = depth // groups
    for c in range(fetch):
        for z in range(groups):
            start = (member ^ z) * share + (chip ^ c) * (share // fetch)
            proj_ref[pl.ds(pl.multiple_of(start, 16), share // fetch)] = parts[c][z]
    rows = [norm_ref[member ^ z][:1].astype(F32) for z in range(groups)]
    gain = jnp.concatenate([row[:, :share] for row in rows], axis=1)
    shift = jnp.concatenate([row[:, share : 2 * share] for row in rows], axis=1)
    part2 = kv_ref.shape[2]
    wide = q_ref.shape[2]
    size = kv_ref.shape[1]
    for j in range(2):
        x = jnp.concatenate([ref[j] for ref in tokens], axis=0).astype(F32)
        unit, _ = norm_parts(x)
        normed = (unit * gain + shift).astype(BF16)
        unit_ref[j] = unit
        normed_ref[j] = normed
        mixed = mm(normed, proj_ref[...]).astype(BF16)
        kv_ref[j] = mixed[:, :part2]
        q_ref[j, :, : across - part2] = mixed[:, part2:]
        if wide > across - part2:
            q_ref[j, :, across - part2 :] = jnp.zeros((size, wide - across + part2), BF16)


def second_kernel(meta, *refs, groups):
    pieces = refs[:groups]
    x_ref, proj_ref, vec_ref, resid_ref, second_ref = refs[groups:]
    member = meta[1]
    slot, part = pieces[0].shape[1:]
    total = x_ref[...].astype(F32) + vec_ref[0:1]
    for z in range(groups):
        total += mm(pieces[z][...].reshape(2 * slot, part), proj_ref[member ^ z])
    resid_ref[...] = total
    unit, _ = norm_parts(total)
    second_ref[...] = (unit * vec_ref[1:2] + vec_ref[2:3]).astype(BF16)


def branch_kernel(meta, *refs, groups, chips):
    sums = refs[:chips]
    resid_ref, grad_ref, proj_ref, vec_ref = refs[chips : chips + 4]
    outs = refs[chips + 4 : chips + 4 + groups]
    resid_grad_ref, branch_ref, totals_ref = refs[chips + 4 + groups :]
    member = meta[1]
    slot, part = outs[0].shape[1:]
    second_grad = sum(ref[...].astype(F32) for ref in sums)
    unit, rate = norm_parts(resid_ref[...])
    dout = grad_ref[...].astype(F32)
    resid_grad = dout + norm_back(unit, rate, vec_ref[1:2], second_grad)
    resid_grad_ref[...] = resid_grad
    branch = resid_grad.astype(BF16)
    branch_ref[...] = branch
    for z in range(groups):
        grads = contract_cols(branch, proj_ref[member ^ z]).astype(BF16)
        outs[z][...] = grads.reshape(2, slot, part)
    totals_ref[0:1] = jnp.sum(branch.astype(F32), axis=0, keepdims=True)
    totals_ref[1:2] = jnp.sum(second_grad * unit, axis=0, keepdims=True)
    totals_ref[2:3] = jnp.sum(second_grad, axis=0, keepdims=True)
    totals_ref[3:4] = jnp.sum(dout, axis=0, keepdims=True)
    totals_ref[4:] = jnp.zeros((4, totals_ref.shape[1]), F32)


def handed_kernel(meta, *refs, groups, chips, cut, share, with_out):
    sums = refs[:chips]
    dq_ref, normed_ref, unit_ref, proj_ref, totals_ref, up_bias_ref = refs[chips : chips + 6]
    at = chips + 6
    attended = refs[at : at + groups] if with_out else ()
    branches = refs[at + groups] if with_out else None
    at += (groups + 1) * with_out
    outs = refs[at : at + groups]
    keep_ref, send_ref, grad_ref, term_ref, out_term_ref, vec_ref = refs[at + groups :]
    here, member = meta[0], meta[1]
    fetch = keep_ref.shape[0]
    across = keep_ref.shape[3]
    part2 = sums[0].shape[2]
    slot = outs[0].shape[1]
    size = slot * groups
    width = unit_ref.shape[2]
    gain_total = jnp.zeros((1, width), F32)
    shift_total = jnp.zeros((1, width), F32)
    for j in range(2):
        keyval = sum(ref[j].astype(F32) for ref in sums).astype(BF16)
        grad = jnp.concatenate([keyval, dq_ref[j]], axis=1)
        grad_ref[j] = grad
        normed_grad = contract_cols(grad, proj_ref[...])
        gain_total += jnp.sum(normed_grad * unit_ref[j], axis=0, keepdims=True)
        shift_total += jnp.sum(normed_grad, axis=0, keepdims=True)
        for z in range(groups):
            outs[z][j] = normed_grad[z * slot : (z + 1) * slot].astype(BF16)
    term_ref[...] = contract_rows(
        normed_ref[...].reshape(2 * size, width), grad_ref[...].reshape(2 * size, across)
    )
    if with_out:
        out_term_ref[...] = sum(
            contract_rows(piece[...].reshape(2 * slot, share), branches[z])
            for z, piece in enumerate(attended)
        )
    hidden = up_bias_ref.shape[1]
    vec_ref[...] = jnp.zeros_like(vec_ref)
    for z in range(groups):
        cols = slice(z * share, (z + 1) * share)
        vec_ref[z, 0:1, :share] = gain_total[:, cols]
        vec_ref[z, 0:1, share : 2 * share] = shift_total[:, cols]
        vec_ref[z, 1:2, :share] = totals_ref[0:1, cols]
        vec_ref[z, 1:2, share : 2 * share] = totals_ref[1:2, cols]
        vec_ref[z, 2:3, :share] = totals_ref[2:3, cols]
        vec_ref[z, 2:3, share : 2 * share] = totals_ref[3:4, cols]
        done = 0
        while done < hidden:
            size_now = min(across, hidden - done)
            row = 3 + done // across
            vec_ref[z, row : row + 1, :size_now] = up_bias_ref[z : z + 1, done : done + size_now]
            done += size_now
    for core, to_ref in enumerate((keep_ref, send_ref)):
        for r in range(fetch):
            mine = ((here ^ (2 * r + core)) & (2 * fetch - 1)) * cut
            for z in range(groups):
                owner = member ^ z
                start = pl.multiple_of(owner * share + mine, 8)
                rows = term_ref[pl.ds(start, cut)]
                to_ref[r, z] = jnp.concatenate([rows, vec_ref[owner]], axis=0).astype(BF16)
            if with_out:
                rows = out_term_ref[pl.ds(pl.multiple_of(mine, 8), cut)]
                rest = jnp.concatenate(
                    [rows[8 * i : 8 * i + 8, across:] for i in range(cut // 8)], axis=1
                )
                to_ref[r, groups] = jnp.concatenate([rows[:, :across], rest], axis=0).astype(BF16)


def home_kernel(meta, *refs, groups, cut, fetch, part, width, with_out):
    pieces = refs[: 2 * fetch]
    out_ref, out_out_ref = refs[2 * fetch :]
    here, member = meta[0], meta[1]
    across = 3 * part
    for i, piece in enumerate(pieces):
        r = 2 * (i % fetch) + i // fetch
        start = pl.multiple_of(((here ^ r) & (2 * fetch - 1)) * cut, 8)
        held = [piece[z ^ member].astype(F32) for z in range(groups)]
        for k, home in enumerate((width, 2 * width, 0)):
            whole = jnp.concatenate([h[:cut, k * part : (k + 1) * part] for h in held], axis=1)
            out_ref[pl.ds(start, cut), home : home + width] = whole[:, :width]
        if with_out:
            block = piece[groups].astype(F32)
            rest = jnp.concatenate(
                [
                    block[cut : cut + 8, i * (width - across) : (i + 1) * (width - across)]
                    for i in range(cut // 8)
                ],
                axis=0,
            )
            out_out_ref[pl.ds(start, cut)] = jnp.concatenate([block[:cut], rest], axis=1)
        elif i == 0:
            out_out_ref[...] = jnp.zeros_like(out_out_ref)


def tokens_kernel(meta, grad_ref, x_ref, gain_ref, resid_grad_ref, out_ref):
    rows, width = x_ref.shape
    grad = grad_ref[...].astype(F32).reshape(rows, width)
    unit, rate = norm_parts(x_ref[...].astype(F32))
    out_ref[...] = resid_grad_ref[...] + norm_back(unit, rate, gain_ref[...], grad)


def in_vmem(kernel, meta, arrays, outs, scratch=(), flops=0, there=()):
    vmem = pl.BlockSpec(memory_space=pltpu.VMEM)
    anywhere = pl.BlockSpec(memory_space=pl.ANY)
    return pl.pallas_call(
        kernel,
        grid_spec=pltpu.PrefetchScalarGridSpec(
            num_scalar_prefetch=1,
            grid=(),
            in_specs=[anywhere if i in there else vmem for i in range(len(arrays))],
            out_specs=[vmem] * len(outs),
            scratch_shapes=list(scratch),
        ),
        out_shape=outs,
        compiler_params=pltpu.CompilerParams(vmem_limit_bytes=VMEM_LIMIT),
        cost_estimate=pl.CostEstimate(flops=flops, bytes_accessed=1 << 20, transcendentals=0),
    )(meta, *arrays)


def norm_parts(values):
    center = values - jnp.mean(values, axis=-1, keepdims=True)
    rate = lax.rsqrt(jnp.mean(center * center, axis=-1, keepdims=True) + EPS)
    return center * rate, rate


def norm_back(unit, rate, gain, grad):
    e = gain * grad
    return rate * (
        e
        - jnp.mean(e, axis=-1, keepdims=True)
        - unit * jnp.mean(e * unit, axis=-1, keepdims=True)
    )


def after(x, *others):
    return lax.optimization_barrier((x,) + others)[0]


def per_device(
    tokens,
    block_owner,
    first_gain,
    first_shift,
    mixer_in,
    mixer_out,
    mixer_bias,
    second_gain,
    second_shift,
    up_weight,
    up_bias,
    down_weight,
    down_bias,
    out_grad,
):
    groups = lax.axis_size("fsdp")
    member = lax.axis_index("fsdp")
    n_ctx = lax.axis_size("ctx")
    here = lax.axis_index("ctx")
    slot, width = tokens.shape[2:]
    block_len = slot * groups
    local_rows = 2 * slot
    count_rows = 2 * block_len
    blocks = 2 * n_ctx
    share = width // groups
    hidden = up_weight.shape[0]
    hidden_cut = hidden // n_ctx
    heads = -(-HEADS // groups)
    part = heads * HEAD_DIM
    wide = -(-part // 128) * 128
    chips = n_ctx // 2
    fetch = max(f for f in (1, 2, 4, 8, 16) if f <= chips and share % (16 * f) == 0)
    fold = max(f for f in (1, 2, 4, 8, 16) if f <= chips and share % (16 * f) == 0)
    chip = (here // 2) % fetch
    cut = share // (2 * fold)
    spread_c = jnp.arange(n_ctx, dtype=jnp.int32)

    own = tokens.reshape(2, slot, width)
    rows16 = tokens.reshape(local_rows, width)
    grad16 = out_grad.reshape(local_rows, width)
    index = jnp.stack([here, member, chip]).astype(jnp.int32)

    in_cut = lax.dynamic_slice_in_dim(mixer_in, chip * (share // fetch), share // fetch, 0)
    in_cut = in_cut.reshape(-1, 3, width)
    in_cut = jnp.pad(in_cut, ((0, 0), (0, 0), (0, groups * part - width)))
    in_cut = in_cut.reshape(-1, 3, groups, part)
    in_cut = jnp.stack([in_cut[:, 1], in_cut[:, 2], in_cut[:, 0]], axis=2)
    in_cut = in_cut.transpose(1, 0, 2, 3).reshape(groups, share // fetch, 3 * part)
    norm_row = jnp.pad(jnp.concatenate([first_gain, first_shift]), (0, 3 * part - 2 * share))
    norm_rows = jnp.broadcast_to(norm_row, (groups, 16, 3 * part))
    in_cut = jnp.concatenate([in_cut, norm_rows], axis=1)
    in_pieces = z_exchange([pick(in_cut, member ^ r) for r in range(groups)])
    in_pieces = jnp.stack(in_pieces)
    group_tokens = z_gather(after(own, in_pieces))
    norm_part = in_pieces[:, share // fetch :]
    in_parts = chip_spread(in_pieces[:, : share // fetch], fetch)
    group_tokens = after(tuple(group_tokens), *in_parts)
    gain_one = jnp.concatenate(
        [pick(norm_part[:, 0, :share], member ^ r)[None] for r in range(groups)]
    ).reshape(1, width).astype(F32)

    pieces = jax.ShapeDtypeStruct((2, block_len, width), BF16)
    keyval, query, normed16, unit_one, proj_in = in_vmem(
        functools.partial(project_kernel, groups=groups, fetch=fetch),
        index,
        list(group_tokens) + [norm_part] + in_parts,
        [
            jax.ShapeDtypeStruct((2, block_len, 2 * part), BF16),
            jax.ShapeDtypeStruct((2, block_len, wide), BF16),
            pieces,
            jax.ShapeDtypeStruct((2, block_len, width), F32),
            jax.ShapeDtypeStruct((width, 3 * part), BF16),
        ],
    )
    keyvals = chip_spread(keyval, chips)

    owners = block_owner.reshape(-1)
    numbers = jnp.arange(blocks, dtype=jnp.int32)
    places = jnp.sum(jnp.where(owners[None, :] == numbers[:, None], numbers[None, :], 0), axis=1)
    offset = (places // 2) ^ here
    places = (offset % 2) * n_ctx + (offset // 2) * 2 + places % 2
    meta = jnp.concatenate(
        [
            places,
            lax.dynamic_index_in_dim(block_owner, here, 0, keepdims=False),
            (member * slot)[None],
        ]
    ).astype(jnp.int32)

    grads_all = lax.all_gather(grad16, "ctx", axis=0, tiled=True)
    order = jnp.concatenate([spread_c[0::2], spread_c[1::2]]) ^ here
    grads_all = shuffle(grads_all.reshape(n_ctx, local_rows, width), order, BF16)
    grads_all = grads_all.reshape(n_ctx * local_rows, width)
    extra = jnp.concatenate([mixer_bias, second_gain, second_shift, down_bias]).reshape(1, 4 * share)
    extra = jnp.concatenate([extra, jnp.pad(up_bias, (0, 4 * share - hidden))[None]])
    extra = jnp.pad(extra, ((0, 14), (0, width - 4 * share)))
    out_pack = after(jnp.concatenate([mixer_out, extra]), *group_tokens)
    out_pack = lax.all_gather(out_pack, "fsdp", axis=0, tiled=True)
    out_pack = out_pack.reshape(groups, share + 16, width)
    proj_out = out_pack[:, :share].reshape(width, width)
    proj_out = jnp.pad(proj_out, ((0, groups * part - width), (0, 0)))
    proj_out = proj_out.reshape(groups, part, width)
    vectors = jnp.concatenate(
        [out_pack[:, share, i * share : (i + 1) * share].reshape(1, width) for i in range(4)]
        + [jnp.zeros((4, width), BF16)]
    ).astype(F32)
    up_bias_part = lax.dynamic_slice_in_dim(
        out_pack[:, share + 1], here * hidden_cut, hidden_cut, 1
    ).reshape(groups * hidden_cut)
    *keyvals, grads_all = lax.optimization_barrier((*keyvals, grads_all))
    keyvals = keyvals + [swap(piece, "ctx", 1) for piece in keyvals]
    ffn_cut = jnp.concatenate(
        [
            lax.dynamic_slice_in_dim(up_weight, here * hidden_cut, hidden_cut, 0),
            lax.dynamic_slice_in_dim(down_weight, here * hidden_cut, hidden_cut, 0),
        ]
    )
    ffn_parts = lax.all_gather(after(ffn_cut, grads_all), "fsdp", axis=0, tiled=True)
    ffn_parts = ffn_parts.reshape(groups, 2, hidden_cut, width)
    up_part = ffn_parts[:, 0].reshape(groups * hidden_cut, width)
    down_part = ffn_parts[:, 1].reshape(groups * hidden_cut, width)

    attend_flops = 40 * blocks * block_len * block_len * wide * heads
    pair = jax.ShapeDtypeStruct((2, slot, part), BF16)
    results = in_vmem(
        functools.partial(attend_kernel, heads=heads, pieces=n_ctx, groups=groups),
        meta,
        [query] + keyvals,
        [pair] * groups
        + [
            jax.ShapeDtypeStruct((2, part, block_len), F32),
            jax.ShapeDtypeStruct((2, heads, block_len), F32),
        ],
        [
            pltpu.VMEM((blocks, block_len, 2 * part), BF16),
            pltpu.SemaphoreType.DMA((n_ctx,)),
        ],
        attend_flops,
        range(1, 1 + n_ctx),
    )
    own_attended = results[:groups]
    sums, lse = results[groups:]
    attended = z_exchange(results[:groups])
    proj_out, vectors, *attended = lax.optimization_barrier((proj_out, vectors, *attended))
    resid, second16 = in_vmem(
        functools.partial(second_kernel, groups=groups),
        index,
        attended + [rows16, proj_out, vectors],
        [
            jax.ShapeDtypeStruct((local_rows, width), F32),
            jax.ShapeDtypeStruct((local_rows, width), BF16),
        ],
    )

    second_all = jnp.concatenate(ctx_spread(second16))
    pre = contract_cols(second_all, up_part) + up_bias_part.astype(F32)
    act, gate_pull = jax.vjp(functools.partial(jax.nn.gelu, approximate=True), pre)
    act16 = act.astype(BF16)
    pre_grad = gate_pull(contract_cols(grads_all, down_part))[0].astype(BF16)
    second_part = mm(pre_grad, up_part).astype(BF16).reshape(2, chips, local_rows, width)
    up_term = contract_rows(pre_grad, second_all).astype(BF16)
    down_term = contract_rows(act16, grads_all).astype(BF16)
    feed_part = mm(act16, down_part).astype(BF16)
    second_sums = ctx_collect(second_part[0], second_part[1])
    back_order = spread_c ^ here
    back_order = (back_order % 2) * chips + back_order // 2
    feed = shuffle(feed_part.reshape(n_ctx, local_rows, width), back_order, BF16)
    feed = feed.reshape(n_ctx * local_rows, width)
    ffn_terms = jnp.concatenate(
        [
            up_term.reshape(groups, hidden_cut, width),
            down_term.reshape(groups, hidden_cut, width),
        ],
        axis=1,
    ).reshape(groups * 2 * hidden_cut, width)
    feed, ffn_terms, *second_sums = lax.optimization_barrier((feed, ffn_terms, *second_sums))
    feed = lax.psum_scatter(feed, "ctx", scatter_dimension=0, tiled=True)
    results = in_vmem(
        functools.partial(branch_kernel, groups=groups, chips=chips),
        index,
        second_sums + [resid, grad16, proj_out, vectors],
        [pair] * groups
        + [
            jax.ShapeDtypeStruct((local_rows, width), F32),
            jax.ShapeDtypeStruct((local_rows, width), BF16),
            jax.ShapeDtypeStruct((8, width), F32),
        ],
    )
    resid_grad, branch_grad16, totals = results[groups:]
    attend_grads = z_exchange(results[:groups])
    branches = branch_grad16[None]
    branches = jnp.concatenate([branches, swap(branches, "fsdp", 1)])
    branches, *attend_grads = lax.optimization_barrier((branches, *attend_grads))
    mask = 2
    while mask < groups:
        branches = jnp.concatenate([branches, swap(branches, "fsdp", mask)])
        mask *= 2

    half = jax.ShapeDtypeStruct((chips, 2, block_len, 2 * part), BF16)
    query_grad, keyval_keep, keyval_send = in_vmem(
        functools.partial(attend_back_kernel, heads=heads, pieces=n_ctx, groups=groups),
        meta,
        [query] + keyvals + attend_grads + [sums, lse],
        [jax.ShapeDtypeStruct((2, block_len, part), BF16), half, half],
        [
            pltpu.VMEM((blocks, block_len, 2 * part), BF16),
            pltpu.SemaphoreType.DMA((n_ctx,)),
            pltpu.VMEM((blocks, block_len, 2 * part), F32),
            pltpu.VMEM((part, block_len), F32),
        ],
        attend_flops,
        range(1, 1 + n_ctx),
    )
    keyval_sums = ctx_collect(keyval_keep, after(keyval_send, branches, feed))

    ffn_terms = after(ffn_terms, branches, query_grad)
    ffn_term = lax.psum_scatter(ffn_terms, "fsdp", scatter_dimension=0, tiled=True)

    with_out = part == share and (cut // 8) * (width - 3 * part) == 3 * part
    up_bias_terms = jnp.sum(pre_grad.astype(F32), axis=0).reshape(groups, hidden_cut)
    up_bias_terms = lax.dynamic_update_slice(
        jnp.zeros((groups, hidden), F32), up_bias_terms, (0, here * hidden_cut)
    )
    half = jax.ShapeDtypeStruct((fold, groups + with_out, cut + 8, 3 * part), BF16)
    results = in_vmem(
        functools.partial(
            handed_kernel, groups=groups, chips=chips, cut=cut, share=share, with_out=with_out
        ),
        index,
        keyval_sums
        + [query_grad, normed16, unit_one, proj_in, totals, up_bias_terms]
        + (list(own_attended) + [branches] if with_out else []),
        [jax.ShapeDtypeStruct((2, slot, width), BF16)] * groups + [half, half],
        [
            pltpu.VMEM((2, block_len, 3 * part), BF16),
            pltpu.VMEM((width, 3 * part), F32),
            pltpu.VMEM((share, width), F32),
            pltpu.VMEM((groups, 8, 3 * part), F32),
        ],
    )
    in_keep, in_send = results[groups:]
    ffn_grads = lax.all_gather(after(ffn_term, in_keep), "ctx", axis=0, tiled=True)
    in_sums = ctx_collect(in_keep, in_send)
    normed_pieces = list(results[:groups])
    mask = groups // 2
    while mask:
        came = swap(jnp.stack(normed_pieces[mask:]), "fsdp", mask)
        if mask == groups // 2:
            came, *in_sums = lax.optimization_barrier((came, *in_sums))
        normed_pieces = [add16(piece, came[i]) for i, piece in enumerate(normed_pieces[:mask])]
        mask //= 2
    normed_grad = normed_pieces[0]
    in_term = sum(piece.astype(F32) for piece in in_sums).astype(BF16)
    mask = 2 * fold
    while mask < n_ctx:
        in_term = add16(in_term, swap(in_term, "ctx", mask))
        mask *= 2
    handed = z_exchange([in_term[r] for r in range(groups)])
    small = sum(piece[cut:].astype(F32) for piece in handed)
    in_term = jnp.stack(handed + [in_term[groups]] if with_out else handed)
    in_held = chip_spread(in_term, fold)
    in_held = in_held + [swap(piece, "ctx", 1) for piece in in_held]
    tokens_grad = in_vmem(
        tokens_kernel,
        index,
        [normed_grad, rows16, gain_one, resid_grad],
        [jax.ShapeDtypeStruct((local_rows, width), F32)],
    )[0]
    block_out = (resid + feed.astype(F32) + vectors[3:4]).astype(BF16)

    ffn_grads = ffn_grads.reshape(n_ctx, 2, hidden_cut, width).astype(F32)
    up_grad = ffn_grads[:, 0].reshape(hidden, width)
    down_grad = ffn_grads[:, 1].reshape(hidden, width)
    up_grad, down_grad, tokens_grad, *in_held = lax.optimization_barrier(
        (up_grad, down_grad, tokens_grad, *in_held)
    )
    mixer_in_grad, mixer_out_grad = in_vmem(
        functools.partial(
            home_kernel,
            groups=groups,
            cut=cut,
            fetch=fold,
            part=part,
            width=width,
            with_out=with_out,
        ),
        index,
        in_held,
        [
            jax.ShapeDtypeStruct((share, 3 * width), F32),
            jax.ShapeDtypeStruct((share, width), F32),
        ],
    )

    if not with_out:
        whole = jnp.stack(attended).reshape(groups, local_rows, part)
        whole = jnp.concatenate([pick(whole, member ^ i) for i in range(groups)], axis=1)
        out_term = contract_rows(whole[:, :width], branch_grad16).astype(BF16)
        out_term = lax.psum_scatter(out_term, "fsdp", scatter_dimension=0, tiled=True)
        mixer_out_grad = lax.psum(out_term, "ctx").astype(F32)

    bias_rows = -(-hidden // (3 * part))
    up_bias_grad = small[3 : 3 + bias_rows].reshape(-1)[:hidden]
    return (
        block_out.reshape(1, 2, slot, width),
        tokens_grad.reshape(1, 2, slot, width),
        small[0, :share],
        small[0, share : 2 * share],
        mixer_in_grad,
        mixer_out_grad,
        small[1, :share],
        small[1, share : 2 * share],
        small[2, :share],
        up_grad,
        up_bias_grad,
        down_grad,
        small[2, share : 2 * share],
    )


def solution(mesh):
    in_specs = (
        P("ctx", None, "fsdp", None),
        P(),
        P("fsdp"),
        P("fsdp"),
        P("fsdp", None),
        P("fsdp", None),
        P("fsdp"),
        P("fsdp"),
        P("fsdp"),
        P("fsdp", None),
        P("fsdp"),
        P("fsdp", None),
        P("fsdp"),
        P("ctx", None, "fsdp", None),
    )
    out_specs = (
        P("ctx", None, "fsdp", None),
        P("ctx", None, "fsdp", None),
        P("fsdp"),
        P("fsdp"),
        P("fsdp", None),
        P("fsdp", None),
        P("fsdp"),
        P("fsdp"),
        P("fsdp"),
        P("fsdp", None),
        P("fsdp"),
        P("fsdp", None),
        P("fsdp"),
    )
    return jax.shard_map(
        per_device, mesh=mesh, in_specs=in_specs, out_specs=out_specs, check_vma=False
    )
```

```python
import functools

import jax
import jax.numpy as jnp
from jax import lax
from jax.experimental import pallas as pl
from jax.experimental.pallas import tpu as pltpu
from jax.sharding import PartitionSpec as P

HEADS = 12
HEAD_DIM = 64

EPS = 1e-05
MASKED = -1e30
F32 = jnp.float32
BF16 = jnp.bfloat16
VMEM_LIMIT = 56 * 1024 * 1024


def swap(x, axis, mask):
    return lax.ppermute(x, axis, [(i, i ^ mask) for i in range(lax.axis_size(axis))])


def add16(left, right):
    return (left.astype(F32) + right.astype(F32)).astype(BF16)


def z_gather(x):
    return [x] + [swap(x, "fsdp", r) for r in range(1, lax.axis_size("fsdp"))]


def z_exchange(pieces):
    return [pieces[0]] + [swap(pieces[r], "fsdp", r) for r in range(1, len(pieces))]


def z_sum(pieces):
    return sum(piece.astype(F32) for piece in z_exchange(pieces))


def chip_spread(x, chips):
    return [x] + [swap(x, "ctx", 2 * r) for r in range(1, chips)]


def ctx_spread(x):
    held = chip_spread(x, lax.axis_size("ctx") // 2)
    return held + [swap(piece, "ctx", 1) for piece in held]


def ctx_collect(keep, send):
    came = swap(send, "ctx", 1)
    pieces = [add16(keep[r], came[r]) for r in range(keep.shape[0])]
    return [pieces[0]] + [swap(pieces[r], "ctx", 2 * r) for r in range(1, len(pieces))]


def pick(stacked, index):
    return lax.dynamic_index_in_dim(stacked, index, 0, keepdims=False)


def shuffle_kernel(table, x_ref, out_ref):
    width = x_ref.shape[2]
    extra = out_ref.shape[2] - width
    for i in range(out_ref.shape[0]):
        out_ref[i, :, :width] = x_ref[table[i]].astype(out_ref.dtype)
        if extra:
            out_ref[i, :, width:] = jnp.zeros((x_ref.shape[1], extra), out_ref.dtype)


def shuffle(x, table, kind, width=None):
    shape = (table.shape[0], x.shape[1], width or x.shape[2])
    return pl.pallas_call(
        shuffle_kernel,
        grid_spec=pltpu.PrefetchScalarGridSpec(
            num_scalar_prefetch=1,
            grid=(),
            in_specs=[pl.BlockSpec(memory_space=pltpu.VMEM)],
            out_specs=pl.BlockSpec(memory_space=pltpu.VMEM),
        ),
        out_shape=jax.ShapeDtypeStruct(shape, kind),
        compiler_params=pltpu.CompilerParams(vmem_limit_bytes=VMEM_LIMIT),
    )(table, x)


def mm(left, right):
    return jnp.dot(left, right, preferred_element_type=F32)


def contract_rows(left, right):
    return lax.dot_general(left, right, (((0,), (0,)), ((), ())), preferred_element_type=F32)


def contract_cols(left, right):
    return lax.dot_general(left, right, (((1,), (1,)), ((), ())), preferred_element_type=F32)


def head_cols(values, at, heads):
    cols = lax.broadcasted_iota(jnp.int32, values.shape, 1) - at
    return [
        jnp.where((cols >= h * HEAD_DIM) & (cols < (h + 1) * HEAD_DIM), values, 0.0).astype(BF16)
        for h in range(heads)
    ]


def causal_mask(heads, size, flip):
    queries = lax.broadcasted_iota(jnp.int32, (heads * size, size), 0) % size ^ flip
    keys = lax.broadcasted_iota(jnp.int32, (heads * size, size), 1) ^ flip
    return keys <= queries


def lanes(combine, values):
    return functools.reduce(
        combine, [values[:, i : i + 128] for i in range(0, values.shape[1], 128)]
    )


def widen(values, width):
    return jnp.concatenate([values] * (width // 128), axis=1)


def load_pieces(pieces, kv_ref, sems):
    copies = [
        pltpu.make_async_copy(piece, kv_ref.at[pl.ds(2 * i, 2)], sems.at[i])
        for i, piece in enumerate(pieces)
    ]
    for copy in copies:
        copy.start()
    return copies


def in_pairs(start, stop, step):
    def both(i, carry):
        step((start + 2 * i, start + 2 * i + 1))
        return carry

    def one(n, carry):
        step((n,))
        return carry

    half = (stop - start) // 2
    lax.fori_loop(0, half, both, 0)
    lax.fori_loop(start + 2 * half, stop, one, 0)


def attend_kernel(meta, *refs, heads, pieces, groups, rows):
    q_ref = refs[0]
    piece_refs = refs[1 : 1 + pieces]
    outs = refs[1 + pieces : 1 + pieces + groups]
    sum_ref, lse_ref, kv_ref, sems, score_ref, top_ref, total_ref, acc_ref = refs[
        1 + pieces + groups :
    ]
    size, wide = q_ref.shape[1:]
    slot = size // groups
    count = 2 * pieces
    width = heads * HEAD_DIM
    scale = HEAD_DIM ** (-0.5)
    copies = load_pieces(piece_refs, kv_ref, sems)
    for copy in copies:
        copy.wait()
    for j in range(2):
        block = meta[count + j]
        for tile in range(size // rows):
            spot = pl.ds(tile * rows, rows)
            query = jnp.concatenate(head_cols(q_ref[j, spot].astype(F32) * scale, 0, heads), axis=0)

            def score(n):
                return contract_cols(query, kv_ref[meta[n], :, :wide])

            def scores(ns):
                found = [score(n) for n in ns]
                top = top_ref[...]
                for n, value in zip(ns, found, strict=True):
                    score_ref[n] = value
                    top = jnp.maximum(top, lanes(jnp.maximum, value))
                top_ref[...] = top

            def weights(ns):
                total = total_ref[...]
                acc = acc_ref[...]
                top = widen(top_ref[...], size)
                for n in ns:
                    weight = jnp.exp(score_ref[n] - top)
                    total += lanes(jnp.add, weight)
                    acc += mm(weight.astype(BF16), kv_ref[meta[n], :, 2 * width - wide :])
                total_ref[...] = total
                acc_ref[...] = acc

            seen = causal_mask(heads, size, meta[count + 2])
            if rows < size:
                seen = jnp.concatenate(
                    [seen[h * size + tile * rows :][:rows] for h in range(heads)], axis=0
                )
            own = jnp.where(seen, score(block), MASKED)
            score_ref[block] = own
            top_ref[...] = lanes(jnp.maximum, own)
            in_pairs(0, block, scores)
            top_ref[...] = jnp.broadcast_to(
                jnp.max(top_ref[...], axis=1, keepdims=True), top_ref.shape
            )
            total_ref[...] = jnp.zeros_like(total_ref)
            acc_ref[...] = jnp.zeros_like(acc_ref)
            in_pairs(0, block + 1, weights)
            total = jnp.sum(total_ref[...], axis=1, keepdims=True)
            lse = jnp.broadcast_to(top_ref[:, :1] + jnp.log(total), top_ref.shape)
            result = acc_ref[...] / total
            mine = lax.broadcasted_iota(jnp.int32, (rows, wide), 1) - (wide - width)
            whole = sum(
                jnp.where(
                    (mine >= h * HEAD_DIM) & (mine < (h + 1) * HEAD_DIM),
                    result[h * rows : (h + 1) * rows],
                    0.0,
                )
                for h in range(heads)
            )
            sum_ref[j, spot] = whole
            whole = whole[:, wide - width :].astype(BF16)
            for h in range(heads):
                lse_ref[j, pl.ds(h * size + tile * rows, rows)] = lse[h * rows : (h + 1) * rows]
            for i in range(rows // slot):
                outs[tile * rows // slot + i][j] = whole[i * slot : (i + 1) * slot]


def attend_back_kernel(meta, *refs, heads, pieces, groups):
    q_ref = refs[0]
    piece_refs = refs[1 : 1 + pieces]
    grad_refs = refs[1 + pieces : 1 + pieces + groups]
    sum_ref, lse_ref, dq_ref, keep_ref, send_ref, kv_ref, sems, acc_ref, dq_acc = refs[
        1 + pieces + groups :
    ]
    size, wide = q_ref.shape[1:]
    count = 2 * pieces
    width = heads * HEAD_DIM
    pad = wide - width
    scale = HEAD_DIM ** (-0.5)
    copies = load_pieces(piece_refs, kv_ref, sems)
    acc_ref[...] = jnp.zeros_like(acc_ref)
    for copy in copies:
        copy.wait()
    for j in range(2):
        block = meta[count + j]
        query = q_ref[j].astype(F32) * scale
        query_turned = jnp.transpose(query).astype(BF16)
        queries = jnp.concatenate(head_cols(query, 0, heads), axis=0)
        grad = jnp.concatenate([grad_refs[r][j] for r in range(groups)], axis=0)
        grad_turned = jnp.transpose(grad.astype(F32))
        if pad:
            grad_turned = jnp.concatenate([jnp.zeros((pad, size), F32), grad_turned], axis=0)
        grad = jnp.transpose(grad_turned)
        grad_turned = grad_turned.astype(BF16)
        cols = head_cols(grad, pad, heads)
        grads = jnp.concatenate(cols, axis=0)
        dots = jnp.concatenate(
            [jnp.sum(col.astype(F32) * sum_ref[j], axis=1, keepdims=True) for col in cols], axis=0
        )
        dots = jnp.broadcast_to(dots, (heads * size, 128))
        dq_acc[...] = jnp.zeros_like(dq_acc)

        def visit(ns, diagonal=False):
            dq = dq_acc[...]
            for n in ns:
                place = meta[n]
                keys = kv_ref[place, :, :wide]
                values = kv_ref[place, :, 2 * width - wide :]
                score = contract_cols(queries, keys)
                if diagonal:
                    score = jnp.where(causal_mask(heads, size, meta[count + 2]), score, MASKED)
                prob = jnp.exp(score - widen(lse_ref[j], size))
                prob_grad = contract_cols(grads, values)
                score_grad = (prob * (prob_grad - widen(dots, size))).astype(BF16)
                prob = prob.astype(BF16)
                dq += mm(score_grad, keys)
                for h in range(heads):
                    mine = slice(h * size, (h + 1) * size)
                    at = h * HEAD_DIM
                    acc_ref[place, at : at + HEAD_DIM] += mm(
                        query_turned[at : at + HEAD_DIM], score_grad[mine]
                    )
                    acc_ref[place, width + at : width + at + HEAD_DIM] += mm(
                        grad_turned[pad + at : pad + at + HEAD_DIM], prob[mine]
                    )
            dq_acc[...] = dq

        visit((block,), True)
        in_pairs(0, block, visit)
        mine = lax.broadcasted_iota(jnp.int32, (size, wide), 1)
        whole = sum(
            jnp.where(
                (mine >= h * HEAD_DIM) & (mine < (h + 1) * HEAD_DIM),
                dq_acc[h * size : (h + 1) * size],
                0.0,
            )
            for h in range(heads)
        )
        dq_ref[j] = (whole[:, :width] * scale).astype(BF16)
    for i in range(count):
        to_ref = keep_ref if i < pieces else send_ref
        to_ref[i % pieces // 2, i % 2] = jnp.transpose(acc_ref[i]).astype(BF16)


def forward_call(meta, query, keyvals, heads, groups):
    size, wide = query.shape[1:]
    part = heads * HEAD_DIM
    pieces = len(keyvals)
    rows = size
    while heads * rows * size * 2 * pieces > 1 << 22 and rows > size // groups:
        rows //= 2
    return in_vmem(
        functools.partial(attend_kernel, heads=heads, pieces=pieces, groups=groups, rows=rows),
        meta,
        [query] + keyvals,
        [jax.ShapeDtypeStruct((2, size // groups, part), BF16)] * groups
        + [
            jax.ShapeDtypeStruct((2, size, wide), F32),
            jax.ShapeDtypeStruct((2, heads * size, 128), F32),
        ],
        [
            pltpu.VMEM((2 * pieces, size, 2 * part), BF16),
            pltpu.SemaphoreType.DMA((pieces,)),
            pltpu.VMEM((2 * pieces, heads * rows, size), F32),
            pltpu.VMEM((heads * rows, 128), F32),
            pltpu.VMEM((heads * rows, 128), F32),
            pltpu.VMEM((heads * rows, wide), F32),
        ],
        16 * pieces * size * size * wide * heads,
        range(1, 1 + pieces),
    )


def backward_call(meta, query, keyvals, grads, sums, lse, heads, groups):
    size, wide = query.shape[1:]
    part = heads * HEAD_DIM
    pieces = len(keyvals)
    half = jax.ShapeDtypeStruct((pieces // 2, 2, size, 2 * part), BF16)
    return in_vmem(
        functools.partial(attend_back_kernel, heads=heads, pieces=pieces, groups=groups),
        meta,
        [query] + keyvals + grads + [sums, lse],
        [jax.ShapeDtypeStruct((2, size, part), BF16), half, half],
        [
            pltpu.VMEM((2 * pieces, size, 2 * part), BF16),
            pltpu.SemaphoreType.DMA((pieces,)),
            pltpu.VMEM((2 * pieces, 2 * part, size), F32),
            pltpu.VMEM((heads * size, wide), F32),
        ],
        24 * pieces * size * size * wide * heads,
        range(1, 1 + pieces),
    )


def project_kernel(meta, *refs, groups, fetch):
    tokens = refs[:groups]
    norm_ref = refs[groups]
    parts = refs[groups + 1 : groups + 1 + fetch]
    kv_ref, q_ref, normed_ref, unit_ref, proj_ref = refs[groups + 1 + fetch :]
    member, chip = meta[1], meta[2]
    depth, across = proj_ref.shape
    share = depth // groups
    for c in range(fetch):
        for z in range(groups):
            start = (member ^ z) * share + (chip ^ c) * (share // fetch)
            proj_ref[pl.ds(pl.multiple_of(start, 16), share // fetch)] = parts[c][z]
    rows = [norm_ref[member ^ z][:1].astype(F32) for z in range(groups)]
    gain = jnp.concatenate([row[:, :share] for row in rows], axis=1)
    shift = jnp.concatenate([row[:, share : 2 * share] for row in rows], axis=1)
    part2 = kv_ref.shape[2]
    wide = q_ref.shape[2]
    size = kv_ref.shape[1]
    for j in range(2):
        x = jnp.concatenate([ref[j] for ref in tokens], axis=0).astype(F32)
        unit, _ = norm_parts(x)
        normed = (unit * gain + shift).astype(BF16)
        unit_ref[j] = unit
        normed_ref[j] = normed
        mixed = mm(normed, proj_ref[...]).astype(BF16)
        kv_ref[j] = mixed[:, :part2]
        q_ref[j, :, : across - part2] = mixed[:, part2:]
        if wide > across - part2:
            q_ref[j, :, across - part2 :] = jnp.zeros((size, wide - across + part2), BF16)


def second_kernel(meta, *refs, groups):
    pieces = refs[:groups]
    x_ref, proj_ref, vec_ref, resid_ref, second_ref = refs[groups:]
    member = meta[1]
    slot, part = pieces[0].shape[1:]
    total = x_ref[...].astype(F32) + vec_ref[0:1]
    for z in range(groups):
        total += mm(pieces[z][...].reshape(2 * slot, part), proj_ref[member ^ z])
    resid_ref[...] = total
    unit, _ = norm_parts(total)
    second_ref[...] = (unit * vec_ref[1:2] + vec_ref[2:3]).astype(BF16)


def branch_kernel(meta, *refs, groups, chips):
    sums = refs[:chips]
    resid_ref, grad_ref, proj_ref, vec_ref = refs[chips : chips + 4]
    outs = refs[chips + 4 : chips + 4 + groups]
    resid_grad_ref, branch_ref, totals_ref = refs[chips + 4 + groups :]
    member = meta[1]
    slot, part = outs[0].shape[1:]
    second_grad = sum(ref[...].astype(F32) for ref in sums)
    unit, rate = norm_parts(resid_ref[...])
    dout = grad_ref[...].astype(F32)
    resid_grad = dout + norm_back(unit, rate, vec_ref[1:2], second_grad)
    resid_grad_ref[...] = resid_grad
    branch = resid_grad.astype(BF16)
    branch_ref[...] = branch
    for z in range(groups):
        grads = contract_cols(branch, proj_ref[member ^ z]).astype(BF16)
        outs[z][...] = grads.reshape(2, slot, part)
    totals_ref[0:1] = jnp.sum(branch.astype(F32), axis=0, keepdims=True)
    totals_ref[1:2] = jnp.sum(second_grad * unit, axis=0, keepdims=True)
    totals_ref[2:3] = jnp.sum(second_grad, axis=0, keepdims=True)
    totals_ref[3:4] = jnp.sum(dout, axis=0, keepdims=True)
    totals_ref[4:] = jnp.zeros((4, totals_ref.shape[1]), F32)


def handed_kernel(meta, *refs, groups, chips, cut, share, with_out):
    sums = refs[:chips]
    dq_ref, normed_ref, unit_ref, proj_ref, totals_ref, up_bias_ref = refs[chips : chips + 6]
    at = chips + 6
    attended = refs[at : at + groups] if with_out else ()
    branches = refs[at + groups] if with_out else None
    at += (groups + 1) * with_out
    half = groups // 2
    outs = refs[at : at + half]
    far_ref, keep_ref, send_ref, grad_ref, term_ref, out_term_ref, vec_ref = refs[at + half :]
    here, member = meta[0], meta[1]
    fetch = keep_ref.shape[0]
    across = keep_ref.shape[3]
    part2 = sums[0].shape[2]
    slot = outs[0].shape[1]
    size = slot * groups
    width = unit_ref.shape[2]
    gain_total = jnp.zeros((1, width), F32)
    shift_total = jnp.zeros((1, width), F32)
    for j in range(2):
        keyval = sum(ref[j].astype(F32) for ref in sums).astype(BF16)
        grad = jnp.concatenate([keyval, dq_ref[j]], axis=1)
        grad_ref[j] = grad
        normed_grad = contract_cols(grad, proj_ref[...])
        gain_total += jnp.sum(normed_grad * unit_ref[j], axis=0, keepdims=True)
        shift_total += jnp.sum(normed_grad, axis=0, keepdims=True)
        for z in range(groups):
            piece = normed_grad[z * slot : (z + 1) * slot].astype(BF16)
            if z < half:
                outs[z][j] = piece
            else:
                far_ref[z - half, j] = piece
    term_ref[...] = contract_rows(
        normed_ref[...].reshape(2 * size, width), grad_ref[...].reshape(2 * size, across)
    )
    if with_out:
        out_term_ref[...] = sum(
            contract_rows(piece[...].reshape(2 * slot, share), branches[z])
            for z, piece in enumerate(attended)
        )
    hidden = up_bias_ref.shape[1]
    vec_ref[...] = jnp.zeros_like(vec_ref)
    for z in range(groups):
        cols = slice(z * share, (z + 1) * share)
        vec_ref[z, 0:1, :share] = gain_total[:, cols]
        vec_ref[z, 0:1, share : 2 * share] = shift_total[:, cols]
        vec_ref[z, 1:2, :share] = totals_ref[0:1, cols]
        vec_ref[z, 1:2, share : 2 * share] = totals_ref[1:2, cols]
        vec_ref[z, 2:3, :share] = totals_ref[2:3, cols]
        vec_ref[z, 2:3, share : 2 * share] = totals_ref[3:4, cols]
        done = 0
        while done < hidden:
            size_now = min(across, hidden - done)
            row = 3 + done // across
            vec_ref[z, row : row + 1, :size_now] = up_bias_ref[z : z + 1, done : done + size_now]
            done += size_now
    for core, to_ref in enumerate((keep_ref, send_ref)):
        for r in range(fetch):
            mine = ((here ^ (2 * r + core)) & (2 * fetch - 1)) * cut
            for z in range(groups):
                owner = member ^ z
                start = pl.multiple_of(owner * share + mine, 8)
                rows = term_ref[pl.ds(start, cut)]
                to_ref[r, z] = jnp.concatenate([rows, vec_ref[owner]], axis=0).astype(BF16)
            if with_out:
                rows = out_term_ref[pl.ds(pl.multiple_of(mine, 8), cut)]
                rest = jnp.concatenate(
                    [rows[8 * i : 8 * i + 8, across:] for i in range(cut // 8)], axis=1
                )
                to_ref[r, groups] = jnp.concatenate([rows[:, :across], rest], axis=0).astype(BF16)


def rows_kernel(meta, *refs, groups, cut, part, width, with_out):
    pieces = refs[:groups]
    block_ref, small_ref, turned = refs[-3:]
    member = meta[1]
    across = 3 * part
    total = jnp.zeros(small_ref.shape, F32)
    for z in range(groups):
        value = pieces[z][...].astype(F32)
        total += value[cut:]
        turned[member ^ z] = value[:cut]
    small_ref[...] = total
    held = [turned[z] for z in range(groups)]
    for k, home in enumerate((width, 2 * width, 0)):
        whole = jnp.concatenate([h[:, k * part : (k + 1) * part] for h in held], axis=1)
        block_ref[:, home : home + width] = whole[:, :width].astype(BF16)
    if with_out:
        block = refs[groups][...].astype(F32)
        rest = jnp.concatenate(
            [
                block[cut : cut + 8, i * (width - across) : (i + 1) * (width - across)]
                for i in range(cut // 8)
            ],
            axis=0,
        )
        block = jnp.concatenate([block[:cut], rest], axis=1)
        block_ref[:, 3 * width :] = block.astype(BF16)


def home_kernel(meta, *refs, cut, fetch, with_out):
    pieces = refs[: 2 * fetch]
    outs = refs[2 * fetch :]
    here = meta[0]
    for i, piece in enumerate(pieces):
        r = 2 * (i % fetch) + i // fetch
        start = pl.multiple_of(((here ^ r) & (2 * fetch - 1)) * cut, 8)
        block = piece[...].astype(F32)
        at = 0
        for out in outs:
            out[pl.ds(start, cut)] = block[:, at : at + out.shape[1]]
            at += out.shape[1]


def tokens_kernel(meta, grad_ref, x_ref, gain_ref, resid_grad_ref, out_ref):
    rows, width = x_ref.shape
    grad = grad_ref[...].astype(F32).reshape(rows, width)
    unit, rate = norm_parts(x_ref[...].astype(F32))
    out_ref[...] = resid_grad_ref[...] + norm_back(unit, rate, gain_ref[...], grad)


def in_vmem(kernel, meta, arrays, outs, scratch=(), flops=0, there=()):
    vmem = pl.BlockSpec(memory_space=pltpu.VMEM)
    anywhere = pl.BlockSpec(memory_space=pl.ANY)
    return pl.pallas_call(
        kernel,
        grid_spec=pltpu.PrefetchScalarGridSpec(
            num_scalar_prefetch=1,
            grid=(),
            in_specs=[anywhere if i in there else vmem for i in range(len(arrays))],
            out_specs=[vmem] * len(outs),
            scratch_shapes=list(scratch),
        ),
        out_shape=outs,
        compiler_params=pltpu.CompilerParams(vmem_limit_bytes=VMEM_LIMIT),
        cost_estimate=pl.CostEstimate(flops=flops, bytes_accessed=1 << 20, transcendentals=0),
    )(meta, *arrays)


def norm_parts(values):
    center = values - jnp.mean(values, axis=-1, keepdims=True)
    rate = lax.rsqrt(jnp.mean(center * center, axis=-1, keepdims=True) + EPS)
    return center * rate, rate


def norm_back(unit, rate, gain, grad):
    e = gain * grad
    return rate * (
        e
        - jnp.mean(e, axis=-1, keepdims=True)
        - unit * jnp.mean(e * unit, axis=-1, keepdims=True)
    )


def after(x, *others):
    return lax.optimization_barrier((x,) + others)[0]


def per_device(
    tokens,
    block_owner,
    first_gain,
    first_shift,
    mixer_in,
    mixer_out,
    mixer_bias,
    second_gain,
    second_shift,
    up_weight,
    up_bias,
    down_weight,
    down_bias,
    out_grad,
):
    groups = lax.axis_size("fsdp")
    member = lax.axis_index("fsdp")
    n_ctx = lax.axis_size("ctx")
    here = lax.axis_index("ctx")
    slot, width = tokens.shape[2:]
    block_len = slot * groups
    local_rows = 2 * slot
    count_rows = 2 * block_len
    blocks = 2 * n_ctx
    share = width // groups
    hidden = up_weight.shape[0]
    hidden_cut = hidden // n_ctx
    heads = -(-HEADS // groups)
    part = heads * HEAD_DIM
    wide = -(-part // 128) * 128
    chips = n_ctx // 2
    fetch = max(f for f in (1, 2, 4, 8, 16) if f <= chips and share % (16 * f) == 0)
    fold = max(f for f in (1, 2, 4, 8, 16) if f <= chips and share % (16 * f) == 0)
    chip = (here // 2) % fetch
    cut = share // (2 * fold)
    spread_c = jnp.arange(n_ctx, dtype=jnp.int32)

    own = tokens.reshape(2, slot, width)
    rows16 = tokens.reshape(local_rows, width)
    grad16 = out_grad.reshape(local_rows, width)
    index = jnp.stack([here, member, chip]).astype(jnp.int32)

    in_cut = lax.dynamic_slice_in_dim(mixer_in, chip * (share // fetch), share // fetch, 0)
    in_cut = in_cut.reshape(-1, 3, width)
    in_cut = jnp.pad(in_cut, ((0, 0), (0, 0), (0, groups * part - width)))
    in_cut = in_cut.reshape(-1, 3, groups, part)
    in_cut = jnp.stack([in_cut[:, 1], in_cut[:, 2], in_cut[:, 0]], axis=2)
    in_cut = in_cut.transpose(1, 0, 2, 3).reshape(groups, share // fetch, 3 * part)
    norm_row = jnp.pad(jnp.concatenate([first_gain, first_shift]), (0, 3 * part - 2 * share))
    norm_rows = jnp.broadcast_to(norm_row, (groups, 16, 3 * part))
    in_cut = jnp.concatenate([in_cut, norm_rows], axis=1)
    in_pieces = z_exchange([pick(in_cut, member ^ r) for r in range(groups)])
    in_pieces = jnp.stack(in_pieces)
    group_tokens = z_gather(after(own, in_pieces))
    norm_part = in_pieces[:, share // fetch :]
    in_parts = chip_spread(in_pieces[:, : share // fetch], fetch)
    group_tokens = after(tuple(group_tokens), *in_parts)
    gain_one = jnp.concatenate(
        [pick(norm_part[:, 0, :share], member ^ r)[None] for r in range(groups)]
    ).reshape(1, width).astype(F32)

    pieces = jax.ShapeDtypeStruct((2, block_len, width), BF16)
    keyval, query, normed16, unit_one, proj_in = in_vmem(
        functools.partial(project_kernel, groups=groups, fetch=fetch),
        index,
        list(group_tokens) + [norm_part] + in_parts,
        [
            jax.ShapeDtypeStruct((2, block_len, 2 * part), BF16),
            jax.ShapeDtypeStruct((2, block_len, wide), BF16),
            pieces,
            jax.ShapeDtypeStruct((2, block_len, width), F32),
            jax.ShapeDtypeStruct((width, 3 * part), BF16),
        ],
    )
    keyvals = chip_spread(keyval, chips)

    owners = block_owner.reshape(-1)
    numbers = jnp.arange(blocks, dtype=jnp.int32)
    places = jnp.sum(jnp.where(owners[None, :] == numbers[:, None], numbers[None, :], 0), axis=1)
    offset = (places // 2) ^ here
    places = (offset % 2) * n_ctx + (offset // 2) * 2 + places % 2
    meta = jnp.concatenate(
        [
            places,
            lax.dynamic_index_in_dim(block_owner, here, 0, keepdims=False),
            (member * slot)[None],
        ]
    ).astype(jnp.int32)

    grads_all = lax.all_gather(grad16, "ctx", axis=0, tiled=True)
    order = jnp.concatenate([spread_c[0::2], spread_c[1::2]]) ^ here
    grads_all = shuffle(grads_all.reshape(n_ctx, local_rows, width), order, BF16)
    grads_all = grads_all.reshape(n_ctx * local_rows, width)
    extra = jnp.concatenate([mixer_bias, second_gain, second_shift, down_bias]).reshape(1, 4 * share)
    extra = jnp.concatenate([extra, jnp.pad(up_bias, (0, 4 * share - hidden))[None]])
    extra = jnp.pad(extra, ((0, 14), (0, width - 4 * share)))
    out_pack = after(jnp.concatenate([mixer_out, extra]), *group_tokens)
    out_pack = lax.all_gather(out_pack, "fsdp", axis=0, tiled=True)
    out_pack = out_pack.reshape(groups, share + 16, width)
    proj_out = out_pack[:, :share].reshape(width, width)
    proj_out = jnp.pad(proj_out, ((0, groups * part - width), (0, 0)))
    proj_out = proj_out.reshape(groups, part, width)
    vectors = jnp.concatenate(
        [out_pack[:, share, i * share : (i + 1) * share].reshape(1, width) for i in range(4)]
        + [jnp.zeros((4, width), BF16)]
    ).astype(F32)
    up_bias_part = lax.dynamic_slice_in_dim(
        out_pack[:, share + 1], here * hidden_cut, hidden_cut, 1
    ).reshape(groups * hidden_cut)
    *keyvals, grads_all = lax.optimization_barrier((*keyvals, grads_all))
    keyvals = keyvals + [swap(piece, "ctx", 1) for piece in keyvals]
    ffn_cut = jnp.concatenate(
        [
            lax.dynamic_slice_in_dim(up_weight, here * hidden_cut, hidden_cut, 0),
            lax.dynamic_slice_in_dim(down_weight, here * hidden_cut, hidden_cut, 0),
        ]
    )
    ffn_parts = lax.all_gather(after(ffn_cut, *group_tokens), "fsdp", axis=0, tiled=True)
    ffn_parts = ffn_parts.reshape(groups, 2, hidden_cut, width)
    up_part = ffn_parts[:, 0].reshape(groups * hidden_cut, width)
    down_part = ffn_parts[:, 1].reshape(groups * hidden_cut, width)

    pair = jax.ShapeDtypeStruct((2, slot, part), BF16)
    results = forward_call(meta, query, keyvals, heads, groups)
    own_attended = results[:groups]
    sums, lse = results[groups:]
    attended = z_exchange(results[:groups])
    proj_out, vectors, *attended = lax.optimization_barrier((proj_out, vectors, *attended))
    resid, second16 = in_vmem(
        functools.partial(second_kernel, groups=groups),
        index,
        attended + [rows16, proj_out, vectors],
        [
            jax.ShapeDtypeStruct((local_rows, width), F32),
            jax.ShapeDtypeStruct((local_rows, width), BF16),
        ],
    )

    second_held = chip_spread(second16, chips)
    up_part, down_part, *second_held = lax.optimization_barrier((up_part, down_part, *second_held))
    second_all = jnp.concatenate(second_held + [swap(s, "ctx", 1) for s in second_held])
    pre = contract_cols(second_all, up_part) + up_bias_part.astype(F32)
    act, gate_pull = jax.vjp(functools.partial(jax.nn.gelu, approximate=True), pre)
    act16 = act.astype(BF16)
    pre_grad = gate_pull(contract_cols(grads_all, down_part))[0].astype(BF16)
    second_part = mm(pre_grad, up_part).astype(BF16).reshape(2, chips, local_rows, width)
    up_term = contract_rows(pre_grad, second_all).astype(BF16)
    down_term = contract_rows(act16, grads_all).astype(BF16)
    feed_part = mm(act16, down_part).astype(BF16)
    second_sums = ctx_collect(second_part[0], second_part[1])
    back_order = spread_c ^ here
    back_order = (back_order % 2) * chips + back_order // 2
    feed = shuffle(feed_part.reshape(n_ctx, local_rows, width), back_order, BF16)
    feed = feed.reshape(n_ctx * local_rows, width)
    ffn_terms = jnp.concatenate(
        [
            up_term.reshape(groups, hidden_cut, width),
            down_term.reshape(groups, hidden_cut, width),
        ],
        axis=1,
    ).reshape(groups * 2 * hidden_cut, width)
    feed, ffn_terms, *second_sums = lax.optimization_barrier((feed, ffn_terms, *second_sums))
    feed = lax.psum_scatter(feed, "ctx", scatter_dimension=0, tiled=True)
    results = in_vmem(
        functools.partial(branch_kernel, groups=groups, chips=chips),
        index,
        second_sums + [resid, grad16, proj_out, vectors],
        [pair] * groups
        + [
            jax.ShapeDtypeStruct((local_rows, width), F32),
            jax.ShapeDtypeStruct((local_rows, width), BF16),
            jax.ShapeDtypeStruct((8, width), F32),
        ],
    )
    resid_grad, branch_grad16, totals = results[groups:]
    attend_grads = z_exchange(results[:groups])
    branches = branch_grad16[None]
    branches = jnp.concatenate([branches, swap(branches, "fsdp", 1)])
    branches, *attend_grads = lax.optimization_barrier((branches, *attend_grads))
    mask = 2
    while mask < groups:
        branches = jnp.concatenate([branches, swap(branches, "fsdp", mask)])
        mask *= 2

    query_grad, keyval_keep, keyval_send = backward_call(
        meta, query, keyvals, attend_grads, sums, lse, heads, groups
    )
    keyval_sums = ctx_collect(keyval_keep, after(keyval_send, branches))
    feed, *keyval_sums = lax.optimization_barrier((feed, *keyval_sums))

    ffn_terms = after(ffn_terms, branches, query_grad)
    ffn_term = lax.psum_scatter(ffn_terms, "fsdp", scatter_dimension=0, tiled=True)

    with_out = part == share and (cut // 8) * (width - 3 * part) == 3 * part
    up_bias_terms = jnp.sum(pre_grad.astype(F32), axis=0).reshape(groups, hidden_cut)
    up_bias_terms = lax.dynamic_update_slice(
        jnp.zeros((groups, hidden), F32), up_bias_terms, (0, here * hidden_cut)
    )
    half = jax.ShapeDtypeStruct((fold, groups + with_out, cut + 8, 3 * part), BF16)
    results = in_vmem(
        functools.partial(
            handed_kernel, groups=groups, chips=chips, cut=cut, share=share, with_out=with_out
        ),
        index,
        keyval_sums
        + [query_grad, normed16, unit_one, proj_in, totals, up_bias_terms]
        + (list(own_attended) + [branches] if with_out else []),
        [jax.ShapeDtypeStruct((2, slot, width), BF16)] * (groups // 2)
        + [jax.ShapeDtypeStruct((groups // 2, 2, slot, width), BF16), half, half],
        [
            pltpu.VMEM((2, block_len, 3 * part), BF16),
            pltpu.VMEM((width, 3 * part), F32),
            pltpu.VMEM((share, width), F32),
            pltpu.VMEM((groups, 8, 3 * part), F32),
        ],
    )
    *normed_pieces, normed_far, in_keep, in_send = results
    in_sums = ctx_collect(in_keep, in_send)
    ffn_grads = lax.all_gather(after(ffn_term, in_sums[0]), "ctx", axis=0, tiled=True)
    mask = groups // 2
    came = swap(normed_far, "fsdp", mask)
    came, *in_sums = lax.optimization_barrier((came, *in_sums))
    normed_pieces = [add16(piece, came[i]) for i, piece in enumerate(normed_pieces)]
    while mask > 1:
        mask //= 2
        came = swap(jnp.stack(normed_pieces[mask:]), "fsdp", mask)
        normed_pieces = [add16(piece, came[i]) for i, piece in enumerate(normed_pieces[:mask])]
    normed_grad = normed_pieces[0]
    in_term = sum(piece.astype(F32) for piece in in_sums).astype(BF16)
    mask = 2 * fold
    while mask < n_ctx:
        in_term = add16(in_term, swap(in_term, "ctx", mask))
        mask *= 2
    handed = z_exchange([in_term[r] for r in range(groups)])
    across = (3 + with_out) * width
    in_block, small = in_vmem(
        functools.partial(
            rows_kernel, groups=groups, cut=cut, part=part, width=width, with_out=with_out
        ),
        index,
        handed + ([in_term[groups]] if with_out else []),
        [
            jax.ShapeDtypeStruct((cut, across), BF16),
            jax.ShapeDtypeStruct((8, 3 * part), F32),
        ],
        [pltpu.VMEM((groups, cut, 3 * part), F32)],
    )
    in_held = chip_spread(in_block, fold)
    tokens_grad = in_vmem(
        tokens_kernel,
        index,
        [normed_grad, rows16, gain_one, resid_grad],
        [jax.ShapeDtypeStruct((local_rows, width), F32)],
    )[0]
    block_out = (resid + feed.astype(F32) + vectors[3:4]).astype(BF16)

    ffn_grads = ffn_grads.reshape(n_ctx, 2, hidden_cut, width).astype(F32)
    up_grad = ffn_grads[:, 0].reshape(hidden, width)
    down_grad = ffn_grads[:, 1].reshape(hidden, width)
    up_grad, down_grad, *in_held = lax.optimization_barrier((up_grad, down_grad, *in_held))
    in_held = in_held + [swap(piece, "ctx", 1) for piece in in_held]
    tokens_grad, *in_held = lax.optimization_barrier((tokens_grad, *in_held))
    homes = in_vmem(
        functools.partial(home_kernel, cut=cut, fetch=fold, with_out=with_out),
        index,
        in_held,
        [
            jax.ShapeDtypeStruct((share, wide_out), F32)
            for wide_out in ((3 * width, width) if with_out else (3 * width,))
        ],
    )
    mixer_in_grad, mixer_out_grad = homes[0], homes[-1]

    if not with_out:
        whole = jnp.stack(attended).reshape(groups, local_rows, part)
        whole = jnp.concatenate([pick(whole, member ^ i) for i in range(groups)], axis=1)
        out_term = contract_rows(whole[:, :width], branch_grad16).astype(BF16)
        out_term = lax.psum_scatter(out_term, "fsdp", scatter_dimension=0, tiled=True)
        mixer_out_grad = lax.psum(out_term, "ctx").astype(F32)

    bias_rows = -(-hidden // (3 * part))
    up_bias_grad = small[3 : 3 + bias_rows].reshape(-1)[:hidden]
    return (
        block_out.reshape(1, 2, slot, width),
        tokens_grad.reshape(1, 2, slot, width),
        small[0, :share],
        small[0, share : 2 * share],
        mixer_in_grad,
        mixer_out_grad,
        small[1, :share],
        small[1, share : 2 * share],
        small[2, :share],
        up_grad,
        up_bias_grad,
        down_grad,
        small[2, share : 2 * share],
    )


def solution(mesh):
    in_specs = (
        P("ctx", None, "fsdp", None),
        P(),
        P("fsdp"),
        P("fsdp"),
        P("fsdp", None),
        P("fsdp", None),
        P("fsdp"),
        P("fsdp"),
        P("fsdp"),
        P("fsdp", None),
        P("fsdp"),
        P("fsdp", None),
        P("fsdp"),
        P("ctx", None, "fsdp", None),
    )
    out_specs = (
        P("ctx", None, "fsdp", None),
        P("ctx", None, "fsdp", None),
        P("fsdp"),
        P("fsdp"),
        P("fsdp", None),
        P("fsdp", None),
        P("fsdp"),
        P("fsdp"),
        P("fsdp"),
        P("fsdp", None),
        P("fsdp"),
        P("fsdp", None),
        P("fsdp"),
    )
    return jax.shard_map(
        per_device, mesh=mesh, in_specs=in_specs, out_specs=out_specs, check_vma=False
    )
```

```python
import functools

import jax
import jax.numpy as jnp
from jax import lax
from jax.experimental import pallas as pl
from jax.experimental.pallas import tpu as pltpu
from jax.sharding import PartitionSpec as P

HEADS = 12
HEAD_DIM = 64

EPS = 1e-05
MASKED = -1e30
F32 = jnp.float32
BF16 = jnp.bfloat16
VMEM_LIMIT = 56 * 1024 * 1024


def swap(x, axis, mask):
    return lax.ppermute(x, axis, [(i, i ^ mask) for i in range(lax.axis_size(axis))])


def add16(left, right):
    return (left.astype(F32) + right.astype(F32)).astype(BF16)


def z_gather(x):
    return [x] + [swap(x, "fsdp", r) for r in range(1, lax.axis_size("fsdp"))]


def z_exchange(pieces):
    return [pieces[0]] + [swap(pieces[r], "fsdp", r) for r in range(1, len(pieces))]


def z_sum(pieces):
    return sum(piece.astype(F32) for piece in z_exchange(pieces))


def chip_spread(x, chips):
    return [x] + [swap(x, "ctx", 2 * r) for r in range(1, chips)]


def ctx_spread(x):
    held = chip_spread(x, lax.axis_size("ctx") // 2)
    return held + [swap(piece, "ctx", 1) for piece in held]


def ctx_collect(keep, send):
    came = swap(send, "ctx", 1)
    pieces = [add16(keep[r], came[r]) for r in range(keep.shape[0])]
    return [pieces[0]] + [swap(pieces[r], "ctx", 2 * r) for r in range(1, len(pieces))]


def pick(stacked, index):
    return lax.dynamic_index_in_dim(stacked, index, 0, keepdims=False)


def shuffle_kernel(table, x_ref, out_ref):
    width = x_ref.shape[2]
    extra = out_ref.shape[2] - width
    for i in range(out_ref.shape[0]):
        out_ref[i, :, :width] = x_ref[table[i]].astype(out_ref.dtype)
        if extra:
            out_ref[i, :, width:] = jnp.zeros((x_ref.shape[1], extra), out_ref.dtype)


def shuffle(x, table, kind, width=None):
    shape = (table.shape[0], x.shape[1], width or x.shape[2])
    return pl.pallas_call(
        shuffle_kernel,
        grid_spec=pltpu.PrefetchScalarGridSpec(
            num_scalar_prefetch=1,
            grid=(),
            in_specs=[pl.BlockSpec(memory_space=pltpu.VMEM)],
            out_specs=pl.BlockSpec(memory_space=pltpu.VMEM),
        ),
        out_shape=jax.ShapeDtypeStruct(shape, kind),
        compiler_params=pltpu.CompilerParams(vmem_limit_bytes=VMEM_LIMIT),
    )(table, x)


def mm(left, right):
    return jnp.dot(left, right, preferred_element_type=F32)


def contract_rows(left, right):
    return lax.dot_general(left, right, (((0,), (0,)), ((), ())), preferred_element_type=F32)


def contract_cols(left, right):
    return lax.dot_general(left, right, (((1,), (1,)), ((), ())), preferred_element_type=F32)


def head_cols(values, at, heads):
    cols = lax.broadcasted_iota(jnp.int32, values.shape, 1) - at
    return [
        jnp.where((cols >= h * HEAD_DIM) & (cols < (h + 1) * HEAD_DIM), values, 0.0).astype(BF16)
        for h in range(heads)
    ]


def causal_mask(heads, size, flip):
    queries = lax.broadcasted_iota(jnp.int32, (heads * size, size), 0) % size ^ flip
    keys = lax.broadcasted_iota(jnp.int32, (heads * size, size), 1) ^ flip
    return keys <= queries


def lanes(combine, values):
    return functools.reduce(
        combine, [values[:, i : i + 128] for i in range(0, values.shape[1], 128)]
    )


def widen(values, width):
    return jnp.concatenate([values] * (width // 128), axis=1)


def load_pieces(pieces, kv_ref, sems):
    copies = [
        pltpu.make_async_copy(piece, kv_ref.at[pl.ds(2 * i, 2)], sems.at[i])
        for i, piece in enumerate(pieces)
    ]
    for copy in copies:
        copy.start()
    return copies


def in_pairs(start, stop, step):
    def both(i, carry):
        step((start + 2 * i, start + 2 * i + 1))
        return carry

    def one(n, carry):
        step((n,))
        return carry

    half = (stop - start) // 2
    lax.fori_loop(0, half, both, 0)
    lax.fori_loop(start + 2 * half, stop, one, 0)


def attend_kernel(meta, *refs, heads, pieces, groups, rows):
    q_ref = refs[0]
    piece_refs = refs[1 : 1 + pieces]
    outs = refs[1 + pieces : 1 + pieces + groups]
    sum_ref, lse_ref, kv_ref, sems, score_ref, top_ref, total_ref, acc_ref = refs[
        1 + pieces + groups :
    ]
    size, wide = q_ref.shape[1:]
    slot = size // groups
    count = 2 * pieces
    width = heads * HEAD_DIM
    scale = HEAD_DIM ** (-0.5)
    copies = load_pieces(piece_refs, kv_ref, sems)
    copies[0].wait()
    for j in range(2):
        block = meta[count + j]
        for tile in range(size // rows):
            spot = pl.ds(tile * rows, rows)
            query = jnp.concatenate(head_cols(q_ref[j, spot].astype(F32) * scale, 0, heads), axis=0)

            def score(n):
                return contract_cols(query, kv_ref[meta[n], :, :wide])

            def scores(ns):
                found = [score(n) for n in ns]
                top = top_ref[...]
                for n, value in zip(ns, found, strict=True):
                    score_ref[n] = value
                    top = jnp.maximum(top, lanes(jnp.maximum, value))
                top_ref[...] = top

            def weights(ns):
                total = total_ref[...]
                acc = acc_ref[...]
                top = widen(top_ref[...], size)
                for n in ns:
                    weight = jnp.exp(score_ref[n] - top)
                    total += lanes(jnp.add, weight)
                    acc += mm(weight.astype(BF16), kv_ref[meta[n], :, 2 * width - wide :])
                total_ref[...] = total
                acc_ref[...] = acc

            seen = causal_mask(heads, size, meta[count + 2])
            if rows < size:
                seen = jnp.concatenate(
                    [seen[h * size + tile * rows :][:rows] for h in range(heads)], axis=0
                )
            own = jnp.where(seen, score(block), MASKED)
            score_ref[block] = own
            top_ref[...] = lanes(jnp.maximum, own)
            if j == 0 and tile == 0:
                for copy in copies[1:]:
                    copy.wait()
            in_pairs(0, block, scores)
            top_ref[...] = jnp.broadcast_to(
                jnp.max(top_ref[...], axis=1, keepdims=True), top_ref.shape
            )
            total_ref[...] = jnp.zeros_like(total_ref)
            acc_ref[...] = jnp.zeros_like(acc_ref)
            in_pairs(0, block + 1, weights)
            total = jnp.sum(total_ref[...], axis=1, keepdims=True)
            lse = jnp.broadcast_to(top_ref[:, :1] + jnp.log(total), top_ref.shape)
            result = acc_ref[...] / total
            mine = lax.broadcasted_iota(jnp.int32, (rows, wide), 1) - (wide - width)
            whole = sum(
                jnp.where(
                    (mine >= h * HEAD_DIM) & (mine < (h + 1) * HEAD_DIM),
                    result[h * rows : (h + 1) * rows],
                    0.0,
                )
                for h in range(heads)
            )
            sum_ref[j, spot] = whole
            whole = whole[:, wide - width :].astype(BF16)
            for h in range(heads):
                lse_ref[j, pl.ds(h * size + tile * rows, rows)] = lse[h * rows : (h + 1) * rows]
            for i in range(rows // slot):
                outs[tile * rows // slot + i][j] = whole[i * slot : (i + 1) * slot]


def attend_back_kernel(meta, *refs, heads, pieces, groups):
    q_ref = refs[0]
    piece_refs = refs[1 : 1 + pieces]
    grad_refs = refs[1 + pieces : 1 + pieces + groups]
    sum_ref, lse_ref, dq_ref, keep_ref, send_ref, kv_ref, sems, acc_ref, dq_acc = refs[
        1 + pieces + groups :
    ]
    size, wide = q_ref.shape[1:]
    count = 2 * pieces
    width = heads * HEAD_DIM
    pad = wide - width
    scale = HEAD_DIM ** (-0.5)
    copies = load_pieces(piece_refs, kv_ref, sems)
    acc_ref[...] = jnp.zeros_like(acc_ref)
    for copy in copies:
        copy.wait()
    for j in range(2):
        block = meta[count + j]
        query = q_ref[j].astype(F32) * scale
        query_turned = jnp.transpose(query).astype(BF16)
        queries = jnp.concatenate(head_cols(query, 0, heads), axis=0)
        grad = jnp.concatenate([grad_refs[r][j] for r in range(groups)], axis=0)
        grad_turned = jnp.transpose(grad.astype(F32))
        if pad:
            grad_turned = jnp.concatenate([jnp.zeros((pad, size), F32), grad_turned], axis=0)
        grad = jnp.transpose(grad_turned)
        grad_turned = grad_turned.astype(BF16)
        cols = head_cols(grad, pad, heads)
        grads = jnp.concatenate(cols, axis=0)
        dots = jnp.concatenate(
            [jnp.sum(col.astype(F32) * sum_ref[j], axis=1, keepdims=True) for col in cols], axis=0
        )
        dots = jnp.broadcast_to(dots, (heads * size, 128))
        dq_acc[...] = jnp.zeros_like(dq_acc)

        def visit(ns, diagonal=False):
            dq = dq_acc[...]
            for n in ns:
                place = meta[n]
                keys = kv_ref[place, :, :wide]
                values = kv_ref[place, :, 2 * width - wide :]
                score = contract_cols(queries, keys)
                if diagonal:
                    score = jnp.where(causal_mask(heads, size, meta[count + 2]), score, MASKED)
                prob = jnp.exp(score - widen(lse_ref[j], size))
                prob_grad = contract_cols(grads, values)
                score_grad = (prob * (prob_grad - widen(dots, size))).astype(BF16)
                prob = prob.astype(BF16)
                dq += mm(score_grad, keys)
                for h in range(heads):
                    mine = slice(h * size, (h + 1) * size)
                    at = h * HEAD_DIM
                    acc_ref[place, at : at + HEAD_DIM] += mm(
                        query_turned[at : at + HEAD_DIM], score_grad[mine]
                    )
                    acc_ref[place, width + at : width + at + HEAD_DIM] += mm(
                        grad_turned[pad + at : pad + at + HEAD_DIM], prob[mine]
                    )
            dq_acc[...] = dq

        visit((block,), True)
        in_pairs(0, block, visit)
        mine = lax.broadcasted_iota(jnp.int32, (size, wide), 1)
        whole = sum(
            jnp.where(
                (mine >= h * HEAD_DIM) & (mine < (h + 1) * HEAD_DIM),
                dq_acc[h * size : (h + 1) * size],
                0.0,
            )
            for h in range(heads)
        )
        dq_ref[j] = (whole[:, :width] * scale).astype(BF16)
    for i in range(count):
        to_ref = keep_ref if i < pieces else send_ref
        to_ref[i % pieces // 2, i % 2] = acc_ref[i].astype(BF16)


def forward_call(meta, query, keyvals, heads, groups):
    size, wide = query.shape[1:]
    part = heads * HEAD_DIM
    pieces = len(keyvals)
    rows = size
    while heads * rows * size * 2 * pieces > 1 << 22 and rows > size // groups:
        rows //= 2
    return in_vmem(
        functools.partial(attend_kernel, heads=heads, pieces=pieces, groups=groups, rows=rows),
        meta,
        [query] + keyvals,
        [jax.ShapeDtypeStruct((2, size // groups, part), BF16)] * groups
        + [
            jax.ShapeDtypeStruct((2, size, wide), F32),
            jax.ShapeDtypeStruct((2, heads * size, 128), F32),
        ],
        [
            pltpu.VMEM((2 * pieces, size, 2 * part), BF16),
            pltpu.SemaphoreType.DMA((pieces,)),
            pltpu.VMEM((2 * pieces, heads * rows, size), F32),
            pltpu.VMEM((heads * rows, 128), F32),
            pltpu.VMEM((heads * rows, 128), F32),
            pltpu.VMEM((heads * rows, wide), F32),
        ],
        40 * pieces * size * size * wide * heads,
        range(1, 1 + pieces),
    )


def backward_call(meta, query, keyvals, grads, sums, lse, heads, groups):
    size, wide = query.shape[1:]
    part = heads * HEAD_DIM
    pieces = len(keyvals)
    half = jax.ShapeDtypeStruct((pieces // 2, 2, 2 * part, size), BF16)
    return in_vmem(
        functools.partial(attend_back_kernel, heads=heads, pieces=pieces, groups=groups),
        meta,
        [query] + keyvals + grads + [sums, lse],
        [jax.ShapeDtypeStruct((2, size, part), BF16), half, half],
        [
            pltpu.VMEM((2 * pieces, size, 2 * part), BF16),
            pltpu.SemaphoreType.DMA((pieces,)),
            pltpu.VMEM((2 * pieces, 2 * part, size), F32),
            pltpu.VMEM((heads * size, wide), F32),
        ],
        24 * pieces * size * size * wide * heads,
        range(1, 1 + pieces),
    )


def project_kernel(meta, *refs, groups, fetch):
    tokens = refs[:groups]
    norm_ref = refs[groups]
    parts = refs[groups + 1 : groups + 1 + fetch]
    kv_ref, q_ref, normed_ref, unit_ref, proj_ref = refs[groups + 1 + fetch :]
    member, chip = meta[1], meta[2]
    depth, across = proj_ref.shape
    share = depth // groups
    for c in range(fetch):
        for z in range(groups):
            start = (member ^ z) * share + (chip ^ c) * (share // fetch)
            proj_ref[pl.ds(pl.multiple_of(start, 16), share // fetch)] = parts[c][z]
    rows = [norm_ref[member ^ z][:1].astype(F32) for z in range(groups)]
    gain = jnp.concatenate([row[:, :share] for row in rows], axis=1)
    shift = jnp.concatenate([row[:, share : 2 * share] for row in rows], axis=1)
    part2 = kv_ref.shape[2]
    wide = q_ref.shape[2]
    size = kv_ref.shape[1]
    for j in range(2):
        x = jnp.concatenate([ref[j] for ref in tokens], axis=0).astype(F32)
        unit, _ = norm_parts(x)
        normed = (unit * gain + shift).astype(BF16)
        unit_ref[j] = unit
        normed_ref[j] = normed
        mixed = mm(normed, proj_ref[...]).astype(BF16)
        kv_ref[j] = mixed[:, :part2]
        q_ref[j, :, : across - part2] = mixed[:, part2:]
        if wide > across - part2:
            q_ref[j, :, across - part2 :] = jnp.zeros((size, wide - across + part2), BF16)


def second_kernel(meta, *refs, groups):
    pieces = refs[:groups]
    x_ref, proj_ref, vec_ref, resid_ref, second_ref = refs[groups:]
    member = meta[1]
    slot, part = pieces[0].shape[1:]
    total = x_ref[...].astype(F32) + vec_ref[0:1]
    for z in range(groups):
        total += mm(pieces[z][...].reshape(2 * slot, part), proj_ref[member ^ z])
    resid_ref[...] = total
    unit, _ = norm_parts(total)
    second_ref[...] = (unit * vec_ref[1:2] + vec_ref[2:3]).astype(BF16)


def branch_kernel(meta, *refs, groups, chips):
    sums = refs[:chips]
    resid_ref, grad_ref, proj_ref, vec_ref = refs[chips : chips + 4]
    outs = refs[chips + 4 : chips + 4 + groups]
    resid_grad_ref, branch_ref, totals_ref = refs[chips + 4 + groups :]
    member = meta[1]
    slot, part = outs[0].shape[1:]
    second_grad = sum(ref[...].astype(F32) for ref in sums)
    unit, rate = norm_parts(resid_ref[...])
    dout = grad_ref[...].astype(F32)
    resid_grad = dout + norm_back(unit, rate, vec_ref[1:2], second_grad)
    resid_grad_ref[...] = resid_grad
    branch = resid_grad.astype(BF16)
    branch_ref[...] = branch
    for z in range(groups):
        grads = contract_cols(branch, proj_ref[member ^ z]).astype(BF16)
        outs[z][...] = grads.reshape(2, slot, part)
    totals_ref[0:1] = jnp.sum(branch.astype(F32), axis=0, keepdims=True)
    totals_ref[1:2] = jnp.sum(second_grad * unit, axis=0, keepdims=True)
    totals_ref[2:3] = jnp.sum(second_grad, axis=0, keepdims=True)
    totals_ref[3:4] = jnp.sum(dout, axis=0, keepdims=True)
    totals_ref[4:] = jnp.zeros((4, totals_ref.shape[1]), F32)


def handed_kernel(meta, *refs, groups, chips, cut, share, with_out):
    sums = refs[:chips]
    dq_ref, normed_ref, unit_ref, proj_ref, totals_ref, up_bias_ref = refs[chips : chips + 6]
    at = chips + 6
    attended = refs[at : at + groups] if with_out else ()
    branches = refs[at + groups] if with_out else None
    at += (groups + 1) * with_out
    half = groups // 2
    outs = refs[at : at + half]
    far_ref, keep_ref, send_ref, grad_ref, term_ref, out_term_ref, vec_ref = refs[at + half :]
    here, member = meta[0], meta[1]
    fetch = keep_ref.shape[0]
    across = keep_ref.shape[3]
    slot = outs[0].shape[1]
    size = slot * groups
    width = unit_ref.shape[2]
    gain_total = jnp.zeros((1, width), F32)
    shift_total = jnp.zeros((1, width), F32)
    for j in range(2):
        keyval = jnp.transpose(sum(ref[j].astype(F32) for ref in sums)).astype(BF16)
        grad = jnp.concatenate([keyval, dq_ref[j]], axis=1)
        grad_ref[j] = grad
        normed_grad = contract_cols(grad, proj_ref[...])
        gain_total += jnp.sum(normed_grad * unit_ref[j], axis=0, keepdims=True)
        shift_total += jnp.sum(normed_grad, axis=0, keepdims=True)
        for z in range(groups):
            piece = normed_grad[z * slot : (z + 1) * slot].astype(BF16)
            if z < half:
                outs[z][j] = piece
            else:
                far_ref[z - half, j] = piece
    term_ref[...] = contract_rows(
        normed_ref[...].reshape(2 * size, width), grad_ref[...].reshape(2 * size, across)
    )
    if with_out:
        out_term_ref[...] = sum(
            contract_rows(piece[...].reshape(2 * slot, share), branches[z])
            for z, piece in enumerate(attended)
        )
    hidden = up_bias_ref.shape[1]
    vec_ref[...] = jnp.zeros_like(vec_ref)
    for z in range(groups):
        cols = slice(z * share, (z + 1) * share)
        vec_ref[z, 0:1, :share] = gain_total[:, cols]
        vec_ref[z, 0:1, share : 2 * share] = shift_total[:, cols]
        vec_ref[z, 1:2, :share] = totals_ref[0:1, cols]
        vec_ref[z, 1:2, share : 2 * share] = totals_ref[1:2, cols]
        vec_ref[z, 2:3, :share] = totals_ref[2:3, cols]
        vec_ref[z, 2:3, share : 2 * share] = totals_ref[3:4, cols]
        done = 0
        while done < hidden:
            size_now = min(across, hidden - done)
            row = 3 + done // across
            vec_ref[z, row : row + 1, :size_now] = up_bias_ref[z : z + 1, done : done + size_now]
            done += size_now
    for core, to_ref in enumerate((keep_ref, send_ref)):
        for r in range(fetch):
            mine = ((here ^ (2 * r + core)) & (2 * fetch - 1)) * cut
            for z in range(groups):
                owner = member ^ z
                start = pl.multiple_of(owner * share + mine, 8)
                rows = term_ref[pl.ds(start, cut)]
                to_ref[r, z] = jnp.concatenate([rows, vec_ref[owner]], axis=0).astype(BF16)
            if with_out:
                rows = out_term_ref[pl.ds(pl.multiple_of(mine, 8), cut)]
                rest = jnp.concatenate(
                    [rows[8 * i : 8 * i + 8, across:] for i in range(cut // 8)], axis=1
                )
                to_ref[r, groups] = jnp.concatenate([rows[:, :across], rest], axis=0).astype(BF16)


def rows_kernel(meta, *refs, groups, cut, part, width, with_out):
    pieces = refs[:groups]
    block_ref, small_ref, turned = refs[-3:]
    member = meta[1]
    across = 3 * part
    total = jnp.zeros(small_ref.shape, F32)
    for z in range(groups):
        value = pieces[z][...].astype(F32)
        total += value[cut:]
        turned[member ^ z] = value[:cut]
    small_ref[...] = total
    held = [turned[z] for z in range(groups)]
    for k, home in enumerate((width, 2 * width, 0)):
        whole = jnp.concatenate([h[:, k * part : (k + 1) * part] for h in held], axis=1)
        block_ref[:, home : home + width] = whole[:, :width].astype(BF16)
    if with_out:
        block = refs[groups][...].astype(F32)
        rest = jnp.concatenate(
            [
                block[cut : cut + 8, i * (width - across) : (i + 1) * (width - across)]
                for i in range(cut // 8)
            ],
            axis=0,
        )
        block = jnp.concatenate([block[:cut], rest], axis=1)
        block_ref[:, 3 * width :] = block.astype(BF16)


def home_kernel(meta, *refs, cut, fetch, with_out):
    pieces = refs[: 2 * fetch]
    outs = refs[2 * fetch :]
    here = meta[0]
    for i, piece in enumerate(pieces):
        r = 2 * (i % fetch) + i // fetch
        start = pl.multiple_of(((here ^ r) & (2 * fetch - 1)) * cut, 8)
        block = piece[...].astype(F32)
        at = 0
        for out in outs:
            out[pl.ds(start, cut)] = block[:, at : at + out.shape[1]]
            at += out.shape[1]


def tokens_kernel(meta, grad_ref, x_ref, gain_ref, resid_grad_ref, out_ref):
    rows, width = x_ref.shape
    grad = grad_ref[...].astype(F32).reshape(rows, width)
    unit, rate = norm_parts(x_ref[...].astype(F32))
    out_ref[...] = resid_grad_ref[...] + norm_back(unit, rate, gain_ref[...], grad)


def in_vmem(kernel, meta, arrays, outs, scratch=(), flops=0, there=()):
    vmem = pl.BlockSpec(memory_space=pltpu.VMEM)
    anywhere = pl.BlockSpec(memory_space=pl.ANY)
    return pl.pallas_call(
        kernel,
        grid_spec=pltpu.PrefetchScalarGridSpec(
            num_scalar_prefetch=1,
            grid=(),
            in_specs=[anywhere if i in there else vmem for i in range(len(arrays))],
            out_specs=[vmem] * len(outs),
            scratch_shapes=list(scratch),
        ),
        out_shape=outs,
        compiler_params=pltpu.CompilerParams(vmem_limit_bytes=VMEM_LIMIT),
        cost_estimate=pl.CostEstimate(flops=flops, bytes_accessed=1 << 20, transcendentals=0),
    )(meta, *arrays)


def norm_parts(values):
    center = values - jnp.mean(values, axis=-1, keepdims=True)
    rate = lax.rsqrt(jnp.mean(center * center, axis=-1, keepdims=True) + EPS)
    return center * rate, rate


def norm_back(unit, rate, gain, grad):
    e = gain * grad
    return rate * (
        e
        - jnp.mean(e, axis=-1, keepdims=True)
        - unit * jnp.mean(e * unit, axis=-1, keepdims=True)
    )


def after(x, *others):
    return lax.optimization_barrier((x,) + others)[0]


def per_device(
    tokens,
    block_owner,
    first_gain,
    first_shift,
    mixer_in,
    mixer_out,
    mixer_bias,
    second_gain,
    second_shift,
    up_weight,
    up_bias,
    down_weight,
    down_bias,
    out_grad,
):
    groups = lax.axis_size("fsdp")
    member = lax.axis_index("fsdp")
    n_ctx = lax.axis_size("ctx")
    here = lax.axis_index("ctx")
    slot, width = tokens.shape[2:]
    block_len = slot * groups
    local_rows = 2 * slot
    count_rows = 2 * block_len
    blocks = 2 * n_ctx
    share = width // groups
    hidden = up_weight.shape[0]
    hidden_cut = hidden // n_ctx
    heads = -(-HEADS // groups)
    part = heads * HEAD_DIM
    wide = -(-part // 128) * 128
    chips = n_ctx // 2
    fetch = max(f for f in (1, 2, 4, 8, 16) if f <= chips and share % (16 * f) == 0)
    fold = max(f for f in (1, 2, 4, 8, 16) if f <= chips and share % (16 * f) == 0)
    chip = (here // 2) % fetch
    cut = share // (2 * fold)
    spread_c = jnp.arange(n_ctx, dtype=jnp.int32)

    own = tokens.reshape(2, slot, width)
    rows16 = tokens.reshape(local_rows, width)
    grad16 = out_grad.reshape(local_rows, width)
    index = jnp.stack([here, member, chip]).astype(jnp.int32)

    in_cut = lax.dynamic_slice_in_dim(mixer_in, chip * (share // fetch), share // fetch, 0)
    in_cut = in_cut.reshape(-1, 3, width)
    in_cut = jnp.pad(in_cut, ((0, 0), (0, 0), (0, groups * part - width)))
    in_cut = in_cut.reshape(-1, 3, groups, part)
    in_cut = jnp.stack([in_cut[:, 1], in_cut[:, 2], in_cut[:, 0]], axis=2)
    in_cut = in_cut.transpose(1, 0, 2, 3).reshape(groups, share // fetch, 3 * part)
    norm_row = jnp.pad(jnp.concatenate([first_gain, first_shift]), (0, 3 * part - 2 * share))
    norm_rows = jnp.broadcast_to(norm_row, (groups, 16, 3 * part))
    in_cut = jnp.concatenate([in_cut, norm_rows], axis=1)
    in_pieces = z_exchange([pick(in_cut, member ^ r) for r in range(groups)])
    in_pieces = jnp.stack(in_pieces)
    group_tokens = z_gather(after(own, in_pieces))
    norm_part = in_pieces[:, share // fetch :]
    in_parts = chip_spread(in_pieces[:, : share // fetch], fetch)
    group_tokens = after(tuple(group_tokens), *in_parts)
    gain_one = jnp.concatenate(
        [pick(norm_part[:, 0, :share], member ^ r)[None] for r in range(groups)]
    ).reshape(1, width).astype(F32)

    pieces = jax.ShapeDtypeStruct((2, block_len, width), BF16)
    keyval, query, normed16, unit_one, proj_in = in_vmem(
        functools.partial(project_kernel, groups=groups, fetch=fetch),
        index,
        list(group_tokens) + [norm_part] + in_parts,
        [
            jax.ShapeDtypeStruct((2, block_len, 2 * part), BF16),
            jax.ShapeDtypeStruct((2, block_len, wide), BF16),
            pieces,
            jax.ShapeDtypeStruct((2, block_len, width), F32),
            jax.ShapeDtypeStruct((width, 3 * part), BF16),
        ],
    )
    keyvals = chip_spread(keyval, chips)

    owners = block_owner.reshape(-1)
    numbers = jnp.arange(blocks, dtype=jnp.int32)
    places = jnp.sum(jnp.where(owners[None, :] == numbers[:, None], numbers[None, :], 0), axis=1)
    offset = (places // 2) ^ here
    places = (offset % 2) * n_ctx + (offset // 2) * 2 + places % 2
    meta = jnp.concatenate(
        [
            places,
            lax.dynamic_index_in_dim(block_owner, here, 0, keepdims=False),
            (member * slot)[None],
        ]
    ).astype(jnp.int32)

    grads_all = lax.all_gather(grad16, "ctx", axis=0, tiled=True)
    order = jnp.concatenate([spread_c[0::2], spread_c[1::2]]) ^ here
    grads_all = shuffle(grads_all.reshape(n_ctx, local_rows, width), order, BF16)
    grads_all = grads_all.reshape(n_ctx * local_rows, width)
    extra = jnp.concatenate([mixer_bias, second_gain, second_shift, down_bias]).reshape(1, 4 * share)
    extra = jnp.concatenate([extra, jnp.pad(up_bias, (0, 4 * share - hidden))[None]])
    extra = jnp.pad(extra, ((0, 14), (0, width - 4 * share)))
    out_pack = after(jnp.concatenate([mixer_out, extra]), *group_tokens)
    out_pack = lax.all_gather(out_pack, "fsdp", axis=0, tiled=True)
    out_pack = out_pack.reshape(groups, share + 16, width)
    proj_out = out_pack[:, :share].reshape(width, width)
    proj_out = jnp.pad(proj_out, ((0, groups * part - width), (0, 0)))
    proj_out = proj_out.reshape(groups, part, width)
    vectors = jnp.concatenate(
        [out_pack[:, share, i * share : (i + 1) * share].reshape(1, width) for i in range(4)]
        + [jnp.zeros((4, width), BF16)]
    ).astype(F32)
    up_bias_part = lax.dynamic_slice_in_dim(
        out_pack[:, share + 1], here * hidden_cut, hidden_cut, 1
    ).reshape(groups * hidden_cut)
    *keyvals, grads_all = lax.optimization_barrier((*keyvals, grads_all))
    keyvals = keyvals + [swap(piece, "ctx", 1) for piece in keyvals]
    ffn_cut = jnp.concatenate(
        [
            lax.dynamic_slice_in_dim(up_weight, here * hidden_cut, hidden_cut, 0),
            lax.dynamic_slice_in_dim(down_weight, here * hidden_cut, hidden_cut, 0),
        ]
    )
    ffn_parts = lax.all_gather(after(ffn_cut, *group_tokens), "fsdp", axis=0, tiled=True)
    ffn_parts = ffn_parts.reshape(groups, 2, hidden_cut, width)
    up_part = ffn_parts[:, 0].reshape(groups * hidden_cut, width)
    down_part = ffn_parts[:, 1].reshape(groups * hidden_cut, width)

    pair = jax.ShapeDtypeStruct((2, slot, part), BF16)
    results = forward_call(meta, query, keyvals, heads, groups)
    own_attended = results[:groups]
    sums, lse = results[groups:]
    attended = z_exchange(results[:groups])
    proj_out, vectors, *attended = lax.optimization_barrier((proj_out, vectors, *attended))
    resid, second16 = in_vmem(
        functools.partial(second_kernel, groups=groups),
        index,
        attended + [rows16, proj_out, vectors],
        [
            jax.ShapeDtypeStruct((local_rows, width), F32),
            jax.ShapeDtypeStruct((local_rows, width), BF16),
        ],
    )

    second_held = chip_spread(second16, chips)
    up_part, down_part, *second_held = lax.optimization_barrier((up_part, down_part, *second_held))
    second_all = jnp.concatenate(second_held + [swap(s, "ctx", 1) for s in second_held])
    pre = contract_cols(second_all, up_part) + up_bias_part.astype(F32)
    act, gate_pull = jax.vjp(functools.partial(jax.nn.gelu, approximate=True), pre)
    act16 = act.astype(BF16)
    pre_grad = gate_pull(contract_cols(grads_all, down_part))[0].astype(BF16)
    second_part = mm(pre_grad, up_part).astype(BF16).reshape(2, chips, local_rows, width)
    up_term = contract_rows(pre_grad, second_all).astype(BF16)
    down_term = contract_rows(act16, grads_all).astype(BF16)
    feed_part = mm(act16, down_part).astype(BF16)
    second_sums = ctx_collect(second_part[0], second_part[1])
    back_order = spread_c ^ here
    back_order = (back_order % 2) * chips + back_order // 2
    feed = shuffle(feed_part.reshape(n_ctx, local_rows, width), back_order, BF16)
    feed = feed.reshape(n_ctx * local_rows, width)
    ffn_terms = jnp.concatenate(
        [
            up_term.reshape(groups, hidden_cut, width),
            down_term.reshape(groups, hidden_cut, width),
        ],
        axis=1,
    ).reshape(groups * 2 * hidden_cut, width)
    feed, ffn_terms, *second_sums = lax.optimization_barrier((feed, ffn_terms, *second_sums))
    feed = lax.psum_scatter(feed, "ctx", scatter_dimension=0, tiled=True)
    results = in_vmem(
        functools.partial(branch_kernel, groups=groups, chips=chips),
        index,
        second_sums + [resid, grad16, proj_out, vectors],
        [pair] * groups
        + [
            jax.ShapeDtypeStruct((local_rows, width), F32),
            jax.ShapeDtypeStruct((local_rows, width), BF16),
            jax.ShapeDtypeStruct((8, width), F32),
        ],
    )
    resid_grad, branch_grad16, totals = results[groups:]
    attend_grads = z_exchange(results[:groups])
    branches = branch_grad16[None]
    branches = jnp.concatenate([branches, swap(branches, "fsdp", 1)])
    branches, *attend_grads = lax.optimization_barrier((branches, *attend_grads))
    mask = 2
    while mask < groups:
        branches = jnp.concatenate([branches, swap(branches, "fsdp", mask)])
        mask *= 2

    query_grad, keyval_keep, keyval_send = backward_call(
        meta, query, keyvals, attend_grads, sums, lse, heads, groups
    )
    keyval_sums = ctx_collect(keyval_keep, after(keyval_send, branches))
    feed, *keyval_sums = lax.optimization_barrier((feed, *keyval_sums))

    ffn_terms = after(ffn_terms, branches, query_grad)
    ffn_term = lax.psum_scatter(ffn_terms, "fsdp", scatter_dimension=0, tiled=True)

    with_out = part == share and (cut // 8) * (width - 3 * part) == 3 * part
    up_bias_terms = jnp.sum(pre_grad.astype(F32), axis=0).reshape(groups, hidden_cut)
    up_bias_terms = lax.dynamic_update_slice(
        jnp.zeros((groups, hidden), F32), up_bias_terms, (0, here * hidden_cut)
    )
    half = jax.ShapeDtypeStruct((fold, groups + with_out, cut + 8, 3 * part), BF16)
    results = in_vmem(
        functools.partial(
            handed_kernel, groups=groups, chips=chips, cut=cut, share=share, with_out=with_out
        ),
        index,
        keyval_sums
        + [query_grad, normed16, unit_one, proj_in, totals, up_bias_terms]
        + (list(own_attended) + [branches] if with_out else []),
        [jax.ShapeDtypeStruct((2, slot, width), BF16)] * (groups // 2)
        + [jax.ShapeDtypeStruct((groups // 2, 2, slot, width), BF16), half, half],
        [
            pltpu.VMEM((2, block_len, 3 * part), BF16),
            pltpu.VMEM((width, 3 * part), F32),
            pltpu.VMEM((share, width), F32),
            pltpu.VMEM((groups, 8, 3 * part), F32),
        ],
    )
    *normed_pieces, normed_far, in_keep, in_send = results
    ffn_grads = lax.all_gather(after(ffn_term, in_keep), "ctx", axis=0, tiled=True)
    in_sums = ctx_collect(in_keep, in_send)
    mask = groups // 2
    came = swap(normed_far, "fsdp", mask)
    came, *in_sums = lax.optimization_barrier((came, *in_sums))
    normed_pieces = [add16(piece, came[i]) for i, piece in enumerate(normed_pieces)]
    while mask > 1:
        mask //= 2
        came = swap(jnp.stack(normed_pieces[mask:]), "fsdp", mask)
        normed_pieces = [add16(piece, came[i]) for i, piece in enumerate(normed_pieces[:mask])]
    normed_grad = normed_pieces[0]
    in_term = sum(piece.astype(F32) for piece in in_sums).astype(BF16)
    mask = 2 * fold
    while mask < n_ctx:
        in_term = add16(in_term, swap(in_term, "ctx", mask))
        mask *= 2
    handed = z_exchange([in_term[r] for r in range(groups)])
    across = (3 + with_out) * width
    in_block, small = in_vmem(
        functools.partial(
            rows_kernel, groups=groups, cut=cut, part=part, width=width, with_out=with_out
        ),
        index,
        handed + ([in_term[groups]] if with_out else []),
        [
            jax.ShapeDtypeStruct((cut, across), BF16),
            jax.ShapeDtypeStruct((8, 3 * part), F32),
        ],
        [pltpu.VMEM((groups, cut, 3 * part), F32)],
    )
    in_held = chip_spread(in_block, fold)
    tokens_grad = in_vmem(
        tokens_kernel,
        index,
        [normed_grad, rows16, gain_one, resid_grad],
        [jax.ShapeDtypeStruct((local_rows, width), F32)],
    )[0]
    block_out = (resid + feed.astype(F32) + vectors[3:4]).astype(BF16)

    ffn_grads = ffn_grads.reshape(n_ctx, 2, hidden_cut, width).astype(F32)
    up_grad = ffn_grads[:, 0].reshape(hidden, width)
    down_grad = ffn_grads[:, 1].reshape(hidden, width)
    up_grad, down_grad, *in_held = lax.optimization_barrier((up_grad, down_grad, *in_held))
    in_held = in_held + [swap(piece, "ctx", 1) for piece in in_held]
    tokens_grad, *in_held = lax.optimization_barrier((tokens_grad, *in_held))
    homes = in_vmem(
        functools.partial(home_kernel, cut=cut, fetch=fold, with_out=with_out),
        index,
        in_held,
        [
            jax.ShapeDtypeStruct((share, wide_out), F32)
            for wide_out in ((3 * width, width) if with_out else (3 * width,))
        ],
    )
    mixer_in_grad, mixer_out_grad = homes[0], homes[-1]

    if not with_out:
        whole = jnp.stack(attended).reshape(groups, local_rows, part)
        whole = jnp.concatenate([pick(whole, member ^ i) for i in range(groups)], axis=1)
        out_term = contract_rows(whole[:, :width], branch_grad16).astype(BF16)
        out_term = lax.psum_scatter(out_term, "fsdp", scatter_dimension=0, tiled=True)
        mixer_out_grad = lax.psum(out_term, "ctx").astype(F32)

    bias_rows = -(-hidden // (3 * part))
    up_bias_grad = small[3 : 3 + bias_rows].reshape(-1)[:hidden]
    return (
        block_out.reshape(1, 2, slot, width),
        tokens_grad.reshape(1, 2, slot, width),
        small[0, :share],
        small[0, share : 2 * share],
        mixer_in_grad,
        mixer_out_grad,
        small[1, :share],
        small[1, share : 2 * share],
        small[2, :share],
        up_grad,
        up_bias_grad,
        down_grad,
        small[2, share : 2 * share],
    )


def solution(mesh):
    in_specs = (
        P("ctx", None, "fsdp", None),
        P(),
        P("fsdp"),
        P("fsdp"),
        P("fsdp", None),
        P("fsdp", None),
        P("fsdp"),
        P("fsdp"),
        P("fsdp"),
        P("fsdp", None),
        P("fsdp"),
        P("fsdp", None),
        P("fsdp"),
        P("ctx", None, "fsdp", None),
    )
    out_specs = (
        P("ctx", None, "fsdp", None),
        P("ctx", None, "fsdp", None),
        P("fsdp"),
        P("fsdp"),
        P("fsdp", None),
        P("fsdp", None),
        P("fsdp"),
        P("fsdp"),
        P("fsdp"),
        P("fsdp", None),
        P("fsdp"),
        P("fsdp", None),
        P("fsdp"),
    )
    return jax.shard_map(
        per_device, mesh=mesh, in_specs=in_specs, out_specs=out_specs, check_vma=False
    )
```

```python
import functools

import jax
import jax.numpy as jnp
from jax import lax
from jax.experimental import pallas as pl
from jax.experimental.pallas import tpu as pltpu
from jax.sharding import PartitionSpec as P

HEADS = 12
HEAD_DIM = 64

EPS = 1e-05
MASKED = -1e30
F32 = jnp.float32
BF16 = jnp.bfloat16
VMEM_LIMIT = 56 * 1024 * 1024


def swap(x, axis, mask):
    return lax.ppermute(x, axis, [(i, i ^ mask) for i in range(lax.axis_size(axis))])


def add16(left, right):
    return (left.astype(F32) + right.astype(F32)).astype(BF16)


def z_gather(x):
    return [x] + [swap(x, "fsdp", r) for r in range(1, lax.axis_size("fsdp"))]


def z_exchange(pieces):
    return [pieces[0]] + [swap(pieces[r], "fsdp", r) for r in range(1, len(pieces))]


def z_sum(pieces):
    return sum(piece.astype(F32) for piece in z_exchange(pieces))


def chip_spread(x, chips):
    return [x] + [swap(x, "ctx", 2 * r) for r in range(1, chips)]


def ctx_spread(x):
    held = chip_spread(x, lax.axis_size("ctx") // 2)
    return held + [swap(piece, "ctx", 1) for piece in held]


def ctx_collect(keep, send):
    came = swap(send, "ctx", 1)
    pieces = [add16(keep[r], came[r]) for r in range(keep.shape[0])]
    return [pieces[0]] + [swap(pieces[r], "ctx", 2 * r) for r in range(1, len(pieces))]


def pick(stacked, index):
    return lax.dynamic_index_in_dim(stacked, index, 0, keepdims=False)


def shuffle_kernel(table, x_ref, out_ref):
    width = x_ref.shape[2]
    extra = out_ref.shape[2] - width
    for i in range(out_ref.shape[0]):
        out_ref[i, :, :width] = x_ref[table[i]].astype(out_ref.dtype)
        if extra:
            out_ref[i, :, width:] = jnp.zeros((x_ref.shape[1], extra), out_ref.dtype)


def shuffle(x, table, kind, width=None):
    shape = (table.shape[0], x.shape[1], width or x.shape[2])
    return pl.pallas_call(
        shuffle_kernel,
        grid_spec=pltpu.PrefetchScalarGridSpec(
            num_scalar_prefetch=1,
            grid=(),
            in_specs=[pl.BlockSpec(memory_space=pltpu.VMEM)],
            out_specs=pl.BlockSpec(memory_space=pltpu.VMEM),
        ),
        out_shape=jax.ShapeDtypeStruct(shape, kind),
        compiler_params=pltpu.CompilerParams(vmem_limit_bytes=VMEM_LIMIT),
    )(table, x)


def mm(left, right):
    return jnp.dot(left, right, preferred_element_type=F32)


def contract_rows(left, right):
    return lax.dot_general(left, right, (((0,), (0,)), ((), ())), preferred_element_type=F32)


def contract_cols(left, right):
    return lax.dot_general(left, right, (((1,), (1,)), ((), ())), preferred_element_type=F32)


def head_cols(values, at, heads):
    cols = lax.broadcasted_iota(jnp.int32, values.shape, 1) - at
    return [
        jnp.where((cols >= h * HEAD_DIM) & (cols < (h + 1) * HEAD_DIM), values, 0.0).astype(BF16)
        for h in range(heads)
    ]


def causal_mask(heads, size, flip):
    queries = lax.broadcasted_iota(jnp.int32, (heads * size, size), 0) % size ^ flip
    keys = lax.broadcasted_iota(jnp.int32, (heads * size, size), 1) ^ flip
    return keys <= queries


def lanes(combine, values):
    return functools.reduce(
        combine, [values[:, i : i + 128] for i in range(0, values.shape[1], 128)]
    )


def widen(values, width):
    return jnp.concatenate([values] * (width // 128), axis=1)


def load_pieces(pieces, kv_ref, sems):
    copies = [
        pltpu.make_async_copy(piece, kv_ref.at[pl.ds(2 * i, 2)], sems.at[i])
        for i, piece in enumerate(pieces)
    ]
    for copy in copies:
        copy.start()
    return copies


def in_groups(start, stop, step, widest=4):
    many = widest
    while many:

        def some(i, carry, many=many, start=start):
            step(tuple(start + many * i + k for k in range(many)))
            return carry

        steps = (stop - start) // many
        lax.fori_loop(0, steps, some, 0)
        start = start + many * steps
        many //= 2


def attend_kernel(meta, *refs, heads, pieces, groups, rows):
    q_ref = refs[0]
    piece_refs = refs[1 : 1 + pieces]
    outs = refs[1 + pieces : 1 + pieces + groups]
    sum_ref, lse_ref, kv_ref, sems, score_ref, top_ref, total_ref, acc_ref = refs[
        1 + pieces + groups :
    ]
    size, wide = q_ref.shape[1:]
    slot = size // groups
    count = 2 * pieces
    width = heads * HEAD_DIM
    scale = HEAD_DIM ** (-0.5)
    copies = load_pieces(piece_refs, kv_ref, sems)
    copies[0].wait()
    for j in range(2):
        block = meta[count + j]
        for tile in range(size // rows):
            spot = pl.ds(tile * rows, rows)
            query = jnp.concatenate(head_cols(q_ref[j, spot].astype(F32) * scale, 0, heads), axis=0)

            def score(n):
                return contract_cols(query, kv_ref[meta[n], :, :wide])

            def scores(ns):
                found = [score(n) for n in ns]
                top = top_ref[...]
                for n, value in zip(ns, found, strict=True):
                    score_ref[n] = value
                    top = jnp.maximum(top, lanes(jnp.maximum, value))
                top_ref[...] = top

            def weights(ns):
                total = total_ref[...]
                acc = acc_ref[...]
                top = widen(top_ref[...], size)
                for n in ns:
                    weight = jnp.exp(score_ref[n] - top)
                    total += lanes(jnp.add, weight)
                    acc += mm(weight.astype(BF16), kv_ref[meta[n], :, 2 * width - wide :])
                total_ref[...] = total
                acc_ref[...] = acc

            seen = causal_mask(heads, size, meta[count + 2])
            if rows < size:
                seen = jnp.concatenate(
                    [seen[h * size + tile * rows :][:rows] for h in range(heads)], axis=0
                )
            own = jnp.where(seen, score(block), MASKED)
            score_ref[block] = own
            top_ref[...] = lanes(jnp.maximum, own)
            if j == 0 and tile == 0:
                for copy in copies[1:]:
                    copy.wait()
            in_groups(0, block, scores)
            top_ref[...] = jnp.broadcast_to(
                jnp.max(top_ref[...], axis=1, keepdims=True), top_ref.shape
            )
            total_ref[...] = jnp.zeros_like(total_ref)
            acc_ref[...] = jnp.zeros_like(acc_ref)
            in_groups(0, block + 1, weights)
            total = jnp.sum(total_ref[...], axis=1, keepdims=True)
            lse = jnp.broadcast_to(top_ref[:, :1] + jnp.log(total), top_ref.shape)
            result = acc_ref[...] / total
            mine = lax.broadcasted_iota(jnp.int32, (rows, wide), 1) - (wide - width)
            whole = sum(
                jnp.where(
                    (mine >= h * HEAD_DIM) & (mine < (h + 1) * HEAD_DIM),
                    result[h * rows : (h + 1) * rows],
                    0.0,
                )
                for h in range(heads)
            )
            sum_ref[j, spot] = whole
            whole = whole[:, wide - width :].astype(BF16)
            for h in range(heads):
                lse_ref[j, pl.ds(h * size + tile * rows, rows)] = lse[h * rows : (h + 1) * rows]
            for i in range(rows // slot):
                outs[tile * rows // slot + i][j] = whole[i * slot : (i + 1) * slot]


def attend_back_kernel(meta, *refs, heads, pieces, groups):
    q_ref = refs[0]
    piece_refs = refs[1 : 1 + pieces]
    grad_refs = refs[1 + pieces : 1 + pieces + groups]
    sum_ref, lse_ref, dq_ref, keep_ref, send_ref, kv_ref, sems, acc_ref, dq_acc = refs[
        1 + pieces + groups :
    ]
    size, wide = q_ref.shape[1:]
    count = 2 * pieces
    width = heads * HEAD_DIM
    pad = wide - width
    scale = HEAD_DIM ** (-0.5)
    copies = load_pieces(piece_refs, kv_ref, sems)
    acc_ref[...] = jnp.zeros_like(acc_ref)
    for copy in copies:
        copy.wait()
    for j in range(2):
        block = meta[count + j]
        query = q_ref[j].astype(F32) * scale
        query_turned = jnp.transpose(query).astype(BF16)
        queries = jnp.concatenate(head_cols(query, 0, heads), axis=0)
        grad = jnp.concatenate([grad_refs[r][j] for r in range(groups)], axis=0)
        grad_turned = jnp.transpose(grad.astype(F32))
        if pad:
            grad_turned = jnp.concatenate([jnp.zeros((pad, size), F32), grad_turned], axis=0)
        grad = jnp.transpose(grad_turned)
        grad_turned = grad_turned.astype(BF16)
        cols = head_cols(grad, pad, heads)
        grads = jnp.concatenate(cols, axis=0)
        dots = jnp.concatenate(
            [jnp.sum(col.astype(F32) * sum_ref[j], axis=1, keepdims=True) for col in cols], axis=0
        )
        dots = jnp.broadcast_to(dots, (heads * size, 128))
        dq_acc[...] = jnp.zeros_like(dq_acc)

        def visit(ns, diagonal=False):
            dq = dq_acc[...]
            for n in ns:
                place = meta[n]
                keys = kv_ref[place, :, :wide]
                values = kv_ref[place, :, 2 * width - wide :]
                score = contract_cols(queries, keys)
                if diagonal:
                    score = jnp.where(causal_mask(heads, size, meta[count + 2]), score, MASKED)
                prob = jnp.exp(score - widen(lse_ref[j], size))
                prob_grad = contract_cols(grads, values)
                score_grad = (prob * (prob_grad - widen(dots, size))).astype(BF16)
                prob = prob.astype(BF16)
                dq += mm(score_grad, keys)
                for h in range(heads):
                    mine = slice(h * size, (h + 1) * size)
                    at = h * HEAD_DIM
                    acc_ref[place, at : at + HEAD_DIM] += mm(
                        query_turned[at : at + HEAD_DIM], score_grad[mine]
                    )
                    acc_ref[place, width + at : width + at + HEAD_DIM] += mm(
                        grad_turned[pad + at : pad + at + HEAD_DIM], prob[mine]
                    )
            dq_acc[...] = dq

        visit((block,), True)
        in_groups(0, block, visit)
        mine = lax.broadcasted_iota(jnp.int32, (size, wide), 1)
        whole = sum(
            jnp.where(
                (mine >= h * HEAD_DIM) & (mine < (h + 1) * HEAD_DIM),
                dq_acc[h * size : (h + 1) * size],
                0.0,
            )
            for h in range(heads)
        )
        dq_ref[j] = (whole[:, :width] * scale).astype(BF16)
    for i in range(count):
        to_ref = keep_ref if i < pieces else send_ref
        to_ref[i % pieces // 2, i % 2] = acc_ref[i].astype(BF16)


def forward_call(meta, query, keyvals, heads, groups):
    size, wide = query.shape[1:]
    part = heads * HEAD_DIM
    pieces = len(keyvals)
    rows = size
    while heads * rows * size * 2 * pieces > 1 << 22 and rows > size // groups:
        rows //= 2
    return in_vmem(
        functools.partial(attend_kernel, heads=heads, pieces=pieces, groups=groups, rows=rows),
        meta,
        [query] + keyvals,
        [jax.ShapeDtypeStruct((2, size // groups, part), BF16)] * groups
        + [
            jax.ShapeDtypeStruct((2, size, wide), F32),
            jax.ShapeDtypeStruct((2, heads * size, 128), F32),
        ],
        [
            pltpu.VMEM((2 * pieces, size, 2 * part), BF16),
            pltpu.SemaphoreType.DMA((pieces,)),
            pltpu.VMEM((2 * pieces, heads * rows, size), F32),
            pltpu.VMEM((heads * rows, 128), F32),
            pltpu.VMEM((heads * rows, 128), F32),
            pltpu.VMEM((heads * rows, wide), F32),
        ],
        40 * pieces * size * size * wide * heads,
        range(1, 1 + pieces),
    )


def backward_call(meta, query, keyvals, grads, sums, lse, heads, groups):
    size, wide = query.shape[1:]
    part = heads * HEAD_DIM
    pieces = len(keyvals)
    half = jax.ShapeDtypeStruct((pieces // 2, 2, 2 * part, size), BF16)
    return in_vmem(
        functools.partial(attend_back_kernel, heads=heads, pieces=pieces, groups=groups),
        meta,
        [query] + keyvals + grads + [sums, lse],
        [jax.ShapeDtypeStruct((2, size, part), BF16), half, half],
        [
            pltpu.VMEM((2 * pieces, size, 2 * part), BF16),
            pltpu.SemaphoreType.DMA((pieces,)),
            pltpu.VMEM((2 * pieces, 2 * part, size), F32),
            pltpu.VMEM((heads * size, wide), F32),
        ],
        24 * pieces * size * size * wide * heads,
        range(1, 1 + pieces),
    )


def project_kernel(meta, *refs, groups, fetch):
    tokens = refs[:groups]
    norm_ref = refs[groups]
    parts = refs[groups + 1 : groups + 1 + fetch]
    kv_ref, q_ref, normed_ref, unit_ref, proj_ref = refs[groups + 1 + fetch :]
    member, chip = meta[1], meta[2]
    depth, across = proj_ref.shape
    share = depth // groups
    for c in range(fetch):
        for z in range(groups):
            start = (member ^ z) * share + (chip ^ c) * (share // fetch)
            proj_ref[pl.ds(pl.multiple_of(start, 16), share // fetch)] = parts[c][z]
    rows = [norm_ref[member ^ z][:1].astype(F32) for z in range(groups)]
    gain = jnp.concatenate([row[:, :share] for row in rows], axis=1)
    shift = jnp.concatenate([row[:, share : 2 * share] for row in rows], axis=1)
    part2 = kv_ref.shape[2]
    wide = q_ref.shape[2]
    size = kv_ref.shape[1]
    for j in range(2):
        x = jnp.concatenate([ref[j] for ref in tokens], axis=0).astype(F32)
        unit, _ = norm_parts(x)
        normed = (unit * gain + shift).astype(BF16)
        unit_ref[j] = unit
        normed_ref[j] = normed
        mixed = mm(normed, proj_ref[...]).astype(BF16)
        kv_ref[j] = mixed[:, :part2]
        q_ref[j, :, : across - part2] = mixed[:, part2:]
        if wide > across - part2:
            q_ref[j, :, across - part2 :] = jnp.zeros((size, wide - across + part2), BF16)


def second_kernel(meta, *refs, groups):
    pieces = refs[:groups]
    x_ref, proj_ref, vec_ref, resid_ref, second_ref = refs[groups:]
    member = meta[1]
    slot, part = pieces[0].shape[1:]
    total = x_ref[...].astype(F32) + vec_ref[0:1]
    for z in range(groups):
        total += mm(pieces[z][...].reshape(2 * slot, part), proj_ref[member ^ z])
    resid_ref[...] = total
    unit, _ = norm_parts(total)
    second_ref[...] = (unit * vec_ref[1:2] + vec_ref[2:3]).astype(BF16)


def branch_kernel(meta, *refs, groups, chips):
    sums = refs[:chips]
    resid_ref, grad_ref, proj_ref, vec_ref = refs[chips : chips + 4]
    outs = refs[chips + 4 : chips + 4 + groups]
    resid_grad_ref, branch_ref, totals_ref = refs[chips + 4 + groups :]
    member = meta[1]
    slot, part = outs[0].shape[1:]
    second_grad = sum(ref[...].astype(F32) for ref in sums)
    unit, rate = norm_parts(resid_ref[...])
    dout = grad_ref[...].astype(F32)
    resid_grad = dout + norm_back(unit, rate, vec_ref[1:2], second_grad)
    resid_grad_ref[...] = resid_grad
    branch = resid_grad.astype(BF16)
    branch_ref[...] = branch
    for z in range(groups):
        grads = contract_cols(branch, proj_ref[member ^ z]).astype(BF16)
        outs[z][...] = grads.reshape(2, slot, part)
    totals_ref[0:1] = jnp.sum(branch.astype(F32), axis=0, keepdims=True)
    totals_ref[1:2] = jnp.sum(second_grad * unit, axis=0, keepdims=True)
    totals_ref[2:3] = jnp.sum(second_grad, axis=0, keepdims=True)
    totals_ref[3:4] = jnp.sum(dout, axis=0, keepdims=True)
    totals_ref[4:] = jnp.zeros((4, totals_ref.shape[1]), F32)


def handed_kernel(meta, *refs, groups, chips, cut, share, with_out):
    sums = refs[:chips]
    dq_ref, normed_ref, unit_ref, proj_ref, totals_ref, up_bias_ref = refs[chips : chips + 6]
    at = chips + 6
    attended = refs[at : at + groups] if with_out else ()
    branches = refs[at + groups] if with_out else None
    at += (groups + 1) * with_out
    half = groups // 2
    outs = refs[at : at + half]
    far_ref, keep_ref, send_ref, grad_ref, term_ref, out_term_ref, vec_ref = refs[at + half :]
    here, member = meta[0], meta[1]
    fetch = keep_ref.shape[0]
    across = keep_ref.shape[3]
    slot = outs[0].shape[1]
    size = slot * groups
    width = unit_ref.shape[2]
    gain_total = jnp.zeros((1, width), F32)
    shift_total = jnp.zeros((1, width), F32)
    for j in range(2):
        keyval = jnp.transpose(sum(ref[j].astype(F32) for ref in sums)).astype(BF16)
        grad = jnp.concatenate([keyval, dq_ref[j]], axis=1)
        grad_ref[j] = grad
        normed_grad = contract_cols(grad, proj_ref[...])
        gain_total += jnp.sum(normed_grad * unit_ref[j], axis=0, keepdims=True)
        shift_total += jnp.sum(normed_grad, axis=0, keepdims=True)
        for z in range(groups):
            piece = normed_grad[z * slot : (z + 1) * slot].astype(BF16)
            if z < half:
                outs[z][j] = piece
            else:
                far_ref[z - half, j] = piece
    term_ref[...] = contract_rows(
        normed_ref[...].reshape(2 * size, width), grad_ref[...].reshape(2 * size, across)
    )
    if with_out:
        out_term_ref[...] = sum(
            contract_rows(piece[...].reshape(2 * slot, share), branches[z])
            for z, piece in enumerate(attended)
        )
    hidden = up_bias_ref.shape[1]
    vec_ref[...] = jnp.zeros_like(vec_ref)
    for z in range(groups):
        cols = slice(z * share, (z + 1) * share)
        vec_ref[z, 0:1, :share] = gain_total[:, cols]
        vec_ref[z, 0:1, share : 2 * share] = shift_total[:, cols]
        vec_ref[z, 1:2, :share] = totals_ref[0:1, cols]
        vec_ref[z, 1:2, share : 2 * share] = totals_ref[1:2, cols]
        vec_ref[z, 2:3, :share] = totals_ref[2:3, cols]
        vec_ref[z, 2:3, share : 2 * share] = totals_ref[3:4, cols]
        done = 0
        while done < hidden:
            size_now = min(across, hidden - done)
            row = 3 + done // across
            vec_ref[z, row : row + 1, :size_now] = up_bias_ref[z : z + 1, done : done + size_now]
            done += size_now
    for core, to_ref in enumerate((keep_ref, send_ref)):
        for r in range(fetch):
            mine = ((here ^ (2 * r + core)) & (2 * fetch - 1)) * cut
            for z in range(groups):
                owner = member ^ z
                start = pl.multiple_of(owner * share + mine, 8)
                rows = term_ref[pl.ds(start, cut)]
                to_ref[r, z] = jnp.concatenate([rows, vec_ref[owner]], axis=0).astype(BF16)
            if with_out:
                rows = out_term_ref[pl.ds(pl.multiple_of(mine, 8), cut)]
                rest = jnp.concatenate(
                    [rows[8 * i : 8 * i + 8, across:] for i in range(cut // 8)], axis=1
                )
                to_ref[r, groups] = jnp.concatenate([rows[:, :across], rest], axis=0).astype(BF16)


def rows_kernel(meta, *refs, groups, cut, part, width, with_out):
    pieces = refs[:groups]
    block_ref, small_ref, turned = refs[-3:]
    member = meta[1]
    across = 3 * part
    total = jnp.zeros(small_ref.shape, F32)
    for z in range(groups):
        value = pieces[z][...].astype(F32)
        total += value[cut:]
        turned[member ^ z] = value[:cut]
    small_ref[...] = total
    held = [turned[z] for z in range(groups)]
    for k, home in enumerate((width, 2 * width, 0)):
        whole = jnp.concatenate([h[:, k * part : (k + 1) * part] for h in held], axis=1)
        block_ref[:, home : home + width] = whole[:, :width].astype(BF16)
    if with_out:
        block = refs[groups][...].astype(F32)
        rest = jnp.concatenate(
            [
                block[cut : cut + 8, i * (width - across) : (i + 1) * (width - across)]
                for i in range(cut // 8)
            ],
            axis=0,
        )
        block = jnp.concatenate([block[:cut], rest], axis=1)
        block_ref[:, 3 * width :] = block.astype(BF16)


def home_kernel(meta, *refs, cut, fetch, with_out):
    pieces = refs[: 2 * fetch]
    outs = refs[2 * fetch :]
    here = meta[0]
    for i, piece in enumerate(pieces):
        r = 2 * (i % fetch) + i // fetch
        start = pl.multiple_of(((here ^ r) & (2 * fetch - 1)) * cut, 8)
        block = piece[...].astype(F32)
        at = 0
        for out in outs:
            out[pl.ds(start, cut)] = block[:, at : at + out.shape[1]]
            at += out.shape[1]


def tokens_kernel(meta, grad_ref, x_ref, gain_ref, resid_grad_ref, out_ref):
    rows, width = x_ref.shape
    grad = grad_ref[...].astype(F32).reshape(rows, width)
    unit, rate = norm_parts(x_ref[...].astype(F32))
    out_ref[...] = resid_grad_ref[...] + norm_back(unit, rate, gain_ref[...], grad)


def in_vmem(kernel, meta, arrays, outs, scratch=(), flops=0, there=()):
    vmem = pl.BlockSpec(memory_space=pltpu.VMEM)
    anywhere = pl.BlockSpec(memory_space=pl.ANY)
    return pl.pallas_call(
        kernel,
        grid_spec=pltpu.PrefetchScalarGridSpec(
            num_scalar_prefetch=1,
            grid=(),
            in_specs=[anywhere if i in there else vmem for i in range(len(arrays))],
            out_specs=[vmem] * len(outs),
            scratch_shapes=list(scratch),
        ),
        out_shape=outs,
        compiler_params=pltpu.CompilerParams(vmem_limit_bytes=VMEM_LIMIT),
        cost_estimate=pl.CostEstimate(flops=flops, bytes_accessed=1 << 20, transcendentals=0),
    )(meta, *arrays)


def norm_parts(values):
    center = values - jnp.mean(values, axis=-1, keepdims=True)
    rate = lax.rsqrt(jnp.mean(center * center, axis=-1, keepdims=True) + EPS)
    return center * rate, rate


def norm_back(unit, rate, gain, grad):
    e = gain * grad
    return rate * (
        e
        - jnp.mean(e, axis=-1, keepdims=True)
        - unit * jnp.mean(e * unit, axis=-1, keepdims=True)
    )


def after(x, *others):
    return lax.optimization_barrier((x,) + others)[0]


def per_device(
    tokens,
    block_owner,
    first_gain,
    first_shift,
    mixer_in,
    mixer_out,
    mixer_bias,
    second_gain,
    second_shift,
    up_weight,
    up_bias,
    down_weight,
    down_bias,
    out_grad,
):
    groups = lax.axis_size("fsdp")
    member = lax.axis_index("fsdp")
    n_ctx = lax.axis_size("ctx")
    here = lax.axis_index("ctx")
    slot, width = tokens.shape[2:]
    block_len = slot * groups
    local_rows = 2 * slot
    count_rows = 2 * block_len
    blocks = 2 * n_ctx
    share = width // groups
    hidden = up_weight.shape[0]
    hidden_cut = hidden // n_ctx
    heads = -(-HEADS // groups)
    part = heads * HEAD_DIM
    wide = -(-part // 128) * 128
    chips = n_ctx // 2
    fetch = max(f for f in (1, 2, 4, 8, 16) if f <= chips and share % (16 * f) == 0)
    fold = max(f for f in (1, 2, 4, 8, 16) if f <= chips and share % (16 * f) == 0)
    chip = (here // 2) % fetch
    cut = share // (2 * fold)
    spread_c = jnp.arange(n_ctx, dtype=jnp.int32)

    own = tokens.reshape(2, slot, width)
    rows16 = tokens.reshape(local_rows, width)
    grad16 = out_grad.reshape(local_rows, width)
    index = jnp.stack([here, member, chip]).astype(jnp.int32)

    in_cut = lax.dynamic_slice_in_dim(mixer_in, chip * (share // fetch), share // fetch, 0)
    in_cut = in_cut.reshape(-1, 3, width)
    in_cut = jnp.pad(in_cut, ((0, 0), (0, 0), (0, groups * part - width)))
    in_cut = in_cut.reshape(-1, 3, groups, part)
    in_cut = jnp.stack([in_cut[:, 1], in_cut[:, 2], in_cut[:, 0]], axis=2)
    in_cut = in_cut.transpose(1, 0, 2, 3).reshape(groups, share // fetch, 3 * part)
    norm_row = jnp.pad(jnp.concatenate([first_gain, first_shift]), (0, 3 * part - 2 * share))
    norm_rows = jnp.broadcast_to(norm_row, (groups, 16, 3 * part))
    in_cut = jnp.concatenate([in_cut, norm_rows], axis=1)
    in_pieces = z_exchange([pick(in_cut, member ^ r) for r in range(groups)])
    in_pieces = jnp.stack(in_pieces)
    group_tokens = z_gather(after(own, in_pieces))
    norm_part = in_pieces[:, share // fetch :]
    in_parts = chip_spread(in_pieces[:, : share // fetch], fetch)
    group_tokens = after(tuple(group_tokens), *in_parts)
    gain_one = jnp.concatenate(
        [pick(norm_part[:, 0, :share], member ^ r)[None] for r in range(groups)]
    ).reshape(1, width).astype(F32)

    pieces = jax.ShapeDtypeStruct((2, block_len, width), BF16)
    keyval, query, normed16, unit_one, proj_in = in_vmem(
        functools.partial(project_kernel, groups=groups, fetch=fetch),
        index,
        list(group_tokens) + [norm_part] + in_parts,
        [
            jax.ShapeDtypeStruct((2, block_len, 2 * part), BF16),
            jax.ShapeDtypeStruct((2, block_len, wide), BF16),
            pieces,
            jax.ShapeDtypeStruct((2, block_len, width), F32),
            jax.ShapeDtypeStruct((width, 3 * part), BF16),
        ],
    )
    keyvals = chip_spread(keyval, chips)

    owners = block_owner.reshape(-1)
    numbers = jnp.arange(blocks, dtype=jnp.int32)
    places = jnp.sum(jnp.where(owners[None, :] == numbers[:, None], numbers[None, :], 0), axis=1)
    offset = (places // 2) ^ here
    places = (offset % 2) * n_ctx + (offset // 2) * 2 + places % 2
    meta = jnp.concatenate(
        [
            places,
            lax.dynamic_index_in_dim(block_owner, here, 0, keepdims=False),
            (member * slot)[None],
        ]
    ).astype(jnp.int32)

    grads_all = lax.all_gather(grad16, "ctx", axis=0, tiled=True)
    order = jnp.concatenate([spread_c[0::2], spread_c[1::2]]) ^ here
    grads_all = shuffle(grads_all.reshape(n_ctx, local_rows, width), order, BF16)
    grads_all = grads_all.reshape(n_ctx * local_rows, width)
    extra = jnp.concatenate([mixer_bias, second_gain, second_shift, down_bias]).reshape(1, 4 * share)
    extra = jnp.concatenate([extra, jnp.pad(up_bias, (0, 4 * share - hidden))[None]])
    extra = jnp.pad(extra, ((0, 14), (0, width - 4 * share)))
    out_pack = after(jnp.concatenate([mixer_out, extra]), *group_tokens)
    out_pack = lax.all_gather(out_pack, "fsdp", axis=0, tiled=True)
    out_pack = out_pack.reshape(groups, share + 16, width)
    proj_out = out_pack[:, :share].reshape(width, width)
    proj_out = jnp.pad(proj_out, ((0, groups * part - width), (0, 0)))
    proj_out = proj_out.reshape(groups, part, width)
    vectors = jnp.concatenate(
        [out_pack[:, share, i * share : (i + 1) * share].reshape(1, width) for i in range(4)]
        + [jnp.zeros((4, width), BF16)]
    ).astype(F32)
    up_bias_part = lax.dynamic_slice_in_dim(
        out_pack[:, share + 1], here * hidden_cut, hidden_cut, 1
    ).reshape(groups * hidden_cut)
    *keyvals, grads_all = lax.optimization_barrier((*keyvals, grads_all))
    keyvals = keyvals + [swap(piece, "ctx", 1) for piece in keyvals]
    ffn_cut = jnp.concatenate(
        [
            lax.dynamic_slice_in_dim(up_weight, here * hidden_cut, hidden_cut, 0),
            lax.dynamic_slice_in_dim(down_weight, here * hidden_cut, hidden_cut, 0),
        ]
    )
    ffn_parts = lax.all_gather(after(ffn_cut, *group_tokens), "fsdp", axis=0, tiled=True)
    ffn_parts = ffn_parts.reshape(groups, 2, hidden_cut, width)
    up_part = ffn_parts[:, 0].reshape(groups * hidden_cut, width)
    down_part = ffn_parts[:, 1].reshape(groups * hidden_cut, width)

    pair = jax.ShapeDtypeStruct((2, slot, part), BF16)
    results = forward_call(meta, query, keyvals, heads, groups)
    own_attended = results[:groups]
    sums, lse = results[groups:]
    attended = z_exchange(results[:groups])
    proj_out, vectors, *attended = lax.optimization_barrier((proj_out, vectors, *attended))
    resid, second16 = in_vmem(
        functools.partial(second_kernel, groups=groups),
        index,
        attended + [rows16, proj_out, vectors],
        [
            jax.ShapeDtypeStruct((local_rows, width), F32),
            jax.ShapeDtypeStruct((local_rows, width), BF16),
        ],
    )

    second_held = chip_spread(second16, chips)
    up_part, down_part, *second_held = lax.optimization_barrier((up_part, down_part, *second_held))
    second_all = jnp.concatenate(second_held + [swap(s, "ctx", 1) for s in second_held])
    pre = contract_cols(second_all, up_part) + up_bias_part.astype(F32)
    act, gate_pull = jax.vjp(functools.partial(jax.nn.gelu, approximate=True), pre)
    act16 = act.astype(BF16)
    pre_grad = gate_pull(contract_cols(grads_all, down_part))[0].astype(BF16)
    second_part = mm(pre_grad, up_part).astype(BF16).reshape(2, chips, local_rows, width)
    up_term = contract_rows(pre_grad, second_all).astype(BF16)
    down_term = contract_rows(act16, grads_all).astype(BF16)
    feed_part = mm(act16, down_part).astype(BF16)
    second_sums = ctx_collect(second_part[0], second_part[1])
    back_order = spread_c ^ here
    back_order = (back_order % 2) * chips + back_order // 2
    feed = shuffle(feed_part.reshape(n_ctx, local_rows, width), back_order, BF16)
    feed = feed.reshape(n_ctx * local_rows, width)
    ffn_terms = jnp.concatenate(
        [
            up_term.reshape(groups, hidden_cut, width),
            down_term.reshape(groups, hidden_cut, width),
        ],
        axis=1,
    ).reshape(groups * 2 * hidden_cut, width)
    feed, ffn_terms, *second_sums = lax.optimization_barrier((feed, ffn_terms, *second_sums))
    feed = lax.psum_scatter(feed, "ctx", scatter_dimension=0, tiled=True)
    results = in_vmem(
        functools.partial(branch_kernel, groups=groups, chips=chips),
        index,
        second_sums + [resid, grad16, proj_out, vectors],
        [pair] * groups
        + [
            jax.ShapeDtypeStruct((local_rows, width), F32),
            jax.ShapeDtypeStruct((local_rows, width), BF16),
            jax.ShapeDtypeStruct((8, width), F32),
        ],
    )
    resid_grad, branch_grad16, totals = results[groups:]
    attend_grads = z_exchange(results[:groups])
    branches = branch_grad16[None]
    branches = jnp.concatenate([branches, swap(branches, "fsdp", 1)])
    branches, *attend_grads = lax.optimization_barrier((branches, *attend_grads))
    mask = 2
    while mask < groups:
        branches = jnp.concatenate([branches, swap(branches, "fsdp", mask)])
        mask *= 2

    query_grad, keyval_keep, keyval_send = backward_call(
        meta, query, keyvals, attend_grads, sums, lse, heads, groups
    )
    keyval_sums = ctx_collect(keyval_keep, after(keyval_send, branches))
    feed, *keyval_sums = lax.optimization_barrier((feed, *keyval_sums))

    ffn_terms = after(ffn_terms, branches, query_grad)
    ffn_term = lax.psum_scatter(ffn_terms, "fsdp", scatter_dimension=0, tiled=True)

    with_out = part == share and (cut // 8) * (width - 3 * part) == 3 * part
    up_bias_terms = jnp.sum(pre_grad.astype(F32), axis=0).reshape(groups, hidden_cut)
    up_bias_terms = lax.dynamic_update_slice(
        jnp.zeros((groups, hidden), F32), up_bias_terms, (0, here * hidden_cut)
    )
    half = jax.ShapeDtypeStruct((fold, groups + with_out, cut + 8, 3 * part), BF16)
    results = in_vmem(
        functools.partial(
            handed_kernel, groups=groups, chips=chips, cut=cut, share=share, with_out=with_out
        ),
        index,
        keyval_sums
        + [query_grad, normed16, unit_one, proj_in, totals, up_bias_terms]
        + (list(own_attended) + [branches] if with_out else []),
        [jax.ShapeDtypeStruct((2, slot, width), BF16)] * (groups // 2)
        + [jax.ShapeDtypeStruct((groups // 2, 2, slot, width), BF16), half, half],
        [
            pltpu.VMEM((2, block_len, 3 * part), BF16),
            pltpu.VMEM((width, 3 * part), F32),
            pltpu.VMEM((share, width), F32),
            pltpu.VMEM((groups, 8, 3 * part), F32),
        ],
    )
    *normed_pieces, normed_far, in_keep, in_send = results
    ffn_grads = lax.all_gather(after(ffn_term, in_keep), "ctx", axis=0, tiled=True)
    in_sums = ctx_collect(in_keep, in_send)
    mask = groups // 2
    came = swap(normed_far, "fsdp", mask)
    came, *in_sums = lax.optimization_barrier((came, *in_sums))
    normed_pieces = [add16(piece, came[i]) for i, piece in enumerate(normed_pieces)]
    while mask > 1:
        mask //= 2
        came = swap(jnp.stack(normed_pieces[mask:]), "fsdp", mask)
        normed_pieces = [add16(piece, came[i]) for i, piece in enumerate(normed_pieces[:mask])]
    normed_grad = normed_pieces[0]
    in_term = sum(piece.astype(F32) for piece in in_sums).astype(BF16)
    mask = 2 * fold
    while mask < n_ctx:
        in_term = add16(in_term, swap(in_term, "ctx", mask))
        mask *= 2
    handed = z_exchange([in_term[r] for r in range(groups)])
    across = (3 + with_out) * width
    in_block, small = in_vmem(
        functools.partial(
            rows_kernel, groups=groups, cut=cut, part=part, width=width, with_out=with_out
        ),
        index,
        handed + ([in_term[groups]] if with_out else []),
        [
            jax.ShapeDtypeStruct((cut, across), BF16),
            jax.ShapeDtypeStruct((8, 3 * part), F32),
        ],
        [pltpu.VMEM((groups, cut, 3 * part), F32)],
    )
    in_held = chip_spread(in_block, fold)
    tokens_grad = in_vmem(
        tokens_kernel,
        index,
        [normed_grad, rows16, gain_one, resid_grad],
        [jax.ShapeDtypeStruct((local_rows, width), F32)],
    )[0]
    block_out = (resid + feed.astype(F32) + vectors[3:4]).astype(BF16)

    ffn_grads = ffn_grads.reshape(n_ctx, 2, hidden_cut, width).astype(F32)
    up_grad = ffn_grads[:, 0].reshape(hidden, width)
    down_grad = ffn_grads[:, 1].reshape(hidden, width)
    up_grad, down_grad, *in_held = lax.optimization_barrier((up_grad, down_grad, *in_held))
    in_held = in_held + [swap(piece, "ctx", 1) for piece in in_held]
    tokens_grad, *in_held = lax.optimization_barrier((tokens_grad, *in_held))
    homes = in_vmem(
        functools.partial(home_kernel, cut=cut, fetch=fold, with_out=with_out),
        index,
        in_held,
        [
            jax.ShapeDtypeStruct((share, wide_out), F32)
            for wide_out in ((3 * width, width) if with_out else (3 * width,))
        ],
    )
    mixer_in_grad, mixer_out_grad = homes[0], homes[-1]

    if not with_out:
        whole = jnp.stack(attended).reshape(groups, local_rows, part)
        whole = jnp.concatenate([pick(whole, member ^ i) for i in range(groups)], axis=1)
        out_term = contract_rows(whole[:, :width], branch_grad16).astype(BF16)
        out_term = lax.psum_scatter(out_term, "fsdp", scatter_dimension=0, tiled=True)
        mixer_out_grad = lax.psum(out_term, "ctx").astype(F32)

    bias_rows = -(-hidden // (3 * part))
    up_bias_grad = small[3 : 3 + bias_rows].reshape(-1)[:hidden]
    return (
        block_out.reshape(1, 2, slot, width),
        tokens_grad.reshape(1, 2, slot, width),
        small[0, :share],
        small[0, share : 2 * share],
        mixer_in_grad,
        mixer_out_grad,
        small[1, :share],
        small[1, share : 2 * share],
        small[2, :share],
        up_grad,
        up_bias_grad,
        down_grad,
        small[2, share : 2 * share],
    )


def solution(mesh):
    in_specs = (
        P("ctx", None, "fsdp", None),
        P(),
        P("fsdp"),
        P("fsdp"),
        P("fsdp", None),
        P("fsdp", None),
        P("fsdp"),
        P("fsdp"),
        P("fsdp"),
        P("fsdp", None),
        P("fsdp"),
        P("fsdp", None),
        P("fsdp"),
        P("ctx", None, "fsdp", None),
    )
    out_specs = (
        P("ctx", None, "fsdp", None),
        P("ctx", None, "fsdp", None),
        P("fsdp"),
        P("fsdp"),
        P("fsdp", None),
        P("fsdp", None),
        P("fsdp"),
        P("fsdp"),
        P("fsdp"),
        P("fsdp", None),
        P("fsdp"),
        P("fsdp", None),
        P("fsdp"),
    )
    return jax.shard_map(
        per_device, mesh=mesh, in_specs=in_specs, out_specs=out_specs, check_vma=False
    )
```
